32 devices in a mesh: mem: 2 (over x), row: 8 (over z, y), col: 2 (over core).
Axes of the slice: x: 2, y: 2, z: 4, core: 2. Of those that a mesh axis runs over, the one named last changes fastest.
Arguments:
- control: float32 [16, 2, 256, 2048], P('mem', None, 'row', 'col'), may hold values from -6 to 6
- members: bfloat16 [16, 2, 256, 2048], P('mem', None, 'row', 'col'), may hold values from -6 to 6
- obs_corner: int32 [32, 2048], P(('mem', 'row', 'col')), may hold values from 0 to 31742, as said below
- obs_count: int32 [32, 16], P(('mem', 'row', 'col')), may hold values from 0 to 128, as said below
- offset_y: float32 [32, 2048], P(('mem', 'row', 'col')), may hold values from 0 to 1
- offset_x: float32 [32, 2048], P(('mem', 'row', 'col')), may hold values from 0 to 1
- offset_z: float32 [32, 2048], P(('mem', 'row', 'col')), may hold values from 0 to 1
- innovation: float32 [32, 2048], P(('mem', 'row', 'col')), may hold values from -6 to 6
- precision: float32 [32, 2048], P(('mem', 'row', 'col')), may hold values from 1 to 16
Outputs:
- gradient: float32 [16, 2, 256, 2048], P('mem', None, 'row', 'col')
- departures: float32 [32, 2048], P(('mem', 'row', 'col'))
The draws below stay inside these ranges and needn't reach their ends.
Inputs may be any that keep to these rules, and one draw needn't show every extreme that they name: obs_corner is r * 1024 + c with r at most 30 and c at most 1022, so that every stencil lies inside its owner tile. `obs_count`: in every draw some owner tile receives 128 observations from every source.
All inputs are finite; a program needn't handle non-finite values.
Results may differ from the reference program's by a relative error of at most 0.0003.
Values sent between devices are 32-bit elements; how exact they have to be, the bound alone decides.
No kernel may reach another device: no remote copies, remote signals or barrier semaphores. Data moves between devices by JAX's collectives and lax.ppermute only.
A program may use at most 64 MiB of HBM per device.

```python
import math
import jax
import jax.numpy as jnp
from jax import lax

LEV = 2
TY = 32
TX = 1024
CAP = 128
NPASS = 2
MEMBERS = 16
NY = 256
NX = 2048
TILES = 16
SRCS = 32
SLOTS = 2048
N_COL = 2


def draw_obs_corner(key, part):
    first = jax.random.fold_in(key, 11)
    second = jax.random.fold_in(key, 12)
    row_in = jax.random.randint(first, (SRCS, SLOTS), 0, TY - 1)
    col_in = jax.random.randint(second, (SRCS, SLOTS), 0, TX - 1)
    corner = (row_in * TX + col_in).astype(jnp.int32)
    return corner.at[0, 0].set((TY - 2) * TX + TX - 2).astype(jnp.int32)


def draw_obs_count(key, part):
    first = jax.random.fold_in(key, 21)
    second = jax.random.fold_in(key, 22)
    third = jax.random.fold_in(key, 23)
    density = jax.random.randint(first, (TILES,), 2, 6)
    raw_count = jax.random.randint(second, (SRCS, TILES), 0, CAP // 4 + 1)
    counts = jnp.minimum(raw_count * density[None, :], CAP)
    full_tile = jax.random.randint(third, (), 0, TILES)
    counts = jnp.where(jnp.arange(TILES)[None, :] == full_tile, CAP, counts)
    return counts.astype(jnp.int32)


def levels(key, dims, cuts, least, high):
    factor_of = 1.0
    for dim, shards_of in cuts:
        heights = jax.random.uniform(jax.random.fold_in(jax.random.fold_in(key, 6), dim), (shards_of,), jnp.float32, least / len(cuts), high / len(cuts))
        factor_of = factor_of * jnp.repeat(jnp.exp(heights), dims[dim] // shards_of).reshape((-1,) + (1,) * (len(dims) - 1 - dim))
    return factor_of


def normal_values(key, extent, width, limit, cuts=(), dtype=jnp.bfloat16):
    result = width * jax.random.normal(key, extent, jnp.float32)
    if cuts:
        result = result * levels(key, extent, cuts, -0.22, 0.18)
    return jnp.clip(result, -limit, limit).astype(dtype)


def setup_inputs(seed: int = 0) -> dict:
    arg_keys = jax.random.split(jax.random.key(seed), 10)
    return {
        "control": normal_values(arg_keys[0], (MEMBERS, LEV, NY, NX), 1.0, 6.0, ((0, 2), (2, 8), (3, 2)), jnp.float32),
        "members": normal_values(arg_keys[1], (MEMBERS, LEV, NY, NX), 1.0, 6.0, ((0, 2), (2, 8), (3, 2))),
        "obs_corner": draw_obs_corner(jax.random.fold_in(arg_keys[9], 71), 0),
        "obs_count": draw_obs_count(jax.random.fold_in(arg_keys[9], 71), 0),
        "offset_y": jnp.clip(1.0 * jax.random.uniform(arg_keys[4], (SRCS, SLOTS), jnp.float32) ** levels(arg_keys[4], (SRCS, SLOTS), ((0, 32),), -0.2, 0.2), 0.0, 1.0),
        "offset_x": jnp.clip(1.0 * jax.random.uniform(arg_keys[5], (SRCS, SLOTS), jnp.float32) ** levels(arg_keys[5], (SRCS, SLOTS), ((0, 32),), -0.2, 0.2), 0.0, 1.0),
        "offset_z": jnp.clip(1.0 * jax.random.uniform(arg_keys[6], (SRCS, SLOTS), jnp.float32) ** levels(arg_keys[6], (SRCS, SLOTS), ((0, 32),), -0.2, 0.2), 0.0, 1.0),
        "innovation": normal_values(arg_keys[7], (SRCS, SLOTS), 1.0, 6.0, ((0, 32),), jnp.float32),
        "precision": jnp.clip(jnp.exp(math.log(16.0) - 2.7725887 * jax.random.uniform(arg_keys[8], (SRCS, SLOTS), jnp.float32) ** levels(arg_keys[8], (SRCS, SLOTS), ((0, 32),), -0.2, 0.2)), 1.0, 16.0),
    }


def rates(length):
    decay = jnp.exp(-1.0 / length)
    weight = ((1.0 - decay * decay) ** 3 / (1.0 + decay * decay)) ** 0.25
    return decay, weight


def sweep(field, decay, weight, reverse):
    moved = jnp.moveaxis(field, 3, 0)

    def advance(state, column):
        state = decay[None, :, None] * state + weight[None, :, None] * column
        return state, state

    start = jnp.zeros(moved.shape[1:], jnp.float32)
    ignored, swept = lax.scan(advance, start, moved, reverse=reverse)
    return jnp.moveaxis(swept, 0, 3)


def stencil(corner, frac_y, frac_x, frac_z, rows, cols):
    index_list = []
    weight_list = []
    for level in range(2):
        for down in range(2):
            for right in range(2):
                index_list.append(corner + level * rows * cols + down * cols + right)
                weight_z = frac_z if level == 1 else 1.0 - frac_z
                weight_y = frac_y if down == 1 else 1.0 - frac_y
                weight_x = frac_x if right == 1 else 1.0 - frac_x
                weight_list.append(weight_z * weight_y * weight_x)
    return jnp.stack(index_list), jnp.stack(weight_list)


def reference(control, members, obs_corner, obs_count, offset_y, offset_x, offset_z, innovation, precision):
    decay_x, weight_x = rates(jnp.array([TX / 16.0, TX / 64.0], jnp.float32))
    decay_y, weight_y = rates(jnp.array([NY / 2.0, TY / 2.0], jnp.float32))
    scale = float(MEMBERS) ** -0.5
    field = control
    for turn in range(NPASS):
        field = sweep(field, decay_x, weight_x, False)
    field = jnp.swapaxes(field, 2, 3)
    for turn in range(NPASS):
        field = sweep(field, decay_y, weight_y, False)
    field = jnp.swapaxes(field, 2, 3)
    increment = jnp.sum(members.astype(jnp.float32) * field, axis=0) * scale
    slots = jnp.arange(SLOTS)
    tile_of = slots // CAP
    anchor = ((tile_of // N_COL) * TY * NX + (tile_of % N_COL) * TX)[None, :]
    row_in = obs_corner // TX
    col_in = obs_corner - row_in * TX
    global_corner = (anchor + row_in * NX + col_in).astype(jnp.int32)
    indices, weights = stencil(global_corner, offset_y, offset_x, offset_z, NY, NX)
    images = jnp.sum(weights * jnp.take(increment.reshape(-1), indices), axis=0)
    live = (slots % CAP)[None, :] < jnp.take(obs_count, tile_of, axis=1)
    departures = jnp.where(live, precision * (images - innovation), 0.0)
    forcing = jnp.zeros((LEV * NY * NX,), jnp.float32).at[indices.reshape(-1)].add((weights * departures[None]).reshape(-1))
    forcing = forcing.reshape(LEV, NY, NX)
    work = members.astype(jnp.float32) * forcing[None] * scale
    work = jnp.swapaxes(work, 2, 3)
    for turn in range(NPASS):
        work = sweep(work, decay_y, weight_y, True)
    work = jnp.swapaxes(work, 2, 3)
    for turn in range(NPASS):
        work = sweep(work, decay_x, weight_x, True)
    return control + work, departures
```

```python
import functools

import jax
import jax.numpy as jnp
import numpy as np
from jax import lax
from jax.experimental import pallas as pl
from jax.experimental.pallas import tpu as pltpu
from jax.sharding import PartitionSpec as P

LANES = 128
FIELDS = 6
F32 = jnp.float32
BF16 = jnp.bfloat16
MIB = 1 << 20


def filter_rates(lengths):
    decay = np.exp(-1.0 / np.asarray(lengths, np.float64))
    weight = ((1.0 - decay**2) ** 3 / (1.0 + decay**2)) ** 0.25
    return decay, weight


def halves(array):
    array = np.asarray(array, np.float32)
    high = array.astype(BF16)
    low = (array - high.astype(np.float32)).astype(BF16)
    return np.stack([high, low])


def two_pass(decay, weight, lag):
    safe = np.maximum(lag, 0)
    return np.where(lag >= 0, weight**2 * (safe + 1) * decay**safe, 0.0)


def col_constants(rates, size, block, forward):
    decays, weights = rates
    levels = len(decays)
    blocks = size // block
    inner = np.arange(block)
    places = np.arange(size)
    matrices = np.zeros((levels, blocks, block, block))
    edge = np.zeros((levels, size, LANES))
    reach = np.zeros((levels, LANES, size))
    for level, (a, b) in enumerate(zip(decays, weights)):
        for away in range(blocks):
            lag = away * block + inner[None, :] - inner[:, None]
            if not forward:
                lag = away * block + inner[:, None] - inner[None, :]
            matrices[level, away] = two_pass(a, b, lag)
        left = size - 1 - places if forward else places
        edge[level, :, 2 * level] = b * a**left
        edge[level, :, 2 * level + 1] = b**2 * (left + 1) * a**left
        steps = places + 1 if forward else size - places
        reach[level, 2 * level] = b * steps * a**steps
        reach[level, 2 * level + 1] = a**steps
    return halves(matrices), halves(edge), halves(reach)


def row_constants(rates, members, size, forward):
    decays, weights = rates
    levels = len(decays)
    places = np.arange(size)
    eye = np.eye(members)
    matrices = np.zeros((levels, members * size, members * size))
    edge = np.zeros((levels, 2 * members, members * size))
    reach = np.zeros((levels, 2, size, LANES))
    for level, (a, b) in enumerate(zip(decays, weights)):
        lag = places[:, None] - places[None, :]
        if not forward:
            lag = -lag
        matrices[level] = np.kron(eye, two_pass(a, b, lag))
        left = size - 1 - places if forward else places
        edge[level, :members] = np.kron(eye, (b * a**left)[None, :])
        edge[level, members:] = np.kron(eye, (b**2 * (left + 1) * a**left)[None, :])
        steps = places + 1 if forward else size - places
        reach[level, 0] = (b * steps * a**steps)[:, None]
        reach[level, 1] = (a**steps)[:, None]
    return halves(matrices), halves(edge), reach.astype(np.float32)


def split(value):
    high = value.astype(BF16)
    return high, (value - high.astype(F32)).astype(BF16)


def dot(left, right):
    return jnp.dot(left, right, preferred_element_type=F32)


def dot_right(value, ref, *index):
    high, low = split(value)
    first = ref[(0,) + index]
    return dot(high, first) + dot(high, ref[(1,) + index]) + dot(low, first)


def dot_left(ref, level, value):
    high, low = split(value)
    first = ref[0, level]
    return dot(first, high) + dot(ref[1, level], high) + dot(first, low)


def dot_blocks(value, matrix_ref, level, forward, emit):
    blocks, block = matrix_ref.shape[2], matrix_ref.shape[3]
    high, low = split(value)
    for n in range(blocks):
        total = None
        for k in range(n + 1) if forward else range(n, blocks):
            away = abs(n - k)
            part = slice(k * block, (k + 1) * block)
            first = matrix_ref[0, level, away]
            term = dot(high[:, part], first) + dot(high[:, part], matrix_ref[1, level, away])
            term = term + dot(low[:, part], first)
            total = term if total is None else total + term
        emit(n * block, block, total)


def call(kernel, outs, args, limit, smem=(), scratch=(), cost=None):
    return pl.pallas_call(
        kernel,
        out_shape=[jax.ShapeDtypeStruct(shape, dtype) for shape, dtype in outs],
        in_specs=[
            pl.BlockSpec(memory_space=pltpu.SMEM if i in smem else pltpu.VMEM) for i in range(len(args))
        ],
        out_specs=[pl.BlockSpec(memory_space=pltpu.VMEM) for _ in outs],
        scratch_shapes=list(scratch),
        compiler_params=pltpu.CompilerParams(vmem_limit_bytes=limit),
        cost_estimate=cost,
    )(*args)


def level_rows(ref, level):
    value = ref[:, level]
    return value.reshape(value.shape[0] * value.shape[1], value.shape[2])


def work_rows(members_ref, forcing_ref, level):
    value = members_ref[:, level].astype(F32) * forcing_ref[level][None]
    return value.reshape(value.shape[0] * value.shape[1], value.shape[2])


def pack_kernel(control, counts, corner, off_y, off_x, off_z, innovation, precision, edge, message, keep):
    place = lax.axis_index("col")
    total = dot_right(level_rows(control, 0), edge, 0)
    for level in range(1, control.shape[1]):
        total = total + dot_right(level_rows(control, level), edge, level)
    rows = total.shape[0]
    message[0:rows, :] = total
    slot = lax.broadcasted_iota(jnp.int32, (1, LANES), 1)
    for tile_row in range(keep.shape[0] // FIELDS):
        for f, field in enumerate((corner, off_y, off_x, off_z, innovation, precision)):
            pair = []
            for tile_col in range(2):
                tile = 2 * tile_row + tile_col
                value = field[:, tile * LANES : (tile + 1) * LANES].astype(F32)
                if f == FIELDS - 1:
                    value = jnp.where(slot < counts[0, tile], value, 0.0)
                pair.append(value)
            at = tile_row * FIELDS + f
            message[rows + at : rows + at + 1, :] = jnp.where(place == 1, pair[0], pair[1])
            keep[at : at + 1, :] = jnp.where(place == 1, pair[1], pair[0])


def edge_kernel(forward, *refs):
    if forward:
        control, edge, matrix, out = refs
    else:
        members, forcing, edge, matrix, out = refs
    for level in range(out.shape[0]):
        value = level_rows(control, level) if forward else work_rows(members, forcing, level)
        states = dot_left(edge, level, value)

        def emit(at, width, block, level=level):
            out[level, :, at : at + width] = block

        dot_blocks(states, matrix, level, forward, emit)


def send_and_keep(bit, step, spans, unit, read, message, base, keep):
    size = unit << step
    for h in range(spans // 2):
        zero = read((2 * h) * size, size)
        one = read((2 * h + 1) * size, size)
        message[base + h * size : base + (h + 1) * size, :] = jnp.where(bit == 1, zero, one)
        keep[h * size : (h + 1) * size, :] = jnp.where(bit == 1, one, zero)


def enter_kernel(forward, unit, received, keep_in, part, row_edge, reach, message, keep, carried):
    place = lax.axis_index("col")
    row = lax.axis_index("row")
    rows = carried.shape[0]
    live = jnp.where(place == (1 if forward else 0), 1.0, 0.0)
    state = received[0:rows, :] * live
    carried[...] = state
    levels, pairs, size = part.shape
    for level in range(levels):
        inner = dot_left(row_edge, level, state)
        value = part[level] + dot_right(inner, reach, level)
        lay_states(message, level, value)
    base = levels * pairs * size // LANES
    tiles = keep_in.shape[0] // (unit // 2)
    each = unit // 2

    def read(at, width):
        pieces = []
        for tile_row in range(at // unit, (at + width) // unit):
            mine = keep_in[tile_row * each : (tile_row + 1) * each, :]
            other = received[rows + tile_row * each : rows + (tile_row + 1) * each, :]
            pieces.append(jnp.where(place == 1, other, mine))
            pieces.append(jnp.where(place == 1, mine, other))
        return jnp.concatenate(pieces, axis=0)

    send_and_keep(row & 1, 0, tiles, unit, read, message, base, keep)


def lay_states(message, level, value):
    pairs, size = value.shape
    half = pairs // 2
    chunks = size // LANES
    for s in range(2):
        for t in range(chunks):
            at = ((level * 2 + s) * chunks + t) * half
            message[at : at + half, :] = value[s * half : (s + 1) * half, t * LANES : (t + 1) * LANES]


def transfer(rates, level, steps):
    a, b = rates[0][level], rates[1][level]
    return float(a**steps), float(b * steps * a**steps)


def pick(index, values):
    chosen = jnp.float32(values[0])
    for i in range(1, len(values)):
        chosen = jnp.where(index == i, jnp.float32(values[i]), chosen)
    return chosen


def round_kernel(forward, rates, step, steps, tile, unit, spans, *refs):
    last = step == steps - 1
    if step == 0:
        sent, received, keep_in, *outs = refs
        before = None
    else:
        sent, received, keep_in, before, *outs = refs
    row = lax.axis_index("row")
    count = 1 << steps
    bit = (row >> step) & 1
    line = row if forward else count - 1 - row
    upper = ((line >> step) & 1) == 1
    inside = line & ((1 << step) - 1)
    levels = len(rates[0])
    state_rows = outs[-1].shape[0] if last else outs[2].shape[0]
    part = state_rows // (2 * levels)
    for level in range(levels):
        at = 2 * level * part
        first, second = slice(at, at + part), slice(at + part, at + 2 * part)
        got1, got2 = received[first, :], received[second, :]
        table = [transfer(rates, level, q * tile) for q in range(1 << step)]
        near1 = jnp.where(upper, pick(inside, [x[0] for x in table]), 0.0)
        near2 = jnp.where(upper, pick(inside, [x[1] for x in table]), 0.0)
        new1 = near1 * got1
        new2 = near1 * got2 + near2 * got1
        if before is not None:
            new1 = before[first, :] + new1
            new2 = before[second, :] + new2
        states = outs[-1] if last else outs[2]
        states[first, :] = new1
        states[second, :] = new2
        if not last:
            far1, far2 = transfer(rates, level, tile << step)
            own1 = jnp.where(upper, 1.0, far1)
            own2 = jnp.where(upper, 0.0, far2)
            his1 = jnp.where(upper, far1, 1.0)
            his2 = jnp.where(upper, far2, 0.0)
            all1, all2 = sent[first, :], sent[second, :]
            outs[0][first, :] = own1 * all1 + his1 * got1
            outs[0][second, :] = own1 * all2 + own2 * all1 + his1 * got2 + his2 * got1
    size = unit << step

    def join(h):
        mine = keep_in[h * size : (h + 1) * size, :]
        other = received[state_rows + h * size : state_rows + (h + 1) * size, :]
        return jnp.where(bit == 1, other, mine), jnp.where(bit == 1, mine, other)

    if last:
        zero, one = join(0)
        outs[0][0:size, :] = zero
        outs[0][size : 2 * size, :] = one
    else:

        def read(at, width):
            return jnp.concatenate(join(at // width), axis=0)

        send_and_keep((row >> (step + 1)) & 1, step + 1, spans // 2, unit, read, outs[0], state_rows, outs[1])


def merge_kernel(step, kept, other, out):
    bit = (lax.axis_index("row") >> step) & 1
    size = kept.shape[0]
    mine, his = kept[...], other[...]
    out[0:size, :] = jnp.where(bit == 1, his, mine)
    out[size : 2 * size, :] = jnp.where(bit == 1, mine, his)


def swap(value, axis, size, step):
    return lax.ppermute(value, axis, [(i, i ^ (1 << step)) for i in range(size)])


def scan_rows(forward, rates, tile, unit, message, keep, sizes, beside):
    count = lax.axis_size("row")
    steps = count.bit_length() - 1
    spans = count
    state_rows = sizes
    states = None
    extra = None
    for step in range(steps):
        last = step == steps - 1
        if last and beside is not None:
            extra = beside(message, keep, step)
        received = swap(message, "row", count, step)
        args = (message, received, keep) if step == 0 else (message, received, keep, states)
        span_rows = unit << step
        if last:
            outs = [((2 * span_rows, LANES), F32), ((state_rows, LANES), F32)]
        else:
            half = (spans // 4) * 2 * span_rows
            outs = [
                ((state_rows + half, LANES), F32),
                ((half, LANES), F32),
                ((state_rows, LANES), F32),
            ]
        kernel = functools.partial(round_kernel, forward, rates, step, steps, tile, unit, spans)
        result = call(kernel, outs, args, 3 * MIB)
        if last:
            blocks, states = result
        else:
            message, keep, states = result
        spans //= 2
    return blocks, states, extra


def local_kernel(forward, *refs):
    if forward:
        control, members, carried, matrix, reach, row_matrix, out, scratch = refs
    else:
        control, members, forcing, carried, matrix, reach, row_matrix, out, scratch = refs
    count, levels, rows, _ = control.shape
    state = carried[...]
    for level in range(levels):
        value = level_rows(control, level) if forward else work_rows(members, forcing, level)
        block = matrix.shape[3]

        def emit(at, width, total, level=level):
            high, low = split(state)
            near = slice(at, at + width)
            first = reach[0, level, :, near]
            total = total + dot(high, first) + dot(high, reach[1, level, :, near]) + dot(low, first)
            scratch[:, near] = dot_left(row_matrix, level, total)

        dot_blocks(value, matrix, level, forward, emit)
        if forward:
            total = None
            for m in range(count):
                term = members[m, level].astype(F32) * scratch[m * rows : (m + 1) * rows, :]
                total = term if total is None else total + term
            out[level] = total
        else:
            for m in range(count):
                out[m, level] = control[m, level] + scratch[m * rows : (m + 1) * rows, :]


def gather_fields(table, chunk, wide):
    fields = []
    for f in range(FIELDS):
        rows = [table[pl.ds((chunk * wide + i) * FIELDS + f, 1), :] for i in range(wide)]
        fields.append(jnp.concatenate(rows, axis=1))
    return fields


def row_weights(row_at, frac, rows):
    places = lax.broadcasted_iota(jnp.int32, (rows, row_at.shape[1]), 0)
    near = jnp.where(places == row_at, 1.0 - frac, 0.0)
    return near + jnp.where(places == row_at + 1, frac, 0.0)


def one_hot(col_at, cols):
    places = lax.broadcasted_iota(jnp.int32, (cols, col_at.shape[1]), 0)
    return jnp.where(places == col_at, 1.0, 0.0).astype(BF16)


def place_of(corner, cols):
    at = corner.astype(jnp.int32)
    row = lax.div(at, cols)
    return row, at - row * cols


def observe_kernel(scale, wide, group, partial, states, members, reach, table, images, field):
    count, levels, rows, cols = members.shape
    chunks = cols // LANES
    for level in range(levels):
        reach1, reach2 = reach[level, 0], reach[level, 1]
        for t in range(chunks):
            near = slice(t * LANES, (t + 1) * LANES)
            total = partial[level, :, near]
            for m in range(count):
                at = (2 * level * chunks + t) * count + m
                later = at + chunks * count
                entered = reach1 * states[at : at + 1, :] + reach2 * states[later : later + 1, :]
                total = total + members[m, level, :, near].astype(F32) * entered
            total = total * scale
            field[level * rows : (level + 1) * rows, near] = total
    flat = levels * rows
    value = field[...]
    high, low = split(value)
    moved_high, moved_low = split(pltpu.roll(value, cols - 1, 1))
    stack = jnp.concatenate([high, low, moved_high, moved_low], axis=0)
    pieces = table.shape[0] // FIELDS // wide

    def work(chunk):
        corner, frac_y, frac_x, frac_z, _, _ = gather_fields(table, chunk, wide)
        row_at, col_at = place_of(corner, cols)
        seen = dot(stack, one_hot(col_at, cols))
        left = seen[0:flat] + seen[flat : 2 * flat]
        right = seen[2 * flat : 3 * flat] + seen[3 * flat : 4 * flat]
        mixed = left * (1.0 - frac_x) + right * frac_x
        weight = row_weights(row_at, frac_y, rows)
        low_level = jnp.sum(mixed[0:rows] * weight, axis=0, keepdims=True)
        high_level = jnp.sum(mixed[rows : 2 * rows] * weight, axis=0, keepdims=True)
        image = (1.0 - frac_z) * low_level + frac_z * high_level
        for i in range(wide):
            images[pl.ds(chunk * wide + i, 1), :] = image[:, i * LANES : (i + 1) * LANES]

    @pl.loop(0, pieces // group)
    def _(turn):
        for i in range(group):
            work(turn * group + i)


def force_kernel(
    scale, wide, group, images, others, table, members, edge, forcing, message, keep, hot, load, total, misfits
):
    count, levels, rows, cols = members.shape
    flat = levels * rows
    sources = table.shape[0] // FIELDS
    half = sources // 2
    pieces = sources // wide
    span = wide * LANES
    total[...] = jnp.zeros_like(total)

    @pl.loop(0, pieces // group)
    def _(turn):
        for i in range(group):
            chunk = turn * group + i
            corner, frac_y, frac_x, frac_z, innovation, precision = gather_fields(table, chunk, wide)
            row_at, col_at = place_of(corner, cols)
            parts = []
            for j in range(wide):
                source = chunk * wide + j
                swapped = jnp.where(source < half, source + half, source - half)
                parts.append(images[pl.ds(source, 1), :] + others[pl.ds(swapped, 1), :])
            misfit = precision * (jnp.concatenate(parts, axis=1) - innovation)
            for j in range(wide):
                misfits[pl.ds(chunk * wide + j, 1), :] = misfit[:, j * LANES : (j + 1) * LANES]
            weight = row_weights(row_at, frac_y, rows) * misfit
            stack = jnp.concatenate([weight * (1.0 - frac_z), weight * frac_z], axis=0)
            near = slice(i * span, (i + 1) * span)
            load[0:flat, near], load[flat : 2 * flat, near] = split(stack * (1.0 - frac_x))
            load[2 * flat : 3 * flat, near], load[3 * flat : 4 * flat, near] = split(stack * frac_x)
            hot[:, near] = one_hot(col_at, cols)
        total[...] += lax.dot_general(
            load[...], hot[...], (((1,), (1,)), ((), ())), preferred_element_type=F32
        )

    left = total[0:flat, :] + total[flat : 2 * flat, :]
    right = total[2 * flat : 3 * flat, :] + total[3 * flat : 4 * flat, :]
    force = (left + pltpu.roll(right, 1, 1)) * scale
    for level in range(levels):
        forcing[level] = force[level * rows : (level + 1) * rows]
    edges = dot_right(work_rows(members, forcing, 0), edge, 0)
    for level in range(1, levels):
        edges = edges + dot_right(work_rows(members, forcing, level), edge, level)
    flat_rows = edges.shape[0]
    message[0:flat_rows, :] = edges
    place = lax.axis_index("col")
    for tile_row in range(keep.shape[0]):
        zero = misfits[2 * tile_row : 2 * tile_row + 1, :]
        one = misfits[2 * tile_row + 1 : 2 * tile_row + 2, :]
        message[flat_rows + tile_row : flat_rows + tile_row + 1, :] = jnp.where(place == 1, zero, one)
        keep[tile_row : tile_row + 1, :] = jnp.where(place == 1, one, zero)


def finish_kernel(base, states, reach, out):
    level = pl.program_id(1)
    member = pl.program_id(0)
    count = pl.num_programs(0)
    chunks = base.shape[3] // LANES
    reach1, reach2 = reach[0, 0], reach[0, 1]
    for t in range(chunks):
        near = slice(t * LANES, (t + 1) * LANES)
        at = (2 * level * chunks + t) * count + member
        first = states[pl.ds(at, 1), :]
        second = states[pl.ds(at + chunks * count, 1), :]
        out[0, 0, :, near] = base[0, 0, :, near] + reach1 * first + reach2 * second


def body(
    control, members, obs_corner, obs_count, offset_y, offset_x, offset_z, innovation, precision
):
    count, levels, rows, cols = control.shape
    n_mem, n_row, n_col = (lax.axis_size(name) for name in ("mem", "row", "col"))
    if n_mem != 2 or n_col != 2 or n_row & (n_row - 1):
        raise ValueError("unsupported mesh")
    grid_rows = rows * n_row
    block = min(256, cols)
    rates_x = filter_rates([cols / 16.0, cols / 64.0])
    rates_y = filter_rates([grid_rows / 2.0, rows / 2.0])
    scale = float(count * n_mem) ** -0.5
    flat = count * rows
    state_rows = levels * 2 * count * cols // LANES

    matrix, edge, reach = col_constants(rates_x, cols, block, True)
    row_matrix, row_edge, row_reach = row_constants(rates_y, count, rows, True)
    message, keep = call(
        pack_kernel,
        [((flat + n_row * FIELDS, LANES), F32), ((n_row * FIELDS, LANES), F32)],
        (control, obs_count, obs_corner, offset_y, offset_x, offset_z, innovation, precision, edge),
        16 * MIB,
        smem=(1,),
    )
    received = swap(message, "col", n_col, 0)
    (part,) = call(
        functools.partial(edge_kernel, True),
        [((levels, 2 * count, cols), F32)],
        (control, row_edge, matrix),
        16 * MIB,
    )
    unit = n_col * FIELDS
    message, keep, carried = call(
        functools.partial(enter_kernel, True, unit),
        [
            ((state_rows + n_row // 2 * unit, LANES), F32),
            ((n_row // 2 * unit, LANES), F32),
            ((flat, LANES), F32),
        ],
        (received, keep, part, row_edge, reach),
        8 * MIB,
    )
    (partial,) = call(
        functools.partial(local_kernel, True),
        [((levels, rows, cols), F32)],
        (control, members, carried, matrix, reach, row_matrix),
        24 * MIB,
        scratch=[pltpu.VMEM((flat, cols), F32)],
    )

    def beside(message, keep, step):
        other = lax.ppermute(keep, "mem", [(0, 1), (1, 0)])
        pairs = []
        for m in range(n_mem):
            for r in range(n_row):
                pairs.append((m * n_row + r, (1 - m) * n_row + (r ^ (1 << step))))
        cross = lax.ppermute(message[state_rows:], ("mem", "row"), pairs)
        (table,) = call(
            functools.partial(merge_kernel, step),
            [((2 * keep.shape[0], LANES), F32)],
            (other, cross),
            2 * MIB,
        )
        return table

    own_table, states, other_table = scan_rows(
        True, rates_y, rows, unit, message, keep, state_rows, beside
    )
    table = jnp.concatenate([own_table, other_table], axis=0)
    sources = table.shape[0] // FIELDS
    wide = 2
    group = 8
    (images,) = call(
        functools.partial(observe_kernel, scale, wide, group),
        [((sources, LANES), F32)],
        (partial, states, members, row_reach, table),
        24 * MIB,
        scratch=[pltpu.VMEM((levels * rows, cols), F32)],
    )
    others = lax.ppermute(images, "mem", [(0, 1), (1, 0)])

    matrix, edge, reach = col_constants(rates_x, cols, block, False)
    row_matrix, row_edge, row_reach = row_constants(rates_y, count, rows, False)
    forcing, message, keep = call(
        functools.partial(force_kernel, scale, wide, group),
        [
            ((levels, rows, cols), F32),
            ((flat + n_row, LANES), F32),
            ((n_row, LANES), F32),
        ],
        (images, others, table, members, edge),
        32 * MIB,
        scratch=[
            pltpu.VMEM((cols, group * wide * LANES), BF16),
            pltpu.VMEM((4 * levels * rows, group * wide * LANES), BF16),
            pltpu.VMEM((4 * levels * rows, cols), F32),
            pltpu.VMEM((sources, LANES), F32),
        ],
    )
    received = swap(message, "col", n_col, 0)
    (part,) = call(
        functools.partial(edge_kernel, False),
        [((levels, 2 * count, cols), F32)],
        (members, forcing, row_edge, matrix),
        16 * MIB,
    )
    unit = n_col
    message, keep, carried = call(
        functools.partial(enter_kernel, False, unit),
        [
            ((state_rows + n_row // 2 * unit, LANES), F32),
            ((n_row // 2 * unit, LANES), F32),
            ((flat, LANES), F32),
        ],
        (received, keep, part, row_edge, reach),
        8 * MIB,
    )
    (base,) = call(
        functools.partial(local_kernel, False),
        [((count, levels, rows, cols), F32)],
        (control, members, forcing, carried, matrix, reach, row_matrix),
        24 * MIB,
        scratch=[pltpu.VMEM((flat, cols), F32)],
    )
    returned, states, _ = scan_rows(
        False, rates_y, rows, unit, message, keep, state_rows, None
    )
    gradient = pl.pallas_call(
        finish_kernel,
        out_shape=jax.ShapeDtypeStruct(control.shape, F32),
        grid=(count, levels),
        in_specs=[
            pl.BlockSpec((1, 1, rows, cols), lambda m, l: (m, l, 0, 0)),
            pl.BlockSpec((state_rows, LANES), lambda m, l: (0, 0)),
            pl.BlockSpec((1, 2, rows, LANES), lambda m, l: (l, 0, 0, 0)),
        ],
        out_specs=pl.BlockSpec((1, 1, rows, cols), lambda m, l: (m, l, 0, 0)),
        compiler_params=pltpu.CompilerParams(vmem_limit_bytes=4 * MIB),
    )(base, states, row_reach)
    return (gradient, returned.reshape(1, -1))


def solution(mesh):
    spread = P(("mem", "row", "col"), None)
    grid = P("mem", None, "row", "col")
    return jax.shard_map(
        body,
        mesh=mesh,
        in_specs=(grid, grid) + (spread,) * 7,
        out_specs=(grid, spread),
        check_vma=False,
    )
```

```python
import functools

import jax
import jax.numpy as jnp
import numpy as np
from jax import lax
from jax.experimental import pallas as pl
from jax.experimental.pallas import tpu as pltpu
from jax.sharding import PartitionSpec as P

LANES = 128
HALF = LANES // 2
FIELDS = 6
GROUP = 4
PIECE = 256
F32 = jnp.float32
BF16 = jnp.bfloat16
MIB = 1 << 20
OBS = 57


def filter_rates(lengths):
    decay = np.exp(-1.0 / np.asarray(lengths, np.float64))
    weight = ((1.0 - decay**2) ** 3 / (1.0 + decay**2)) ** 0.25
    return decay, weight


def halves(array):
    array = np.asarray(array, np.float32)
    high = array.astype(BF16)
    low = (array - high.astype(np.float32)).astype(BF16)
    return np.stack([high, low])


def two_pass(decay, weight, lag):
    safe = np.maximum(lag, 0)
    return np.where(lag >= 0, weight**2 * (safe + 1) * decay**safe, 0.0)


def col_constants(rates, size, block, forward):
    decays, weights = rates
    levels = len(decays)
    blocks = size // block
    per_level = 2 * (blocks + 1)
    inner = np.arange(block)
    places = np.arange(size)
    if not forward:
        places = places[::-1]
    matrices = np.zeros((levels, block, block))
    edge = np.zeros((size, HALF))
    reach = np.zeros((HALF, size))
    for level, (a, b) in enumerate(zip(decays, weights)):
        lag = inner[None, :] - inner[:, None]
        matrices[level] = two_pass(a, b, lag if forward else -lag)
        for k in range(blocks + 1):
            at = level * per_level + 2 * k
            stop = size if k == blocks else (k + 1) * block
            begin = 0 if k == blocks else k * block
            left = stop - 1 - places
            inside = (places >= begin) & (left >= 0)
            left = np.maximum(left, 0)
            edge[:, at] = np.where(inside, b * a**left, 0.0)
            edge[:, at + 1] = np.where(inside, b**2 * (left + 1) * a**left, 0.0)
            steps = places + 1 - (0 if k == blocks else stop)
            beyond = steps > 0
            steps = np.maximum(steps, 0)
            reach[at] = np.where(beyond, b * steps * a**steps, 0.0)
            reach[at + 1] = np.where(beyond, a**steps, 0.0)
    edge_high, edge_low = halves(edge)
    reach_high, reach_low = halves(reach)
    return (
        halves(matrices),
        np.concatenate([edge_high, edge_low], axis=1),
        np.concatenate([reach_high, reach_high, reach_low, np.zeros_like(reach_low)], axis=0),
    )


def row_constants(rates, members, size, forward):
    decays, weights = rates
    levels = len(decays)
    places = np.arange(size)
    eye = np.eye(members)
    matrices = np.zeros((levels, members * size, members * size))
    reach = np.zeros((levels, 2, size, LANES))
    for level, (a, b) in enumerate(zip(decays, weights)):
        lag = places[:, None] - places[None, :]
        if not forward:
            lag = -lag
        matrices[level] = np.kron(eye, two_pass(a, b, lag))
        steps = places + 1 if forward else size - places
        reach[level, 0] = (b * steps * a**steps)[:, None]
        reach[level, 1] = (a**steps)[:, None]
    return halves(matrices), reach.astype(np.float32)


def side_by_side(pieces, width):
    row = np.concatenate(pieces, axis=1)
    return np.pad(row, ((0, 0), (0, width - row.shape[1])))


def edge_table(matrices, edge, reach):
    width = reach.shape[1]
    return np.concatenate(
        [
            reach,
            side_by_side(list(matrices.reshape(-1, *matrices.shape[2:])), width),
            side_by_side(list(edge.reshape(-1, LANES, LANES)), width),
        ]
    )


class EdgeTable:
    def __init__(self, ref, levels, block):
        self.ref, self.levels, self.block = ref, levels, block
        self.size = ref.shape[1]
        self.first = 4 * HALF

    def reach(self, near=slice(None)):
        return self.ref[0 : self.first, near]

    def matrix(self, level):
        return jnp.concatenate([self.square(level), self.square(self.levels + level), self.square(level)], axis=0)

    def square(self, index):
        return self.ref[self.first : self.first + self.block, index * self.block : (index + 1) * self.block]

    def edge(self):
        at = self.first + self.block
        rows = [self.ref[at : at + LANES, t : t + LANES] for t in range(0, self.size, LANES)]
        return jnp.concatenate(rows + rows, axis=0)


def split(value):
    high = value.astype(BF16)
    return high, (value - high.astype(F32)).astype(BF16)


def dot(left, right):
    return jnp.dot(left, right, preferred_element_type=F32)


def lane_kinds(shape, blocks, level):
    lane = lax.broadcasted_iota(jnp.int32, shape, 1)
    per_level = 2 * (blocks + 1)
    mine = (lane >= level * per_level) & (lane < (level + 1) * per_level)
    return mine, lax.rem(lane, per_level) >= 2 * blocks


def edge_states(value, table, blocks, level):
    high, low = split(value)
    both = dot(jnp.concatenate([high, low], axis=1), table.edge())
    mine, _ = lane_kinds(both.shape, blocks, level)
    return jnp.where(mine, both + pltpu.roll(both, HALF, 1), 0.0)


def packed(states):
    lane = lax.broadcasted_iota(jnp.int32, states.shape, 1)
    high = states.astype(BF16).astype(F32)
    low = states - high
    first = jnp.where(lane < HALF, high, pltpu.roll(low, HALF, 1))
    second = jnp.where(lane < HALF, high, 0.0)
    return jnp.concatenate([first.astype(BF16), second.astype(BF16)], axis=1)


def dot_left(left, value):
    high, low = split(value)
    return dot(left, jnp.concatenate([high, high, low], axis=0))


def dot_right(value, right, *more):
    high, low = split(value)
    left = jnp.concatenate([high, high, low] + [x for x, _ in more], axis=1)
    return dot(left, jnp.concatenate([right] + [x for _, x in more], axis=0))


def cost(micros):
    return pl.CostEstimate(flops=0, bytes_accessed=int(micros * 3.6e6), transcendentals=0)


def call(kernel, outs, args, limit, micros, apart=(), scratch=()):
    return pl.pallas_call(
        kernel,
        out_shape=[jax.ShapeDtypeStruct(shape, dtype) for shape, dtype in outs],
        in_specs=[
            pl.BlockSpec(memory_space=pl.ANY if i in apart else pltpu.VMEM) for i in range(len(args))
        ],
        out_specs=[pl.BlockSpec(memory_space=pltpu.VMEM) for _ in outs],
        scratch_shapes=list(scratch),
        compiler_params=pltpu.CompilerParams(vmem_limit_bytes=limit),
        cost_estimate=cost(micros),
    )(*args)


def level_rows(ref, level):
    value = ref[:, level]
    return value.reshape(value.shape[0] * value.shape[1], value.shape[2])


def work_rows(members_ref, forcing_ref, level):
    value = members_ref[:, level].astype(F32) * forcing_ref[level][None]
    return value.reshape(value.shape[0] * value.shape[1], value.shape[2])


def row_weights_at_edge(forward, rates, level, members, size):
    a, b = rates[0][level], rates[1][level]
    shape = (members, members * size)
    member = lax.broadcasted_iota(jnp.int32, shape, 0)
    place = lax.broadcasted_iota(jnp.int32, shape, 1)
    row = lax.rem(place, size)
    left = (size - 1 - row if forward else row).astype(F32)
    power = jnp.where(lax.div(place, size) == member, float(b) * jnp.exp(left * float(np.log(a))), 0.0)
    high, low = split(jnp.concatenate([power, float(b) * (left + 1.0) * power], axis=0))
    return jnp.concatenate([high, low, high], axis=1)


def put_row_edges(forward, rates, members, values, message):
    for level, value in values:
        size = value.shape[0] // members
        states = dot_left(row_weights_at_edge(forward, rates, level, members, size), value)
        lay_states(message, level, states)


def lay_states(message, level, states):
    half = states.shape[0] // 2
    chunks = states.shape[1] // LANES
    for s in range(2):
        for t in range(chunks):
            at = ((2 * level + s) * chunks + t) * half
            message[at : at + half, :] = states[s * half : (s + 1) * half, t * LANES : (t + 1) * LANES]


def take_states(states, level, half, chunks):
    rows = []
    for s in range(2):
        at = (2 * level + s) * chunks * half
        rows.append(
            jnp.concatenate([states[at + t * half : at + (t + 1) * half, :] for t in range(chunks)], axis=1)
        )
    return jnp.concatenate(rows, axis=0)


def first_kernel(rates, control, _, message):
    values = ((level, level_rows(control, level)) for level in range(control.shape[1]))
    put_row_edges(True, rates, control.shape[0], values, message)


def block_kernel(*refs):
    sources, (send, keep), places, sems = refs[:7], refs[-10:-8], refs[-8:-1], refs[-1]
    copies = [pltpu.make_async_copy(s, p, sems.at[i]) for i, (s, p) in enumerate(zip(sources, places))]
    for copy in copies:
        copy.start()
    for copy in copies:
        copy.wait()
    counts, *fields = places
    rows = counts.shape[1] // 2
    steps = rows.bit_length() - 1
    order = sorted(range(rows), key=lambda row: block_place(True, steps, row))
    bit = (lax.axis_index("row") >> block_bits(True, steps)[0]) & 1
    slot = lax.broadcasted_iota(jnp.int32, (1, LANES), 1)

    def read(tile, f):
        value = fields[f][:, tile * LANES : (tile + 1) * LANES].astype(F32)
        if f == FIELDS - 1:
            value = jnp.where(slot < counts[:, tile : tile + 1], value, 0.0)
        return value

    at = 0
    for h in range(0, rows, 2):
        for tile_col in range(2):
            for f in range(FIELDS):
                zero, one = read(2 * order[h] + tile_col, f), read(2 * order[h + 1] + tile_col, f)
                send[at : at + 1, :], keep[at : at + 1, :] = join(bit, one, zero)
                at += 1


def columns_kernel(forward, block, *refs):
    if forward:
        control, edges, out = refs[0], refs[1], refs[-1]
        levels = control.shape[1]
    else:
        members, forcing, edges, out = refs[0], refs[1], refs[2], refs[-1]
        levels = members.shape[1]
    table = EdgeTable(edges, levels, block)
    total = None
    for level in range(levels):
        value = level_rows(control, level) if forward else work_rows(members, forcing, level)
        states = edge_states(value, table, table.size // block, level)
        total = states if total is None else total + states
    out[...] = total


def entering_rows(forward, rates, level, size):
    a, b = rates[0][level], rates[1][level]
    place = lax.broadcasted_iota(jnp.int32, (1, size), 1)
    steps = (place + 1 if forward else size - place).astype(F32)
    power = jnp.exp(steps * float(np.log(a)))
    return float(b) * steps * power, power


def corner_kernel(forward, rates, step, count, tile, unit, half, block, after, *refs):
    *refs, edges, before, received, keep_in, states, message, keep = refs
    refs = refs[after:]
    last_states(forward, rates, step, count, tile, before, received, states)
    levels = len(rates[0])
    table = EdgeTable(edges, levels, block)
    chunks = table.size // LANES
    at = 0
    for level in range(levels):
        corner = edge_states(take_states(states, level, half, chunks), table, table.size // block, level)
        message[at : at + 2 * half, :] = corner
        at += 2 * half
    bit = (lax.axis_index("row") >> block_bits(forward, step + 1)[step]) & 1
    place = lax.axis_index("col")
    base, size = before.shape[0], keep_in.shape[0]
    each = unit // 2
    if refs:
        pairs = [(keep_in[...], refs[0][...]), (refs[1][...], refs[2][...])]
    else:
        pairs = [(keep_in[...], received[base : base + size, :])]
    start, at = at, 0
    for mine, other in pairs:
        for value in join(bit, mine, other):
            for i in range(0, size, unit):
                send, stay = join(place, value[i + each : i + unit], value[i : i + each])
                message[start + at : start + at + each, :] = send
                keep[at : at + each, :] = stay
                at += each


def inner_kernel(levels, half, block, edges, states, message, part):
    table = EdgeTable(edges, levels, block)
    size = table.size
    blocks = size // block
    for level in range(levels):
        value = take_states(states, level, half, size // LANES)
        pairs = value.shape[0]
        corner = message[level * pairs : (level + 1) * pairs, :]
        _, whole = lane_kinds(corner.shape, blocks, level)
        carry = dot(packed(jnp.where(whole, 0.0, corner)), table.reach())
        stack = jnp.concatenate([value[:, at : at + block] for at in range(0, size, block)], axis=0)
        stack = dot_right(stack, table.matrix(level))
        rows = [stack[n * pairs : (n + 1) * pairs] for n in range(blocks)]
        lay_states(part, level, jnp.concatenate(rows, axis=1) + carry)


def outer_states(forward, rates, per_level, half, part, received, states):
    place = lax.axis_index("col")
    live = jnp.where(place == (1 if forward else 0), 1.0, 0.0)
    levels = len(rates[0])
    chunks = part.shape[0] // (2 * levels * half)
    for level in range(levels):
        lane = (level + 1) * per_level - 2
        ones, twos = entering_rows(forward, rates, level, chunks * LANES)
        for s in range(2):
            at = (2 * level + s) * half
            corner = received[at : at + half, :] * live
            one, two = corner[:, lane : lane + 1], corner[:, lane + 1 : lane + 2]
            for t in range(chunks):
                at = ((2 * level + s) * chunks + t) * half
                near = slice(t * LANES, (t + 1) * LANES)
                states[at : at + half, :] = part[at : at + half, :] + one * ones[:, near] + two * twos[:, near]


def join_columns(each, keep, received, base):
    place = lax.axis_index("col")
    for i in range(0, keep.shape[0], each):
        yield from join(place, keep[i : i + each, :], received[base + i : base + i + each, :])


def collect_kernel(rates, per_level, half, part, received, keep, states, table):
    outer_states(True, rates, per_level, half, part, received, states)
    at = 0
    for value in join_columns(FIELDS, keep, received, 2 * len(rates[0]) * half):
        table[at : at + FIELDS, :] = value
        at += FIELDS


def block_bits(forward, steps):
    bits = list(range(steps))
    if forward:
        bits[0], bits[-1] = bits[-1], bits[0]
    return bits


def block_place(forward, steps, row):
    return sum(((row >> bit) & 1) << i for i, bit in enumerate(block_bits(forward, steps)))


def transfer(rates, level, steps):
    a, b = rates[0][level], rates[1][level]
    return float(a**steps), float(b * steps * a**steps)


def pick(index, values):
    chosen = jnp.float32(values[0])
    for i in range(1, len(values)):
        chosen = jnp.where(index == i, jnp.float32(values[i]), chosen)
    return chosen


def reach_of(forward, rates, step, count, tile, level):
    row = lax.axis_index("row")
    line = row if forward else count - 1 - row
    upper = ((line >> step) & 1) == 1
    inside = line & ((1 << step) - 1)
    table = [transfer(rates, level, q * tile) for q in range(1 << step)]
    near1 = jnp.where(upper, pick(inside, [x[0] for x in table]), 0.0)
    near2 = jnp.where(upper, pick(inside, [x[1] for x in table]), 0.0)
    return near1, near2, upper


def join(bit, mine, other):
    return jnp.where(bit == 1, other, mine), jnp.where(bit == 1, mine, other)


def new_states(forward, rates, step, count, tile, level, before, received, first, second):
    near1, near2, upper = reach_of(forward, rates, step, count, tile, level)
    got1, got2 = received[first, :], received[second, :]
    new1 = near1 * got1
    new2 = near1 * got2 + near2 * got1
    if before is not None:
        new1 = before[first, :] + new1
        new2 = before[second, :] + new2
    return new1, new2, got1, got2, upper


def round_kernel(forward, rates, step, count, tile, unit, spans, apart, after, *refs):
    sent, received, keep_in, *refs = refs
    before = refs.pop(0) if step else None
    blocks = refs.pop(0) if apart else received
    message, keep, states, *send = refs[after:]
    levels = len(rates[0])
    base = states.shape[0]
    start = 0 if apart else base
    part = base // (2 * levels)
    for level in range(levels):
        at = 2 * level * part
        first, second = slice(at, at + part), slice(at + part, at + 2 * part)
        new1, new2, got1, got2, upper = new_states(
            forward, rates, step, count, tile, level, before, received, first, second
        )
        states[first, :] = new1
        states[second, :] = new2
        far1, far2 = transfer(rates, level, tile << step)
        own1 = jnp.where(upper, 1.0, far1)
        own2 = jnp.where(upper, 0.0, far2)
        his1 = jnp.where(upper, far1, 1.0)
        his2 = jnp.where(upper, far2, 0.0)
        all1, all2 = sent[first, :], sent[second, :]
        message[first, :] = own1 * all1 + his1 * got1
        message[second, :] = own1 * all2 + own2 * all1 + his1 * got2 + his2 * got1
    row = lax.axis_index("row")
    bits = block_bits(forward, count.bit_length() - 1)
    bit = (row >> bits[step]) & 1
    next_bit = (row >> bits[step + 1]) & 1
    size = unit << step
    place, first = (send[0], 0) if send else (message, base)

    def span(h):
        near = slice(h * size, (h + 1) * size)
        other = blocks[start + h * size : start + (h + 1) * size, :]
        return jnp.concatenate(join(bit, keep_in[near, :], other), axis=0)

    at = 0
    for h in range(0, spans // 2, 2):
        moved, stay = join(next_bit, span(h + 1), span(h))
        place[first + at : first + at + 2 * size, :] = moved
        keep[at : at + 2 * size, :] = stay
        at += 2 * size


def last_states(forward, rates, step, count, tile, before, received, states):
    levels = len(rates[0])
    part = before.shape[0] // (2 * levels)
    for level in range(levels):
        at = 2 * level * part
        first, second = slice(at, at + part), slice(at + part, at + 2 * part)
        states[first, :], states[second, :], *_ = new_states(
            forward, rates, step, count, tile, level, before, received, first, second
        )


def swap(value, axis, size, step):
    return lax.ppermute(value, axis, [(i, i ^ (1 << step)) for i in range(size)])


def scan_rows(forward, rates, tile, unit, message, blocks, beside):
    count = lax.axis_size("row")
    steps = count.bit_length() - 1
    spans = count
    apart = len(blocks) == 2
    keep = blocks[-1]
    moving = keep.shape[0]
    state_rows = message.shape[0] - (0 if apart else moving)
    states = None
    for step in range(steps - 1):
        received = swap(message, "row", count, step)
        args = (message, received, keep) + (() if step == 0 else (states,))
        if apart:
            args += (swap(blocks[0], "row", count, block_bits(forward, steps)[step]),)
        after = beside(step, message)
        first = len(args)
        args = args + tuple(after)
        kernel = functools.partial(
            round_kernel, forward, rates, step, count, tile, unit, spans, apart, len(after)
        )
        outs = [state_rows + moving, moving, state_rows]
        if forward and step == steps - 2:
            outs = [state_rows, moving, state_rows, moving]
        outs = [((rows, LANES), F32) for rows in outs]
        message, keep, states, *send = call(kernel, outs, args, 4 * MIB, 0.1, apart=range(first, len(args)))
        spans //= 2
        apart = False
    received = swap(message, "row", count, steps - 1)
    beside(steps - 1, message)
    return states, received, send, keep


def local_kernel(forward, level, block, *refs):
    if forward:
        control, members, columns, received, edges, row_matrix, _, out, scratch = refs
    else:
        control, members, forcing, columns, received, edges, row_matrix, _, out, scratch = refs
    count, levels, rows, cols = control.shape
    table = EdgeTable(edges, levels, block)
    value = level_rows(control, level) if forward else work_rows(members, forcing, level)
    mine, whole = lane_kinds((count * rows, LANES), cols // block, level)
    live = jnp.where(lax.axis_index("col") == (1 if forward else 0), 1.0, 0.0)
    entering = jnp.where(whole, received[...] * live, columns[...])
    entering = packed(jnp.where(mine, entering, 0.0))
    weights = table.matrix(level)
    high = row_matrix[0, level]
    left = jnp.concatenate([high, row_matrix[1, level], high], axis=1)
    for n in range(cols // block):
        near = slice(n * block, (n + 1) * block)
        total = dot_right(value[:, near], weights, (entering, table.reach(near)))
        scratch[:, near] = dot_left(left, total)
    if forward:
        total = None
        for m in range(count):
            term = members[m, level].astype(F32) * scratch[m * rows : (m + 1) * rows, :]
            total = term if total is None else total + term
        out[...] = total
    else:
        for m in range(count):
            out[m] = control[m, level] + scratch[m * rows : (m + 1) * rows, :]


def gather_fields(table, chunk, wide):
    fields = []
    for f in range(FIELDS):
        rows = [table[pl.ds((chunk * wide + i) * FIELDS + f, 1), :] for i in range(wide)]
        fields.append(jnp.concatenate(rows, axis=1))
    return fields


def row_weights(row_at, frac, rows):
    places = lax.broadcasted_iota(jnp.int32, (rows, row_at.shape[1]), 0)
    near = jnp.where(places == row_at, 1.0 - frac, 0.0)
    return near + jnp.where(places == row_at + 1, frac, 0.0)


def one_hot(col_at, cols):
    places = lax.broadcasted_iota(jnp.int32, (cols, col_at.shape[1]), 0)
    return jnp.where(places == col_at, 1.0, 0.0).astype(BF16)


def place_of(corner, cols):
    at = corner.astype(jnp.int32)
    row = lax.div(at, cols)
    return row, at - row * cols


def spread_matrix(size, back):
    one = lax.broadcasted_iota(jnp.int32, (size, size), 1 if back else 0)
    two = lax.broadcasted_iota(jnp.int32, (size, size), 0 if back else 1)
    at = (one & (GROUP - 1)) * (size // GROUP) + lax.div(one, GROUP)
    return jnp.where(at == two, 1.0, 0.0).astype(BF16)


def col_weights(col_at, frac):
    within = col_at & (GROUP - 1)
    weights = []
    for j in range(GROUP + 1):
        weight = jnp.where(within == j, 1.0 - frac, 0.0)
        weights.append(weight + jnp.where(within == j - 1, frac, 0.0))
    return weights


def observe_kernel(scale, wide, group, states, members, reach, table, *refs):
    count, levels, rows, cols = members.shape
    partial, (images, field, stack) = refs[:levels], refs[levels:]
    chunks = cols // LANES
    for level in range(levels):
        reach1, reach2 = reach[level, 0], reach[level, 1]
        for t in range(chunks):
            near = slice(t * LANES, (t + 1) * LANES)
            total = partial[level][:, near]
            for m in range(count):
                at = (2 * level * chunks + t) * count + m
                later = at + chunks * count
                entered = reach1 * states[at : at + 1, :] + reach2 * states[later : later + 1, :]
                total = total + members[m, level, :, near].astype(F32) * entered
            field[level * rows : (level + 1) * rows, near] = total * scale
    flat = levels * rows
    high, low = split(field[...])
    both = jnp.concatenate([high, low], axis=0)
    spread = spread_matrix(PIECE, False)
    each = PIECE // GROUP
    pieces = [dot(both[:, at : at + PIECE], spread) for at in range(0, cols, PIECE)]
    wide_k = cols // GROUP
    for j in range(GROUP):
        value = jnp.concatenate([p[:, j * each : (j + 1) * each] for p in pieces], axis=1)
        stack[2 * flat * j : 2 * flat * (j + 1), :] = value.astype(BF16)
        if j == 0:
            moved = pltpu.roll(value, wide_k - 1, 1)
            stack[2 * flat * GROUP : 2 * flat * (GROUP + 1), :] = moved.astype(BF16)
    sources = table.shape[0] // FIELDS // wide

    def work(chunk):
        corner, frac_y, frac_x, frac_z, _, _ = gather_fields(table, chunk, wide)
        row_at, col_at = place_of(corner, cols)
        seen = dot(stack[...], one_hot(lax.div(col_at, GROUP), cols // GROUP))
        mixed = None
        for j, weight in enumerate(col_weights(col_at, frac_x)):
            at = 2 * flat * j
            term = (seen[at : at + flat] + seen[at + flat : at + 2 * flat]) * weight
            mixed = term if mixed is None else mixed + term
        weight = row_weights(row_at, frac_y, rows)
        low_level = jnp.sum(mixed[0:rows] * weight, axis=0, keepdims=True)
        high_level = jnp.sum(mixed[rows : 2 * rows] * weight, axis=0, keepdims=True)
        image = (1.0 - frac_z) * low_level + frac_z * high_level
        for i in range(wide):
            images[pl.ds(chunk * wide + i, 1), :] = image[:, i * LANES : (i + 1) * LANES]

    @pl.loop(0, sources // group)
    def _(turn):
        for i in range(group):
            work(turn * group + i)


def force_kernel(
    scale, wide, group, rates, images, others, table, members, *refs
):
    forcing, message, keep, hot, load, total, misfits = refs
    count, levels, rows, cols = members.shape
    flat = levels * rows
    sources = table.shape[0] // FIELDS
    half = sources // 2
    span = wide * LANES
    total[...] = jnp.zeros_like(total)

    @pl.loop(0, sources // wide // group)
    def _(turn):
        for i in range(group):
            chunk = turn * group + i
            corner, frac_y, frac_x, frac_z, innovation, precision = gather_fields(table, chunk, wide)
            row_at, col_at = place_of(corner, cols)
            parts = []
            for j in range(wide):
                source = chunk * wide + j
                swapped = jnp.where(source < half, source + half, source - half)
                parts.append(images[pl.ds(source, 1), :] + others[pl.ds(swapped, 1), :])
            misfit = precision * (jnp.concatenate(parts, axis=1) - innovation)
            for j in range(wide):
                misfits[pl.ds(chunk * wide + j, 1), :] = misfit[:, j * LANES : (j + 1) * LANES]
            weight = row_weights(row_at, frac_y, rows) * misfit
            stack = jnp.concatenate([weight * (1.0 - frac_z), weight * frac_z], axis=0)
            near = slice(i * span, (i + 1) * span)
            for j, weight in enumerate(col_weights(col_at, frac_x)):
                at = 2 * flat * j
                load[at : at + flat, near], load[at + flat : at + 2 * flat, near] = split(stack * weight)
            hot[:, near] = one_hot(lax.div(col_at, GROUP), cols // GROUP)
        total[...] += lax.dot_general(
            load[...], hot[...], (((1,), (1,)), ((), ())), preferred_element_type=F32
        )

    groups = []
    for j in range(GROUP + 1):
        at = 2 * flat * j
        groups.append(total[at : at + flat, :] + total[at + flat : at + 2 * flat, :])
    groups[0] = groups[0] + pltpu.roll(groups[GROUP], 1, 1)
    spread = spread_matrix(PIECE, True)
    each = PIECE // GROUP
    for t in range(cols // PIECE):
        value = jnp.concatenate([g[:, t * each : (t + 1) * each] for g in groups[:GROUP]], axis=1)
        high, low = split(value * scale)
        force = dot(high, spread) + dot(low, spread)
        for level in range(levels):
            forcing[level, :, t * PIECE : (t + 1) * PIECE] = force[level * rows : (level + 1) * rows]
    values = ((level, work_rows(members, forcing, level)) for level in range(levels))
    put_row_edges(False, rates, count, values, message)
    bit = lax.axis_index("row") & 1
    base = message.shape[0] - keep.shape[0]
    steps = (half // 2).bit_length() - 1

    def of_row(row):
        at = 2 * block_place(True, steps, row)
        return misfits[at : at + 2, :]

    for h in range(half // 4):
        zero, one = of_row(2 * h), of_row(2 * h + 1)
        message[base + 2 * h : base + 2 * h + 2, :], keep[2 * h : 2 * h + 2, :] = join(bit, one, zero)


def finish_kernel(rates, per_level, reach, part, received, keep, *refs):
    levels = reach.shape[0]
    bases, (out, returned, states, buffer, sems) = refs[:levels], refs[levels:]
    half = buffer.shape[0]
    outer_states(False, rates, per_level, half, part, received, states)
    members, _, _, cols = buffer.shape
    chunks = cols // LANES
    copies = []
    for m in range(members):
        for level in range(levels):
            for t in range(chunks):
                near = slice(t * LANES, (t + 1) * LANES)
                at = (2 * level * chunks + t) * members + m
                later = at + chunks * members
                entered = reach[level, 0] * states[at : at + 1, :] + reach[level, 1] * states[later : later + 1, :]
                buffer[m, level, :, near] = bases[level][m, :, near] + entered
        copies.append(pltpu.make_async_copy(buffer.at[m], out.at[m], sems.at[m]))
        copies[-1].start()
    at = 0
    for value in join_columns(1, keep, received, 2 * levels * half):
        returned[:, at : at + LANES] = value
        at += LANES
    for copy in copies:
        copy.wait()


def body(
    control, members, obs_corner, obs_count, offset_y, offset_x, offset_z, innovation, precision
):
    count, levels, rows, cols = control.shape
    n_mem, n_row, n_col = (lax.axis_size(name) for name in ("mem", "row", "col"))
    if n_mem != 2 or n_col != 2 or n_row & (n_row - 1):
        raise ValueError("unsupported mesh")
    grid_rows = rows * n_row
    block = min(256, cols)
    rates_x = filter_rates([cols / 16.0, cols / 64.0])
    rates_y = filter_rates([grid_rows / 2.0, rows / 2.0])
    scale = float(count * n_mem) ** -0.5
    flat = count * rows
    state_rows = levels * 2 * count * cols // LANES
    blocks = cols // block
    last = n_row.bit_length() - 2
    if levels * 2 * (blocks + 1) > HALF or last < 1:
        raise ValueError("unsupported sizes")

    per_level = 2 * (blocks + 1)
    corners = levels * 2 * count

    def columns(forward, edges, *args):
        (sent,) = call(
            functools.partial(columns_kernel, forward, block),
            [((flat, LANES), F32)],
            args,
            16 * MIB,
            1.0,
            apart=(len(args) - 1,),
        )
        return sent, swap(sent, "col", n_col, 0)

    def local(forward, level, *args):
        shape = (rows, cols) if forward else (count, rows, cols)
        return call(
            functools.partial(local_kernel, forward, level, block),
            [(shape, F32)],
            args,
            16 * MIB,
            2.5,
            apart=(len(args) - 1,),
            scratch=[pltpu.VMEM((flat, cols), F32)],
        )[0]

    def close(forward, unit, edges, states, received, keep, after, more=()):
        moving = keep.shape[0] * 2 // unit * (unit // 2) * (1 + len(more) // 2)
        states, message, keep = call(
            functools.partial(
                corner_kernel, forward, rates_y, last, n_row, rows, unit, count, block, len(after)
            ),
            [((state_rows, LANES), F32), ((corners + moving, LANES), F32), ((moving, LANES), F32)],
            (*after, *more, edges, states, received, keep),
            8 * MIB,
            0.4,
            apart=range(len(after)),
        )
        received = swap(message, "col", n_col, 0)
        (part,) = call(
            functools.partial(inner_kernel, levels, count, block),
            [((state_rows, LANES), F32)],
            (edges, states, message),
            8 * MIB,
            0.4,
        )
        return part, received, keep

    row_matrix, row_reach = row_constants(rates_y, count, rows, True)
    edges = edge_table(*col_constants(rates_x, cols, block, True))
    args = (obs_count, obs_corner, offset_y, offset_x, offset_z, innovation, precision, members)
    moving = n_row * FIELDS
    blocks_out = call(
        block_kernel,
        [((moving, LANES), F32)] * 2,
        args,
        OBS * MIB,
        1.5,
        apart=range(len(args)),
        scratch=[pltpu.VMEM(a.shape, a.dtype) for a in args[:-1]]
        + [pltpu.SemaphoreType.DMA((len(args) - 1,))],
    )
    (message,) = call(
        functools.partial(first_kernel, rates_y),
        [((state_rows, LANES), F32)],
        (control, blocks_out[1]),
        16 * MIB,
        1.0,
        apart=(1,),
    )
    partial = []
    sent = []

    def beside(step, message):
        if step == min(1, last - 1):
            sent.extend(columns(True, edges, control, edges, message))
            return sent[1:]
        if step == last:
            for level in range(levels):
                partial.append(local(True, level, control, members, *sent, edges, row_matrix, message))
        return ()

    states, received, (send,), keep = scan_rows(
        True, rates_y, rows, n_col * FIELDS, message, blocks_out, beside
    )
    last_bit = block_bits(True, last + 1)[last]
    pairs = []
    for m in range(n_mem):
        for r in range(n_row):
            pairs.append((m * n_row + r, (1 - m) * n_row + (r ^ (1 << last_bit))))
    row_other = swap(send, "row", n_row, last_bit)
    mem_keep = swap(keep, "mem", n_mem, 0)
    mem_other = lax.ppermute(send, ("mem", "row"), pairs)
    part, received, keep = close(
        True, n_col * FIELDS, edges, states, received, keep, partial, (row_other, mem_keep, mem_other)
    )
    sources = 4 * moving // FIELDS
    states, table = call(
        functools.partial(collect_kernel, rates_x, per_level, count),
        [((state_rows, LANES), F32), ((4 * moving, LANES), F32)],
        (part, received, keep),
        4 * MIB,
        0.1,
    )
    wide = 2
    group = 8
    (images,) = call(
        functools.partial(observe_kernel, scale, wide, group),
        [((sources, LANES), F32)],
        (states, members, row_reach, table, *partial),
        16 * MIB,
        2.8,
        scratch=[
            pltpu.VMEM((levels * rows, cols), F32),
            pltpu.VMEM((2 * levels * rows * (GROUP + 1), cols // GROUP), BF16),
        ],
    )
    others = swap(images, "mem", n_mem, 0)

    row_matrix, row_reach = row_constants(rates_y, count, rows, False)
    edges = edge_table(*col_constants(rates_x, cols, block, False))
    forcing, message, keep = call(
        functools.partial(force_kernel, scale, wide, group, rates_y),
        [
            ((levels, rows, cols), F32),
            ((state_rows + n_row, LANES), F32),
            ((n_row, LANES), F32),
        ],
        (images, others, table, members),
        24 * MIB,
        4.0,
        scratch=[
            pltpu.VMEM((cols // GROUP, group * wide * LANES), BF16),
            pltpu.VMEM((2 * levels * rows * (GROUP + 1), group * wide * LANES), BF16),
            pltpu.VMEM((2 * levels * rows * (GROUP + 1), cols // GROUP), F32),
            pltpu.VMEM((sources, LANES), F32),
        ],
    )
    bases = []
    sent = []

    def back_beside(step, message):
        if step == 0:
            sent.extend(columns(False, edges, members, forcing, edges, message))
            return sent[1:]
        now = []
        if step == 1 or step == last:
            for level in range(len(bases), levels if step == last else levels - 1):
                now.append(local(False, level, control, members, forcing, *sent, edges, row_matrix, message))
        bases.extend(now)
        return now

    states, received, _, keep = scan_rows(False, rates_y, rows, n_col, message, (keep,), back_beside)
    part, received, keep = close(False, n_col, edges, states, received, keep, bases)
    return pl.pallas_call(
        functools.partial(finish_kernel, rates_x, per_level),
        out_shape=[
            jax.ShapeDtypeStruct(control.shape, F32),
            jax.ShapeDtypeStruct(precision.shape, F32),
        ],
        in_specs=[pl.BlockSpec(memory_space=pltpu.VMEM)] * (4 + levels),
        out_specs=[pl.BlockSpec(memory_space=pl.ANY), pl.BlockSpec(memory_space=pltpu.VMEM)],
        scratch_shapes=[
            pltpu.VMEM((state_rows, LANES), F32),
            pltpu.VMEM(control.shape, F32),
            pltpu.SemaphoreType.DMA((count,)),
        ],
        compiler_params=pltpu.CompilerParams(vmem_limit_bytes=8 * MIB),
        cost_estimate=cost(2.0),
    )(row_reach, part, received, keep, *bases)


def solution(mesh):
    spread = P(("mem", "row", "col"), None)
    grid = P("mem", None, "row", "col")
    return jax.shard_map(
        body,
        mesh=mesh,
        in_specs=(grid, grid) + (spread,) * 7,
        out_specs=(grid, spread),
        check_vma=False,
    )
```

```python
import functools

import jax
import jax.numpy as jnp
import numpy as np
from jax import lax
from jax.experimental import pallas as pl
from jax.experimental.pallas import tpu as pltpu
from jax.sharding import PartitionSpec as P

LANES = 128
HALF = LANES // 2
FIELDS = 6
TURNED = 8
GROUP = 4
PIECE = 256
F32 = jnp.float32
BF16 = jnp.bfloat16
MIB = 1 << 20
OBS = 57


def filter_rates(lengths):
    decay = np.exp(-1.0 / np.asarray(lengths, np.float64))
    weight = ((1.0 - decay**2) ** 3 / (1.0 + decay**2)) ** 0.25
    return decay, weight


def row_reach_of(rates, size, forward):
    places = np.arange(size)
    steps = places + 1 if forward else size - places
    reach = np.zeros((len(rates[0]), 2, size, LANES), np.float32)
    for level, (a, b) in enumerate(zip(*rates)):
        reach[level, 0] = (b * steps * a**steps)[:, None]
        reach[level, 1] = (a**steps)[:, None]
    return reach


def by_level(level, values):
    chosen = jnp.full(level.shape, float(values[0]), F32)
    for i in range(1, len(values)):
        chosen = jnp.where(level == i, float(values[i]), chosen)
    return chosen


def two_pass(a, b, lag):
    steps = jnp.maximum(lag, 0).astype(F32)
    return jnp.where(lag >= 0, float(b**2) * (steps + 1.0) * jnp.exp(steps * float(np.log(a))), 0.0)


def table_kernel(forward, rates_x, rates_y, members, block, *refs):
    edges, row_matrix, *passed = refs[len(refs) // 2 if len(refs) > 2 else 0 :]
    for out, ref in zip(passed, refs[1:]):
        out[...] = ref[...]
    levels = len(rates_x[0])
    size = edges.shape[1]
    blocks = size // block
    per_level = 2 * (blocks + 1)
    logs = [float(np.log(a)) for a in rates_x[0]]

    def lanes_of(lane):
        level = lax.div(lane, per_level)
        inner = lax.rem(lane, per_level)
        k = lax.div(inner, 2)
        return level, k, (inner & 1) == 1, (lane < levels * per_level)

    def place_of_column(column):
        return column if forward else size - 1 - column

    shape = (HALF, size)
    level, k, second, used = lanes_of(lax.broadcasted_iota(jnp.int32, shape, 0))
    place = place_of_column(lax.broadcasted_iota(jnp.int32, shape, 1))
    steps = place + 1 - jnp.where(k == blocks, 0, (k + 1) * block)
    used = used & (steps > 0)
    steps = jnp.maximum(steps, 0).astype(F32)
    power = jnp.exp(steps * by_level(level, logs))
    value = jnp.where(second, power, by_level(level, rates_x[1]) * steps * power)
    high, low = split(jnp.where(used, value, 0.0))
    edges[0:HALF, :] = high
    edges[HALF : 2 * HALF, :] = high
    edges[2 * HALF : 3 * HALF, :] = low
    edges[3 * HALF : 4 * HALF, :] = jnp.zeros(shape, BF16)

    first = 4 * HALF
    row = lax.broadcasted_iota(jnp.int32, (block, block), 0)
    column = lax.broadcasted_iota(jnp.int32, (block, block), 1)
    lag = column - row if forward else row - column
    for i, (a, b) in enumerate(zip(*rates_x)):
        for h, value in enumerate(split(two_pass(a, b, lag))):
            at = (h * levels + i) * block
            edges[first : first + block, at : at + block] = value
    at = 2 * levels * block
    if at < size:
        edges[first : first + block, at:] = jnp.zeros((block, size - at), BF16)

    first += block
    shape = (LANES, LANES)
    lane = lax.broadcasted_iota(jnp.int32, shape, 1)
    level, k, second, used = lanes_of(lane & (HALF - 1))
    stop = jnp.where(k == blocks, size, (k + 1) * block)
    begin = jnp.where(k == blocks, 0, k * block)
    log, weight = by_level(level, logs), by_level(level, rates_x[1])
    for t in range(size // LANES):
        place = place_of_column(t * LANES + lax.broadcasted_iota(jnp.int32, shape, 0))
        left = stop - 1 - place
        inside = used & (place >= begin) & (left >= 0)
        left = jnp.maximum(left, 0).astype(F32)
        value = weight * jnp.exp(left * log)
        value = jnp.where(inside, jnp.where(second, weight * (left + 1.0) * value, value), 0.0)
        high = value.astype(BF16)
        near = slice(t * LANES, (t + 1) * LANES)
        edges[first : first + LANES, near] = jnp.where(lane < HALF, high.astype(F32), value - high.astype(F32)).astype(BF16)

    flat = row_matrix.shape[2]
    height = flat // members
    row = lax.broadcasted_iota(jnp.int32, (flat, flat), 0)
    column = lax.broadcasted_iota(jnp.int32, (flat, flat), 1)
    same = lax.div(row, height) == lax.div(column, height)
    lag = row - column if forward else column - row
    for i, (a, b) in enumerate(zip(*rates_y)):
        high, low = split(jnp.where(same, two_pass(a, b, lag), 0.0))
        row_matrix[0, i] = high
        row_matrix[1, i] = low


class EdgeTable:
    def __init__(self, ref, levels, block):
        self.ref, self.levels, self.block = ref, levels, block
        self.size = ref.shape[1]
        self.first = 4 * HALF

    def reach(self, near=slice(None)):
        return self.ref[0 : self.first, near]

    def matrix(self, level):
        return jnp.concatenate([self.square(level), self.square(self.levels + level), self.square(level)], axis=0)

    def square(self, index):
        return self.ref[self.first : self.first + self.block, index * self.block : (index + 1) * self.block]

    def edge(self):
        at = self.first + self.block
        rows = [self.ref[at : at + LANES, t : t + LANES] for t in range(0, self.size, LANES)]
        return jnp.concatenate(rows + rows, axis=0)


def split(value):
    high = value.astype(BF16)
    return high, (value - high.astype(F32)).astype(BF16)


def dot(left, right):
    return jnp.dot(left, right, preferred_element_type=F32)


def lane_kinds(shape, blocks, level):
    lane = lax.broadcasted_iota(jnp.int32, shape, 1)
    per_level = 2 * (blocks + 1)
    mine = (lane >= level * per_level) & (lane < (level + 1) * per_level)
    return mine, lax.rem(lane, per_level) >= 2 * blocks


def edge_states(value, table, blocks, level):
    high, low = split(value)
    both = dot(jnp.concatenate([high, low], axis=1), table.edge())
    mine, _ = lane_kinds(both.shape, blocks, level)
    return jnp.where(mine, both + pltpu.roll(both, HALF, 1), 0.0)


def packed(states):
    lane = lax.broadcasted_iota(jnp.int32, states.shape, 1)
    high = states.astype(BF16).astype(F32)
    low = states - high
    first = jnp.where(lane < HALF, high, pltpu.roll(low, HALF, 1))
    second = jnp.where(lane < HALF, high, 0.0)
    return jnp.concatenate([first.astype(BF16), second.astype(BF16)], axis=1)


def dot_left(left, value):
    high, low = split(value)
    return dot(left, jnp.concatenate([high, high, low], axis=0))


def dot_right(value, right, *more):
    high, low = split(value)
    left = jnp.concatenate([high, high, low] + [x for x, _ in more], axis=1)
    return dot(left, jnp.concatenate([right] + [x for _, x in more], axis=0))


def cost(micros):
    return pl.CostEstimate(flops=0, bytes_accessed=int(micros * 3.6e6), transcendentals=0)


def call(kernel, outs, args, limit, micros, apart=(), scratch=()):
    return pl.pallas_call(
        kernel,
        out_shape=[jax.ShapeDtypeStruct(shape, dtype) for shape, dtype in outs],
        in_specs=[
            pl.BlockSpec(memory_space=pl.ANY if i in apart else pltpu.VMEM) for i in range(len(args))
        ],
        out_specs=[pl.BlockSpec(memory_space=pltpu.VMEM) for _ in outs],
        scratch_shapes=list(scratch),
        compiler_params=pltpu.CompilerParams(vmem_limit_bytes=limit),
        cost_estimate=cost(micros),
    )(*args)


def level_rows(ref, level):
    value = ref[:, level]
    return value.reshape(value.shape[0] * value.shape[1], value.shape[2])


def work_rows(members_ref, forcing_ref, level):
    value = members_ref[:, level].astype(F32) * forcing_ref[level][None]
    return value.reshape(value.shape[0] * value.shape[1], value.shape[2])


def row_weights_at_edge(forward, rates, level, members, size):
    a, b = rates[0][level], rates[1][level]
    shape = (members, members * size)
    member = lax.broadcasted_iota(jnp.int32, shape, 0)
    place = lax.broadcasted_iota(jnp.int32, shape, 1)
    row = lax.rem(place, size)
    left = (size - 1 - row if forward else row).astype(F32)
    power = jnp.where(lax.div(place, size) == member, float(b) * jnp.exp(left * float(np.log(a))), 0.0)
    high, low = split(jnp.concatenate([power, float(b) * (left + 1.0) * power], axis=0))
    return jnp.concatenate([high, low, high], axis=1)


def put_row_edges(forward, rates, members, values, message):
    for level, value in values:
        size = value.shape[0] // members
        states = dot_left(row_weights_at_edge(forward, rates, level, members, size), value)
        lay_states(message, level, states)


def lay_states(message, level, states):
    half = states.shape[0] // 2
    chunks = states.shape[1] // LANES
    for s in range(2):
        for t in range(chunks):
            at = ((2 * level + s) * chunks + t) * half
            message[at : at + half, :] = states[s * half : (s + 1) * half, t * LANES : (t + 1) * LANES]


def take_states(states, level, half, chunks):
    rows = []
    for s in range(2):
        at = (2 * level + s) * chunks * half
        rows.append(
            jnp.concatenate([states[at + t * half : at + (t + 1) * half, :] for t in range(chunks)], axis=1)
        )
    return jnp.concatenate(rows, axis=0)


def first_kernel(rates, *refs):
    sources, (message, send, keep), places, sems = refs[:8], refs[8:11], refs[11:19], refs[19]
    control, counts, *fields = places
    levels = control.shape[1]
    copies = []
    for i, (source, place) in enumerate(zip(sources, places)):
        parts = [(source, place)]
        if i == 0:
            parts = [(source.at[:, level], place.at[:, level]) for level in range(levels)]
        for pair in parts:
            copies.append(pltpu.make_async_copy(*pair, sems.at[len(copies)]))
            copies[-1].start()
    for copy in copies[levels:]:
        copy.wait()
    rows = counts.shape[1] // 2
    steps = rows.bit_length() - 1
    order = sorted(range(rows), key=lambda row: block_place(True, steps, row))
    bit = (lax.axis_index("row") >> block_bits(True, steps)[0]) & 1
    slot = lax.broadcasted_iota(jnp.int32, (1, LANES), 1)

    def read(tile, f):
        value = fields[f][:, tile * LANES : (tile + 1) * LANES].astype(F32)
        if f == FIELDS - 1:
            value = jnp.where(slot < counts[:, tile : tile + 1], value, 0.0)
        return value

    at = 0
    for h in range(0, rows, 2):
        for tile_col in range(2):
            for f in range(FIELDS):
                zero, one = read(2 * order[h] + tile_col, f), read(2 * order[h + 1] + tile_col, f)
                send[at : at + 1, :], keep[at : at + 1, :] = join(bit, one, zero)
                at += 1

    def values():
        for level in range(levels):
            copies[level].wait()
            yield level, level_rows(control, level)

    put_row_edges(True, rates, control.shape[0], values(), message)


def columns_kernel(block, members, forcing, edges, _, out):
    levels = members.shape[1]
    table = EdgeTable(edges, levels, block)
    total = None
    for level in range(levels):
        states = edge_states(work_rows(members, forcing, level), table, table.size // block, level)
        total = states if total is None else total + states
    out[...] = total


def entering_rows(forward, rates, level, size):
    a, b = rates[0][level], rates[1][level]
    place = lax.broadcasted_iota(jnp.int32, (1, size), 1)
    steps = (place + 1 if forward else size - place).astype(F32)
    power = jnp.exp(steps * float(np.log(a)))
    return float(b) * steps * power, power


def corner_kernel(forward, rates, step, count, tile, unit, half, block, after, *refs):
    *refs, edges, before, received, keep_in, states, message, keep = refs
    more, refs = refs[:after], refs[after:]
    last_states(forward, rates, step, count, tile, before, received, states)
    levels = len(rates[0])
    table = EdgeTable(edges, levels, block)
    chunks = table.size // LANES
    at = 0
    for level in range(levels):
        corner = edge_states(take_states(states, level, half, chunks), table, table.size // block, level)
        message[at : at + 2 * half, :] = corner
        at += 2 * half
    bit = (lax.axis_index("row") >> block_bits(forward, step + 1)[step]) & 1
    place = lax.axis_index("col")
    base, size = before.shape[0], keep_in.shape[0]
    each = unit // 2
    if refs:
        pairs = [(keep_in[...], refs[0][...]), (refs[1][...], refs[2][...])]
    else:
        pairs = [(keep_in[...], received[base : base + size, :])]
    start, at = at, 0
    for mine, other in pairs:
        for value in join(bit, mine, other):
            for i in range(0, size, unit):
                send, stay = join(place, value[i + each : i + unit], value[i : i + each])
                message[start + at : start + at + each, :] = send
                keep[at : at + each, :] = stay
                at += each
    if forward:
        turned = more[0][...]
        for ref in more[1:]:
            turned = turned + ref[...]
        for t in range(turned.shape[1] // LANES):
            first = start + at + t * turned.shape[0]
            message[first : first + turned.shape[0], :] = turned[:, t * LANES : (t + 1) * LANES]


def inner_kernel(levels, half, block, edges, states, message, part):
    table = EdgeTable(edges, levels, block)
    size = table.size
    blocks = size // block
    for level in range(levels):
        value = take_states(states, level, half, size // LANES)
        pairs = value.shape[0]
        corner = message[level * pairs : (level + 1) * pairs, :]
        _, whole = lane_kinds(corner.shape, blocks, level)
        carry = dot(packed(jnp.where(whole, 0.0, corner)), table.reach())
        stack = jnp.concatenate([value[:, at : at + block] for at in range(0, size, block)], axis=0)
        stack = dot_right(stack, table.matrix(level))
        rows = [stack[n * pairs : (n + 1) * pairs] for n in range(blocks)]
        lay_states(part, level, jnp.concatenate(rows, axis=1) + carry)


def outer_states(forward, rates, per_level, half, part, received, states):
    place = lax.axis_index("col")
    live = jnp.where(place == (1 if forward else 0), 1.0, 0.0)
    levels = len(rates[0])
    chunks = part.shape[0] // (2 * levels * half)
    for level in range(levels):
        lane = (level + 1) * per_level - 2
        ones, twos = entering_rows(forward, rates, level, chunks * LANES)
        for s in range(2):
            at = (2 * level + s) * half
            corner = received[at : at + half, :] * live
            one, two = corner[:, lane : lane + 1], corner[:, lane + 1 : lane + 2]
            for t in range(chunks):
                at = ((2 * level + s) * chunks + t) * half
                near = slice(t * LANES, (t + 1) * LANES)
                states[at : at + half, :] = part[at : at + half, :] + one * ones[:, near] + two * twos[:, near]


def join_columns(each, keep, received, base):
    place = lax.axis_index("col")
    for i in range(0, keep.shape[0], each):
        yield from join(place, keep[i : i + each, :], received[base + i : base + i + each, :])


def collect_kernel(rates, per_level, half, part, received, keep, states, table, columns):
    outer_states(True, rates, per_level, half, part, received, states)
    at = 0
    for value in join_columns(FIELDS, keep, received, 2 * len(rates[0]) * half):
        table[at : at + FIELDS, :] = value
        at += FIELDS
    live = jnp.where(lax.axis_index("col") == 1, 1.0, 0.0)
    start = 2 * len(rates[0]) * half + keep.shape[0]
    for t in range(columns.shape[0] // LANES):
        turned = received[start + t * TURNED : start + (t + 1) * TURNED, :] * live
        turned = jnp.concatenate([turned, jnp.zeros((LANES - TURNED, LANES), F32)], axis=0)
        columns[t * LANES : (t + 1) * LANES, :] = jnp.transpose(turned)


def block_bits(forward, steps):
    bits = list(range(steps))
    if forward:
        bits[0], bits[-1] = bits[-1], bits[0]
    return bits


def block_place(forward, steps, row):
    return sum(((row >> bit) & 1) << i for i, bit in enumerate(block_bits(forward, steps)))


def transfer(rates, level, steps):
    a, b = rates[0][level], rates[1][level]
    return float(a**steps), float(b * steps * a**steps)


def pick(index, values):
    chosen = jnp.float32(values[0])
    for i in range(1, len(values)):
        chosen = jnp.where(index == i, jnp.float32(values[i]), chosen)
    return chosen


def reach_of(forward, rates, step, count, tile, level):
    row = lax.axis_index("row")
    line = row if forward else count - 1 - row
    upper = ((line >> step) & 1) == 1
    inside = line & ((1 << step) - 1)
    table = [transfer(rates, level, q * tile) for q in range(1 << step)]
    near1 = jnp.where(upper, pick(inside, [x[0] for x in table]), 0.0)
    near2 = jnp.where(upper, pick(inside, [x[1] for x in table]), 0.0)
    return near1, near2, upper


def join(bit, mine, other):
    return jnp.where(bit == 1, other, mine), jnp.where(bit == 1, mine, other)


def new_states(forward, rates, step, count, tile, level, before, received, first, second):
    near1, near2, upper = reach_of(forward, rates, step, count, tile, level)
    got1, got2 = received[first, :], received[second, :]
    new1 = near1 * got1
    new2 = near1 * got2 + near2 * got1
    if before is not None:
        new1 = before[first, :] + new1
        new2 = before[second, :] + new2
    return new1, new2, got1, got2, upper


def round_kernel(forward, rates, step, count, tile, unit, spans, apart, after, *refs):
    sent, received, keep_in, *refs = refs
    before = refs.pop(0) if step else None
    blocks = refs.pop(0) if apart else received
    message, keep, states, *send = refs[after:]
    levels = len(rates[0])
    base = states.shape[0]
    start = 0 if apart else base
    part = base // (2 * levels)
    for level in range(levels):
        at = 2 * level * part
        first, second = slice(at, at + part), slice(at + part, at + 2 * part)
        new1, new2, got1, got2, upper = new_states(
            forward, rates, step, count, tile, level, before, received, first, second
        )
        states[first, :] = new1
        states[second, :] = new2
        far1, far2 = transfer(rates, level, tile << step)
        own1 = jnp.where(upper, 1.0, far1)
        own2 = jnp.where(upper, 0.0, far2)
        his1 = jnp.where(upper, far1, 1.0)
        his2 = jnp.where(upper, far2, 0.0)
        all1, all2 = sent[first, :], sent[second, :]
        message[first, :] = own1 * all1 + his1 * got1
        message[second, :] = own1 * all2 + own2 * all1 + his1 * got2 + his2 * got1
    row = lax.axis_index("row")
    bits = block_bits(forward, count.bit_length() - 1)
    bit = (row >> bits[step]) & 1
    next_bit = (row >> bits[step + 1]) & 1
    size = unit << step
    place, first = (send[0], 0) if send else (message, base)

    def span(h):
        near = slice(h * size, (h + 1) * size)
        other = blocks[start + h * size : start + (h + 1) * size, :]
        return jnp.concatenate(join(bit, keep_in[near, :], other), axis=0)

    at = 0
    for h in range(0, spans // 2, 2):
        moved, stay = join(next_bit, span(h + 1), span(h))
        place[first + at : first + at + 2 * size, :] = moved
        keep[at : at + 2 * size, :] = stay
        at += 2 * size


def last_states(forward, rates, step, count, tile, before, received, states):
    levels = len(rates[0])
    part = before.shape[0] // (2 * levels)
    for level in range(levels):
        at = 2 * level * part
        first, second = slice(at, at + part), slice(at + part, at + 2 * part)
        states[first, :], states[second, :], *_ = new_states(
            forward, rates, step, count, tile, level, before, received, first, second
        )


def swap(value, axis, size, step):
    return lax.ppermute(value, axis, [(i, i ^ (1 << step)) for i in range(size)])


def scan_rows(forward, rates, tile, unit, message, blocks, beside):
    count = lax.axis_size("row")
    steps = count.bit_length() - 1
    spans = count
    apart = len(blocks) == 2
    keep = blocks[-1]
    moving = keep.shape[0]
    state_rows = message.shape[0] - (0 if apart else moving)
    states = None
    for step in range(steps - 1):
        received = swap(message, "row", count, step)
        args = (message, received, keep) + (() if step == 0 else (states,))
        if apart:
            args += (swap(blocks[0], "row", count, block_bits(forward, steps)[step]),)
        after = beside(step, message)
        first = len(args)
        args = args + tuple(after)
        kernel = functools.partial(
            round_kernel, forward, rates, step, count, tile, unit, spans, apart, len(after)
        )
        outs = [state_rows + moving, moving, state_rows]
        if forward and step == steps - 2:
            outs = [state_rows, moving, state_rows, moving]
        outs = [((rows, LANES), F32) for rows in outs]
        message, keep, states, *send = call(kernel, outs, args, 4 * MIB, 0.1, apart=range(first, len(args)))
        spans //= 2
        apart = False
    received = swap(message, "row", count, steps - 1)
    beside(steps - 1, message)
    return states, received, send, keep


def local_kernel(forward, level, block, *refs):
    if forward:
        control, members, edges, row_matrix, out, whole_out, between, scratch = refs
    else:
        control, members, forcing, columns, received, edges, row_matrix, _, out, between, scratch = refs
    count, levels, rows, cols = control.shape
    table = EdgeTable(edges, levels, block)
    high = row_matrix[0, level]
    left = jnp.concatenate([high, row_matrix[1, level], high], axis=1)
    mine, whole = lane_kinds((count * rows, LANES), cols // block, level)
    if forward:
        value = level_rows(control, level)
        states = edge_states(value, table, cols // block, level)
        entering = jnp.where(whole, 0.0, states)
        turned = jnp.transpose(dot_left(left, jnp.where(whole, states, 0.0)))
        first = (level + 1) * 2 * (cols // block + 1) - 2
        whole_out[...] = jnp.zeros_like(whole_out)
        whole_out[2 * level : 2 * level + 2, :] = turned[first : first + 2, :]
    else:
        value = work_rows(members, forcing, level)
        live = jnp.where(lax.axis_index("col") == 0, 1.0, 0.0)
        entering = jnp.where(whole, received[...] * live, columns[...])
        entering = jnp.where(mine, entering, 0.0)
    entering = packed(entering)
    weights = table.matrix(level)
    spans = [slice(at, at + block) for at in range(0, cols, block)]
    for near in spans:
        between[:, near] = dot_right(value[:, near], weights, (entering, table.reach(near)))
    for near in spans:
        scratch[:, near] = dot_left(left, between[:, near])
    if forward:
        total = None
        for m in range(count):
            term = members[m, level].astype(F32) * scratch[m * rows : (m + 1) * rows, :]
            total = term if total is None else total + term
        out[...] = total
    else:
        for m in range(count):
            out[m] = control[m, level] + scratch[m * rows : (m + 1) * rows, :]


def bulk_fields(table, cols, weights, places):
    sources = table.shape[0] // FIELDS
    fields = [table[pl.ds(f, sources, stride=FIELDS), :] for f in range(FIELDS)]
    corner = fields[0].astype(jnp.int32)
    row_at = lax.div(corner, cols)
    col_at = corner - row_at * cols
    values = col_weights(col_at, fields[2]) + [fields[1]] + fields[3:]
    for i, value in enumerate(values):
        weights[i] = value
    places[0] = row_at
    places[1] = lax.div(col_at, GROUP)


def source_row(ref, i, chunk, wide):
    rows = [ref[i, pl.ds(chunk * wide + j, 1), :] for j in range(wide)]
    return jnp.concatenate(rows, axis=1)


def row_weights(row_at, frac, rows):
    places = lax.broadcasted_iota(jnp.int32, (rows, row_at.shape[1]), 0)
    near = jnp.where(places == row_at, 1.0 - frac, 0.0)
    return near + jnp.where(places == row_at + 1, frac, 0.0)


def one_hot(col_at, cols):
    places = lax.broadcasted_iota(jnp.int32, (cols, col_at.shape[1]), 0)
    return jnp.where(places == col_at, 1.0, 0.0).astype(BF16)


def spread_matrix(size, back):
    one = lax.broadcasted_iota(jnp.int32, (size, size), 1 if back else 0)
    two = lax.broadcasted_iota(jnp.int32, (size, size), 0 if back else 1)
    at = (one & (GROUP - 1)) * (size // GROUP) + lax.div(one, GROUP)
    return jnp.where(at == two, 1.0, 0.0).astype(BF16)


def col_weights(col_at, frac):
    within = col_at & (GROUP - 1)
    weights = []
    for j in range(GROUP + 1):
        weight = jnp.where(within == j, 1.0 - frac, 0.0)
        weights.append(weight + jnp.where(within == j - 1, frac, 0.0))
    return weights


def observe_kernel(scale, wide, group, rates, states, columns, members, reach, table, *refs):
    count, levels, rows, cols = members.shape
    partial, (images, field, stack, weights, places) = refs[:levels], refs[levels:]
    bulk_fields(table, cols, weights, places)
    chunks = cols // LANES
    for level in range(levels):
        reach1, reach2 = reach[level, 0], reach[level, 1]
        ones, twos = entering_rows(True, rates, level, cols)
        spans = [slice(t * LANES, (t + 1) * LANES) for t in range(chunks)]
        totals = [partial[level][:, near] for near in spans]
        for m in range(count):
            across = columns[m * rows : (m + 1) * rows, :]
            one = jnp.broadcast_to(across[:, 2 * level : 2 * level + 1], (rows, LANES))
            two = jnp.broadcast_to(across[:, 2 * level + 1 : 2 * level + 2], (rows, LANES))
            for t, near in enumerate(spans):
                at = (2 * level * chunks + t) * count + m
                later = at + chunks * count
                entered = reach1 * states[at : at + 1, :] + reach2 * states[later : later + 1, :]
                entered = entered + one * ones[:, near] + two * twos[:, near]
                totals[t] = totals[t] + members[m, level, :, near].astype(F32) * entered
        for t, near in enumerate(spans):
            field[level * rows : (level + 1) * rows, near] = totals[t] * scale
    flat = levels * rows
    high, low = split(field[...])
    both = jnp.concatenate([high, low], axis=0)
    spread = spread_matrix(PIECE, False)
    each = PIECE // GROUP
    pieces = [dot(both[:, at : at + PIECE], spread) for at in range(0, cols, PIECE)]
    wide_k = cols // GROUP
    for j in range(GROUP):
        value = jnp.concatenate([p[:, j * each : (j + 1) * each] for p in pieces], axis=1)
        stack[2 * flat * j : 2 * flat * (j + 1), :] = value.astype(BF16)
        if j == 0:
            moved = pltpu.roll(value, wide_k - 1, 1)
            stack[2 * flat * GROUP : 2 * flat * (GROUP + 1), :] = moved.astype(BF16)
    sources = table.shape[0] // FIELDS // wide

    def work(chunk):
        row_at, group_at = (source_row(places, i, chunk, wide) for i in range(2))
        *near, frac_y, frac_z = (source_row(weights, i, chunk, wide) for i in range(GROUP + 3))
        seen = dot(stack[...], one_hot(group_at, cols // GROUP))
        mixed = None
        for j, weight in enumerate(near):
            at = 2 * flat * j
            term = (seen[at : at + flat] + seen[at + flat : at + 2 * flat]) * weight
            mixed = term if mixed is None else mixed + term
        weight = row_weights(row_at, frac_y, rows)
        low_level = jnp.sum(mixed[0:rows] * weight, axis=0, keepdims=True)
        high_level = jnp.sum(mixed[rows : 2 * rows] * weight, axis=0, keepdims=True)
        image = (1.0 - frac_z) * low_level + frac_z * high_level
        for i in range(wide):
            images[pl.ds(chunk * wide + i, 1), :] = image[:, i * LANES : (i + 1) * LANES]

    if sources == group:
        for chunk in range(sources):
            work(chunk)
    else:

        @pl.loop(0, sources // group)
        def _(turn):
            for i in range(group):
                work(turn * group + i)


def force_kernel(
    scale, wide, group, rates, images, others, table, members, *refs
):
    forcing, message, keep, hot, load, total, misfits, weights, places = refs
    bulk_fields(table, members.shape[3], weights, places)
    count, levels, rows, cols = members.shape
    flat = levels * rows
    sources = table.shape[0] // FIELDS
    half = sources // 2
    span = wide * LANES
    total[...] = jnp.zeros_like(total)

    @pl.loop(0, sources // wide // group)
    def _(turn):
        for i in range(group):
            chunk = turn * group + i
            row_at, group_at = (source_row(places, i, chunk, wide) for i in range(2))
            *near_weights, frac_y, frac_z, innovation, precision = (
                source_row(weights, i, chunk, wide) for i in range(GROUP + 5)
            )
            parts = []
            for j in range(wide):
                source = chunk * wide + j
                swapped = jnp.where(source < half, source + half, source - half)
                parts.append(images[pl.ds(source, 1), :] + others[pl.ds(swapped, 1), :])
            misfit = precision * (jnp.concatenate(parts, axis=1) - innovation)
            for j in range(wide):
                misfits[pl.ds(chunk * wide + j, 1), :] = misfit[:, j * LANES : (j + 1) * LANES]
            weight = row_weights(row_at, frac_y, rows) * misfit
            stack = jnp.concatenate([weight * (1.0 - frac_z), weight * frac_z], axis=0)
            near = slice(i * span, (i + 1) * span)
            for j, weight in enumerate(near_weights):
                at = 2 * flat * j
                load[at : at + flat, near], load[at + flat : at + 2 * flat, near] = split(stack * weight)
            hot[:, near] = one_hot(group_at, cols // GROUP)
        total[...] += lax.dot_general(
            load[...], hot[...], (((1,), (1,)), ((), ())), preferred_element_type=F32
        )

    groups = []
    for j in range(GROUP + 1):
        at = 2 * flat * j
        groups.append(total[at : at + flat, :] + total[at + flat : at + 2 * flat, :])
    groups[0] = groups[0] + pltpu.roll(groups[GROUP], 1, 1)
    spread = spread_matrix(PIECE, True)
    each = PIECE // GROUP
    for t in range(cols // PIECE):
        value = jnp.concatenate([g[:, t * each : (t + 1) * each] for g in groups[:GROUP]], axis=1)
        high, low = split(value * scale)
        force = dot(high, spread) + dot(low, spread)
        for level in range(levels):
            forcing[level, :, t * PIECE : (t + 1) * PIECE] = force[level * rows : (level + 1) * rows]
    values = ((level, work_rows(members, forcing, level)) for level in range(levels))
    put_row_edges(False, rates, count, values, message)
    bit = lax.axis_index("row") & 1
    base = message.shape[0] - keep.shape[0]
    steps = (half // 2).bit_length() - 1

    def of_row(row):
        at = 2 * block_place(True, steps, row)
        return misfits[at : at + 2, :]

    for h in range(half // 4):
        zero, one = of_row(2 * h), of_row(2 * h + 1)
        message[base + 2 * h : base + 2 * h + 2, :], keep[2 * h : 2 * h + 2, :] = join(bit, one, zero)


def finish_kernel(rates, per_level, reach, part, received, keep, *refs):
    levels = reach.shape[0]
    bases, (out, returned, states, buffer, sems) = refs[:levels], refs[levels:]
    half = buffer.shape[0]
    outer_states(False, rates, per_level, half, part, received, states)
    members, _, _, cols = buffer.shape
    chunks = cols // LANES
    copies = []
    for m in range(members):
        for level in range(levels):
            for t in range(chunks):
                near = slice(t * LANES, (t + 1) * LANES)
                at = (2 * level * chunks + t) * members + m
                later = at + chunks * members
                entered = reach[level, 0] * states[at : at + 1, :] + reach[level, 1] * states[later : later + 1, :]
                buffer[m, level, :, near] = bases[level][m, :, near] + entered
        copies.append(pltpu.make_async_copy(buffer.at[m], out.at[m], sems.at[m]))
        copies[-1].start()
    at = 0
    for value in join_columns(1, keep, received, 2 * levels * half):
        returned[:, at : at + LANES] = value
        at += LANES
    for copy in copies:
        copy.wait()


def body(
    control, members, obs_corner, obs_count, offset_y, offset_x, offset_z, innovation, precision
):
    count, levels, rows, cols = control.shape
    n_mem, n_row, n_col = (lax.axis_size(name) for name in ("mem", "row", "col"))
    if n_mem != 2 or n_col != 2 or n_row & (n_row - 1):
        raise ValueError("unsupported mesh")
    grid_rows = rows * n_row
    block = min(256, cols)
    rates_x = filter_rates([cols / 16.0, cols / 64.0])
    rates_y = filter_rates([grid_rows / 2.0, rows / 2.0])
    scale = float(count * n_mem) ** -0.5
    flat = count * rows
    state_rows = levels * 2 * count * cols // LANES
    blocks = cols // block
    last = n_row.bit_length() - 2
    if levels * 2 * (blocks + 1) > HALF or last < 1:
        raise ValueError("unsupported sizes")

    per_level = 2 * (blocks + 1)
    corners = levels * 2 * count

    def tables(forward, *after):
        return call(
            functools.partial(table_kernel, forward, rates_x, rates_y, count, block),
            [((4 * HALF + block + LANES, cols), BF16), ((2, levels, flat, flat), BF16)]
            + [(a.shape, a.dtype) for a in after[1:]],
            after,
            8 * MIB,
            1.0,
        )

    def local(forward, level, *args):
        outs = [((rows, cols), F32), ((TURNED, flat), F32)] if forward else [((count, rows, cols), F32)]
        return call(
            functools.partial(local_kernel, forward, level, block),
            outs,
            args,
            16 * MIB,
            2.5,
            apart=() if forward else (len(args) - 1,),
            scratch=[pltpu.VMEM((flat, cols), F32)] * 2,
        )

    def close(forward, unit, edges, states, received, keep, after, more=()):
        moving = keep.shape[0] * 2 // unit * (unit // 2) * (1 + len(more) // 2)
        turned = TURNED * flat // LANES if forward else 0
        states, message, keep = call(
            functools.partial(
                corner_kernel, forward, rates_y, last, n_row, rows, unit, count, block, len(after)
            ),
            [((state_rows, LANES), F32), ((corners + moving + turned, LANES), F32), ((moving, LANES), F32)],
            (*after, *more, edges, states, received, keep),
            8 * MIB,
            0.4,
            apart=() if forward else range(len(after)),
        )
        received = swap(message, "col", n_col, 0)
        (part,) = call(
            functools.partial(inner_kernel, levels, count, block),
            [((state_rows, LANES), F32)],
            (edges, states, message),
            8 * MIB,
            0.4,
        )
        return part, received, keep

    row_reach = row_reach_of(rates_y, rows, True)
    args = (control, obs_count, obs_corner, offset_y, offset_x, offset_z, innovation, precision)
    moving = n_row * FIELDS
    message, *blocks_out = call(
        functools.partial(first_kernel, rates_y),
        [((state_rows, LANES), F32)] + [((moving, LANES), F32)] * 2,
        args,
        OBS * MIB,
        2.0,
        apart=range(len(args)),
        scratch=[pltpu.VMEM(a.shape, a.dtype) for a in args]
        + [pltpu.SemaphoreType.DMA((len(args) + levels - 1,))],
    )
    edges, row_matrix, blocks_out[1] = tables(True, message, blocks_out[1])
    partial = []
    turned = []

    def beside(step, message):
        now = [row_matrix] if step == 0 else []
        while step and len(partial) < levels and (len(partial) < levels - 1 or step == last):
            one, two = local(True, len(partial), control, members, edges, row_matrix)
            partial.append(one)
            turned.append(two)
            now.append(two)
        return now

    states, received, (send,), keep = scan_rows(
        True, rates_y, rows, n_col * FIELDS, message, blocks_out, beside
    )
    last_bit = block_bits(True, last + 1)[last]
    pairs = []
    for m in range(n_mem):
        for r in range(n_row):
            pairs.append((m * n_row + r, (1 - m) * n_row + (r ^ (1 << last_bit))))
    row_other = swap(send, "row", n_row, last_bit)
    mem_keep = swap(keep, "mem", n_mem, 0)
    mem_other = lax.ppermute(send, ("mem", "row"), pairs)
    part, received, keep = close(
        True, n_col * FIELDS, edges, states, received, keep, turned, (row_other, mem_keep, mem_other)
    )
    sources = 4 * moving // FIELDS
    states, table, columns = call(
        functools.partial(collect_kernel, rates_x, per_level, count),
        [((state_rows, LANES), F32), ((4 * moving, LANES), F32), ((flat, LANES), F32)],
        (part, received, keep),
        4 * MIB,
        0.1,
    )
    wide = 2
    group = 8
    unpacked = [
        pltpu.VMEM((GROUP + 5, sources, LANES), F32),
        pltpu.VMEM((2, sources, LANES), jnp.int32),
    ]
    (images,) = call(
        functools.partial(observe_kernel, scale, wide, 2 * group, rates_x),
        [((sources, LANES), F32)],
        (states, columns, members, row_reach, table, *partial),
        16 * MIB,
        2.8,
        scratch=[
            pltpu.VMEM((levels * rows, cols), F32),
            pltpu.VMEM((2 * levels * rows * (GROUP + 1), cols // GROUP), BF16),
            *unpacked,
        ],
    )
    others = swap(images, "mem", n_mem, 0)

    row_reach = row_reach_of(rates_y, rows, False)
    edges, row_matrix = tables(False)
    forcing, message, keep = call(
        functools.partial(force_kernel, scale, wide, group, rates_y),
        [
            ((levels, rows, cols), F32),
            ((state_rows + n_row, LANES), F32),
            ((n_row, LANES), F32),
        ],
        (images, others, table, members),
        24 * MIB,
        4.0,
        scratch=[
            pltpu.VMEM((cols // GROUP, group * wide * LANES), BF16),
            pltpu.VMEM((2 * levels * rows * (GROUP + 1), group * wide * LANES), BF16),
            pltpu.VMEM((2 * levels * rows * (GROUP + 1), cols // GROUP), F32),
            pltpu.VMEM((sources, LANES), F32),
            *unpacked,
        ],
    )
    bases = []
    sent = []

    def back_beside(step, message):
        if step == 0:
            sent.extend(
                call(
                    functools.partial(columns_kernel, block),
                    [((flat, LANES), F32)],
                    (members, forcing, edges, message),
                    16 * MIB,
                    1.0,
                    apart=(3,),
                )
            )
            sent.append(swap(sent[0], "col", n_col, 0))
            return sent[1:]
        now = []
        if step == 1 or step == last:
            for level in range(len(bases), levels if step == last else levels - 1):
                now += local(False, level, control, members, forcing, *sent, edges, row_matrix, message)
        bases.extend(now)
        return now

    states, received, _, keep = scan_rows(False, rates_y, rows, n_col, message, (keep,), back_beside)
    part, received, keep = close(False, n_col, edges, states, received, keep, bases)
    return pl.pallas_call(
        functools.partial(finish_kernel, rates_x, per_level),
        out_shape=[
            jax.ShapeDtypeStruct(control.shape, F32),
            jax.ShapeDtypeStruct(precision.shape, F32),
        ],
        in_specs=[pl.BlockSpec(memory_space=pltpu.VMEM)] * (4 + levels),
        out_specs=[pl.BlockSpec(memory_space=pl.ANY), pl.BlockSpec(memory_space=pltpu.VMEM)],
        scratch_shapes=[
            pltpu.VMEM((state_rows, LANES), F32),
            pltpu.VMEM(control.shape, F32),
            pltpu.SemaphoreType.DMA((count,)),
        ],
        compiler_params=pltpu.CompilerParams(vmem_limit_bytes=8 * MIB),
        cost_estimate=cost(2.0),
    )(row_reach, part, received, keep, *bases)


def solution(mesh):
    spread = P(("mem", "row", "col"), None)
    grid = P("mem", None, "row", "col")
    return jax.shard_map(
        body,
        mesh=mesh,
        in_specs=(grid, grid) + (spread,) * 7,
        out_specs=(grid, spread),
        check_vma=False,
    )
```

```python
import functools

import jax
import jax.numpy as jnp
import numpy as np
from jax import lax
from jax.experimental import pallas as pl
from jax.experimental.pallas import tpu as pltpu
from jax.sharding import PartitionSpec as P

LANES = 128
HALF = LANES // 2
FIELDS = 6
TURNED = 8
GROUP = 4
PIECE = 256
F32 = jnp.float32
BF16 = jnp.bfloat16
MIB = 1 << 20
OBS = 57


def filter_rates(lengths):
    decay = np.exp(-1.0 / np.asarray(lengths, np.float64))
    weight = ((1.0 - decay**2) ** 3 / (1.0 + decay**2)) ** 0.25
    return decay, weight


def row_reach_of(rates, size, forward):
    places = np.arange(size)
    steps = places + 1 if forward else size - places
    reach = np.zeros((len(rates[0]), 2, size, LANES), np.float32)
    for level, (a, b) in enumerate(zip(*rates)):
        reach[level, 0] = (b * steps * a**steps)[:, None]
        reach[level, 1] = (a**steps)[:, None]
    return reach


def by_level(level, values):
    chosen = jnp.full(level.shape, float(values[0]), F32)
    for i in range(1, len(values)):
        chosen = jnp.where(level == i, float(values[i]), chosen)
    return chosen


def two_pass(a, b, lag):
    steps = jnp.maximum(lag, 0).astype(F32)
    return jnp.where(lag >= 0, float(b**2) * (steps + 1.0) * jnp.exp(steps * float(np.log(a))), 0.0)


def table_kernel(forward, rates_x, rates_y, members, block, *refs):
    edges, row_matrix, *passed = refs[len(refs) // 2 if len(refs) > 2 else 0 :]
    for out, ref in zip(passed, refs[1:]):
        out[...] = ref[...]
    levels = len(rates_x[0])
    size = edges.shape[1]
    blocks = size // block
    per_level = 2 * (blocks + 1)
    logs = [float(np.log(a)) for a in rates_x[0]]

    def lanes_of(lane):
        level = lax.div(lane, per_level)
        inner = lax.rem(lane, per_level)
        k = lax.div(inner, 2)
        return level, k, (inner & 1) == 1, (lane < levels * per_level)

    def place_of_column(column):
        return column if forward else size - 1 - column

    shape = (HALF, size)
    level, k, second, used = lanes_of(lax.broadcasted_iota(jnp.int32, shape, 0))
    place = place_of_column(lax.broadcasted_iota(jnp.int32, shape, 1))
    steps = place + 1 - jnp.where(k == blocks, 0, (k + 1) * block)
    used = used & (steps > 0)
    steps = jnp.maximum(steps, 0).astype(F32)
    power = jnp.exp(steps * by_level(level, logs))
    value = jnp.where(second, power, by_level(level, rates_x[1]) * steps * power)
    high, low = split(jnp.where(used, value, 0.0))
    edges[0:HALF, :] = high
    edges[HALF : 2 * HALF, :] = high
    edges[2 * HALF : 3 * HALF, :] = low
    edges[3 * HALF : 4 * HALF, :] = jnp.zeros(shape, BF16)

    first = 4 * HALF
    row = lax.broadcasted_iota(jnp.int32, (block, block), 0)
    column = lax.broadcasted_iota(jnp.int32, (block, block), 1)
    lag = column - row if forward else row - column
    for i, (a, b) in enumerate(zip(*rates_x)):
        for h, value in enumerate(split(two_pass(a, b, lag))):
            at = (h * levels + i) * block
            edges[first : first + block, at : at + block] = value
    at = 2 * levels * block
    if at < size:
        edges[first : first + block, at:] = jnp.zeros((block, size - at), BF16)

    first += block
    shape = (LANES, LANES)
    lane = lax.broadcasted_iota(jnp.int32, shape, 1)
    level, k, second, used = lanes_of(lane & (HALF - 1))
    stop = jnp.where(k == blocks, size, (k + 1) * block)
    begin = jnp.where(k == blocks, 0, k * block)
    log, weight = by_level(level, logs), by_level(level, rates_x[1])
    for t in range(size // LANES):
        place = place_of_column(t * LANES + lax.broadcasted_iota(jnp.int32, shape, 0))
        left = stop - 1 - place
        inside = used & (place >= begin) & (left >= 0)
        left = jnp.maximum(left, 0).astype(F32)
        value = weight * jnp.exp(left * log)
        value = jnp.where(inside, jnp.where(second, weight * (left + 1.0) * value, value), 0.0)
        high = value.astype(BF16)
        near = slice(t * LANES, (t + 1) * LANES)
        edges[first : first + LANES, near] = jnp.where(lane < HALF, high.astype(F32), value - high.astype(F32)).astype(BF16)

    flat = row_matrix.shape[2]
    height = flat // members
    row = lax.broadcasted_iota(jnp.int32, (flat, flat), 0)
    column = lax.broadcasted_iota(jnp.int32, (flat, flat), 1)
    same = lax.div(row, height) == lax.div(column, height)
    lag = row - column if forward else column - row
    for i, (a, b) in enumerate(zip(*rates_y)):
        high, low = split(jnp.where(same, two_pass(a, b, lag), 0.0))
        row_matrix[0, i] = high
        row_matrix[1, i] = low


class EdgeTable:
    def __init__(self, ref, levels, block):
        self.ref, self.levels, self.block = ref, levels, block
        self.size = ref.shape[1]
        self.first = 4 * HALF

    def reach(self, near=slice(None)):
        return self.ref[0 : self.first, near]

    def matrix(self, level):
        return jnp.concatenate([self.square(level), self.square(self.levels + level), self.square(level)], axis=0)

    def square(self, index):
        return self.ref[self.first : self.first + self.block, index * self.block : (index + 1) * self.block]

    def edge(self):
        at = self.first + self.block
        rows = [self.ref[at : at + LANES, t : t + LANES] for t in range(0, self.size, LANES)]
        return jnp.concatenate(rows, axis=0)


def split(value):
    high = value.astype(BF16)
    return high, (value - high.astype(F32)).astype(BF16)


def dot(left, right):
    return jnp.dot(left, right, preferred_element_type=F32)


def lane_kinds(shape, blocks, level):
    lane = lax.broadcasted_iota(jnp.int32, shape, 1)
    per_level = 2 * (blocks + 1)
    mine = (lane >= level * per_level) & (lane < (level + 1) * per_level)
    return mine, lax.rem(lane, per_level) >= 2 * blocks


def edge_states(value, table, blocks, level):
    high, low = split(value)
    weights = table.edge()
    both = dot(high, weights) + dot(low, weights)
    mine, _ = lane_kinds(both.shape, blocks, level)
    return jnp.where(mine, both + pltpu.roll(both, HALF, 1), 0.0)


def packed(states):
    lane = lax.broadcasted_iota(jnp.int32, states.shape, 1)
    high = states.astype(BF16).astype(F32)
    low = states - high
    first = jnp.where(lane < HALF, high, pltpu.roll(low, HALF, 1))
    second = jnp.where(lane < HALF, high, 0.0)
    return jnp.concatenate([first.astype(BF16), second.astype(BF16)], axis=1)


def dot_left(left, value):
    high, low = split(value)
    return dot(left, jnp.concatenate([high, high, low], axis=0))


def dot_right(value, right, *more):
    high, low = split(value)
    left = jnp.concatenate([high, high, low] + [x for x, _ in more], axis=1)
    return dot(left, jnp.concatenate([right] + [x for _, x in more], axis=0))


def cost(micros):
    return pl.CostEstimate(flops=0, bytes_accessed=int(micros * 3.6e6), transcendentals=0)


def call(kernel, outs, args, limit, micros, apart=(), scratch=()):
    return pl.pallas_call(
        kernel,
        out_shape=[jax.ShapeDtypeStruct(shape, dtype) for shape, dtype in outs],
        in_specs=[
            pl.BlockSpec(memory_space=pl.ANY if i in apart else pltpu.VMEM) for i in range(len(args))
        ],
        out_specs=[pl.BlockSpec(memory_space=pltpu.VMEM) for _ in outs],
        scratch_shapes=list(scratch),
        compiler_params=pltpu.CompilerParams(vmem_limit_bytes=limit),
        cost_estimate=cost(micros),
    )(*args)


def level_rows(ref, level):
    value = ref[:, level]
    return value.reshape(value.shape[0] * value.shape[1], value.shape[2])


def work_rows(members_ref, forcing_ref, level):
    value = members_ref[:, level].astype(F32) * forcing_ref[level][None]
    return value.reshape(value.shape[0] * value.shape[1], value.shape[2])


def row_weights_at_edge(forward, rates, level, members, size):
    a, b = rates[0][level], rates[1][level]
    shape = (members, members * size)
    member = lax.broadcasted_iota(jnp.int32, shape, 0)
    place = lax.broadcasted_iota(jnp.int32, shape, 1)
    row = lax.rem(place, size)
    left = (size - 1 - row if forward else row).astype(F32)
    power = jnp.where(lax.div(place, size) == member, float(b) * jnp.exp(left * float(np.log(a))), 0.0)
    high, low = split(jnp.concatenate([power, float(b) * (left + 1.0) * power], axis=0))
    return jnp.concatenate([high, low], axis=0)


def put_row_edges(forward, rates, members, values, message):
    for level, value in values:
        weights = row_weights_at_edge(forward, rates, level, members, value.shape[0] // members)
        pairs = weights.shape[0] // 2
        high, low = split(value)
        both = dot(weights, high)
        lay_states(message, level, both[0:pairs] + both[pairs:] + dot(weights[0:pairs], low))


def lay_states(message, level, states):
    half = states.shape[0] // 2
    chunks = states.shape[1] // LANES
    for s in range(2):
        for t in range(chunks):
            at = ((2 * level + s) * chunks + t) * half
            message[at : at + half, :] = states[s * half : (s + 1) * half, t * LANES : (t + 1) * LANES]


def take_states(states, level, half, chunks):
    rows = []
    for s in range(2):
        at = (2 * level + s) * chunks * half
        rows.append(
            jnp.concatenate([states[at + t * half : at + (t + 1) * half, :] for t in range(chunks)], axis=1)
        )
    return jnp.concatenate(rows, axis=0)


def first_kernel(rates, *refs):
    sources, (message, send, keep), places, sems = refs[:8], refs[8:11], refs[11:19], refs[19]
    control, counts, *fields = places
    levels = control.shape[1]
    pairs = list(zip(sources[1:], places[1:]))
    pairs += [(sources[0].at[:, level], control.at[:, level]) for level in range(levels)]
    copies = [pltpu.make_async_copy(*pair, sems.at[i]) for i, pair in enumerate(pairs)]
    for copy in copies:
        copy.start()
    for copy in copies[:-levels]:
        copy.wait()
    rows = counts.shape[1] // 2
    steps = rows.bit_length() - 1
    order = sorted(range(rows), key=lambda row: block_place(True, steps, row))
    bit = (lax.axis_index("row") >> block_bits(True, steps)[0]) & 1
    slot = lax.broadcasted_iota(jnp.int32, (1, LANES), 1)

    def read(tile, f):
        value = fields[f][:, tile * LANES : (tile + 1) * LANES].astype(F32)
        if f == FIELDS - 1:
            value = jnp.where(slot < counts[:, tile : tile + 1], value, 0.0)
        return value

    at = 0
    for h in range(0, rows, 2):
        for tile_col in range(2):
            for f in range(FIELDS):
                zero, one = read(2 * order[h] + tile_col, f), read(2 * order[h + 1] + tile_col, f)
                send[at : at + 1, :], keep[at : at + 1, :] = join(bit, one, zero)
                at += 1

    def values():
        for level in range(levels):
            copies[level - levels].wait()
            yield level, level_rows(control, level)

    put_row_edges(True, rates, control.shape[0], values(), message)


def columns_kernel(block, members, forcing, edges, _, out):
    levels = members.shape[1]
    table = EdgeTable(edges, levels, block)
    total = None
    for level in range(levels):
        states = edge_states(work_rows(members, forcing, level), table, table.size // block, level)
        total = states if total is None else total + states
    out[...] = total


def entering_rows(forward, rates, level, size):
    a, b = rates[0][level], rates[1][level]
    place = lax.broadcasted_iota(jnp.int32, (1, size), 1)
    steps = (place + 1 if forward else size - place).astype(F32)
    power = jnp.exp(steps * float(np.log(a)))
    return float(b) * steps * power, power


def corner_kernel(forward, rates, step, count, tile, unit, half, block, after, *refs):
    *refs, edges, before, received, keep_in, states, message, keep = refs
    more, refs = refs[:after], refs[after:]
    last_states(forward, rates, step, count, tile, before, received, states)
    levels = len(rates[0])
    table = EdgeTable(edges, levels, block)
    chunks = table.size // LANES
    rows = [take_states(states, level, half, chunks) for level in range(levels)]
    high, low = split(jnp.concatenate(rows, axis=0))
    at = high.shape[0]
    both = dot(jnp.concatenate([high, low], axis=0), table.edge())
    both = both[0:at] + both[at:]
    both = both + pltpu.roll(both, HALF, 1)
    for level in range(levels):
        near = slice(2 * half * level, 2 * half * (level + 1))
        mine, _ = lane_kinds((2 * half, LANES), table.size // block, level)
        message[near, :] = jnp.where(mine, both[near], 0.0)
    bit = (lax.axis_index("row") >> block_bits(forward, step + 1)[step]) & 1
    place = lax.axis_index("col")
    base, size = before.shape[0], keep_in.shape[0]
    each = unit // 2
    if refs:
        pairs = [(keep_in[...], refs[0][...]), (refs[1][...], refs[2][...])]
    else:
        pairs = [(keep_in[...], received[base : base + size, :])]
    start, at = at, 0
    for mine, other in pairs:
        for value in join(bit, mine, other):
            for i in range(0, size, unit):
                send, stay = join(place, value[i + each : i + unit], value[i : i + each])
                message[start + at : start + at + each, :] = send
                keep[at : at + each, :] = stay
                at += each
    if forward:
        turned = more[0][...]
        for ref in more[1:]:
            turned = turned + ref[...]
        for t in range(turned.shape[1] // LANES):
            first = start + at + t * turned.shape[0]
            message[first : first + turned.shape[0], :] = turned[:, t * LANES : (t + 1) * LANES]


def inner_kernel(levels, half, block, edges, states, message, part):
    table = EdgeTable(edges, levels, block)
    size = table.size
    blocks = size // block
    for level in range(levels):
        value = take_states(states, level, half, size // LANES)
        pairs = value.shape[0]
        corner = message[level * pairs : (level + 1) * pairs, :]
        _, whole = lane_kinds(corner.shape, blocks, level)
        carry = dot(packed(jnp.where(whole, 0.0, corner)), table.reach())
        stack = jnp.concatenate([value[:, at : at + block] for at in range(0, size, block)], axis=0)
        stack = dot_right(stack, table.matrix(level))
        rows = [stack[n * pairs : (n + 1) * pairs] for n in range(blocks)]
        lay_states(part, level, jnp.concatenate(rows, axis=1) + carry)


def outer_states(forward, rates, per_level, half, part, received, states):
    place = lax.axis_index("col")
    live = jnp.where(place == (1 if forward else 0), 1.0, 0.0)
    levels = len(rates[0])
    chunks = part.shape[0] // (2 * levels * half)
    for level in range(levels):
        lane = (level + 1) * per_level - 2
        ones, twos = entering_rows(forward, rates, level, chunks * LANES)
        for s in range(2):
            at = (2 * level + s) * half
            corner = received[at : at + half, :] * live
            one, two = corner[:, lane : lane + 1], corner[:, lane + 1 : lane + 2]
            for t in range(chunks):
                at = ((2 * level + s) * chunks + t) * half
                near = slice(t * LANES, (t + 1) * LANES)
                states[at : at + half, :] = part[at : at + half, :] + one * ones[:, near] + two * twos[:, near]


def join_columns(each, keep, received, base):
    place = lax.axis_index("col")
    for i in range(0, keep.shape[0], each):
        yield from join(place, keep[i : i + each, :], received[base + i : base + i + each, :])


def collect_kernel(rates, per_level, half, part, received, keep, states, table, columns):
    outer_states(True, rates, per_level, half, part, received, states)
    at = 0
    for value in join_columns(FIELDS, keep, received, 2 * len(rates[0]) * half):
        table[at : at + FIELDS, :] = value
        at += FIELDS
    live = jnp.where(lax.axis_index("col") == 1, 1.0, 0.0)
    start = 2 * len(rates[0]) * half + keep.shape[0]
    for t in range(columns.shape[0] // LANES):
        turned = received[start + t * TURNED : start + (t + 1) * TURNED, :] * live
        turned = jnp.concatenate([turned, jnp.zeros((LANES - TURNED, LANES), F32)], axis=0)
        columns[t * LANES : (t + 1) * LANES, :] = jnp.transpose(turned)


def block_bits(forward, steps):
    bits = list(range(steps))
    if forward:
        bits[0], bits[-1] = bits[-1], bits[0]
    return bits


def block_place(forward, steps, row):
    return sum(((row >> bit) & 1) << i for i, bit in enumerate(block_bits(forward, steps)))


def transfer(rates, level, steps):
    a, b = rates[0][level], rates[1][level]
    return float(a**steps), float(b * steps * a**steps)


def pick(index, values):
    chosen = jnp.float32(values[0])
    for i in range(1, len(values)):
        chosen = jnp.where(index == i, jnp.float32(values[i]), chosen)
    return chosen


def reach_of(forward, rates, step, count, tile, level):
    row = lax.axis_index("row")
    line = row if forward else count - 1 - row
    upper = ((line >> step) & 1) == 1
    inside = line & ((1 << step) - 1)
    table = [transfer(rates, level, q * tile) for q in range(1 << step)]
    near1 = jnp.where(upper, pick(inside, [x[0] for x in table]), 0.0)
    near2 = jnp.where(upper, pick(inside, [x[1] for x in table]), 0.0)
    return near1, near2, upper


def join(bit, mine, other):
    return jnp.where(bit == 1, other, mine), jnp.where(bit == 1, mine, other)


def new_states(forward, rates, step, count, tile, level, before, received, first, second):
    near1, near2, upper = reach_of(forward, rates, step, count, tile, level)
    got1, got2 = received[first, :], received[second, :]
    new1 = near1 * got1
    new2 = near1 * got2 + near2 * got1
    if before is not None:
        new1 = before[first, :] + new1
        new2 = before[second, :] + new2
    return new1, new2, got1, got2, upper


def round_kernel(forward, rates, step, count, tile, unit, spans, apart, after, *refs):
    sent, received, keep_in, *refs = refs
    before = refs.pop(0) if step else None
    blocks = refs.pop(0) if apart else received
    message, keep, states, *send = refs[after:]
    levels = len(rates[0])
    base = states.shape[0]
    start = 0 if apart else base
    part = base // (2 * levels)
    for level in range(levels):
        at = 2 * level * part
        first, second = slice(at, at + part), slice(at + part, at + 2 * part)
        new1, new2, got1, got2, upper = new_states(
            forward, rates, step, count, tile, level, before, received, first, second
        )
        states[first, :] = new1
        states[second, :] = new2
        far1, far2 = transfer(rates, level, tile << step)
        own1 = jnp.where(upper, 1.0, far1)
        own2 = jnp.where(upper, 0.0, far2)
        his1 = jnp.where(upper, far1, 1.0)
        his2 = jnp.where(upper, far2, 0.0)
        all1, all2 = sent[first, :], sent[second, :]
        message[first, :] = own1 * all1 + his1 * got1
        message[second, :] = own1 * all2 + own2 * all1 + his1 * got2 + his2 * got1
    row = lax.axis_index("row")
    bits = block_bits(forward, count.bit_length() - 1)
    bit = (row >> bits[step]) & 1
    next_bit = (row >> bits[step + 1]) & 1
    size = unit << step
    place, first = (send[0], 0) if send else (message, base)

    def span(h):
        near = slice(h * size, (h + 1) * size)
        other = blocks[start + h * size : start + (h + 1) * size, :]
        return jnp.concatenate(join(bit, keep_in[near, :], other), axis=0)

    at = 0
    for h in range(0, spans // 2, 2):
        moved, stay = join(next_bit, span(h + 1), span(h))
        place[first + at : first + at + 2 * size, :] = moved
        keep[at : at + 2 * size, :] = stay
        at += 2 * size


def last_states(forward, rates, step, count, tile, before, received, states):
    levels = len(rates[0])
    part = before.shape[0] // (2 * levels)
    for level in range(levels):
        at = 2 * level * part
        first, second = slice(at, at + part), slice(at + part, at + 2 * part)
        states[first, :], states[second, :], *_ = new_states(
            forward, rates, step, count, tile, level, before, received, first, second
        )


def swap(value, axis, size, step):
    return lax.ppermute(value, axis, [(i, i ^ (1 << step)) for i in range(size)])


def scan_rows(forward, rates, tile, unit, message, blocks, beside):
    count = lax.axis_size("row")
    steps = count.bit_length() - 1
    spans = count
    apart = len(blocks) == 2
    keep = blocks[-1]
    moving = keep.shape[0]
    state_rows = message.shape[0] - (0 if apart else moving)
    states = None
    for step in range(steps - 1):
        received = swap(message, "row", count, step)
        args = (message, received, keep) + (() if step == 0 else (states,))
        if apart:
            args += (swap(blocks[0], "row", count, block_bits(forward, steps)[step]),)
        after = beside(step, message)
        first = len(args)
        args = args + tuple(after)
        kernel = functools.partial(
            round_kernel, forward, rates, step, count, tile, unit, spans, apart, len(after)
        )
        outs = [state_rows + moving, moving, state_rows]
        if forward and step == steps - 2:
            outs = [state_rows, moving, state_rows, moving]
        outs = [((rows, LANES), F32) for rows in outs]
        message, keep, states, *send = call(kernel, outs, args, 4 * MIB, 0.1, apart=range(first, len(args)))
        spans //= 2
        apart = False
    received = swap(message, "row", count, steps - 1)
    beside(steps - 1, message)
    return states, received, send, keep


def local_kernel(forward, level, block, *refs):
    if forward:
        control, members, edges, row_matrix, out, whole_out, between, scratch = refs
    else:
        control, members, forcing, columns, received, edges, row_matrix, _, out, between, scratch = refs
    count, levels, rows, cols = control.shape
    table = EdgeTable(edges, levels, block)
    high = row_matrix[0, level]
    left = jnp.concatenate([high, row_matrix[1, level], high], axis=1)
    mine, whole = lane_kinds((count * rows, LANES), cols // block, level)
    if forward:
        value = level_rows(control, level)
        states = edge_states(value, table, cols // block, level)
        entering = jnp.where(whole, 0.0, states)
        turned = jnp.transpose(dot_left(left, jnp.where(whole, states, 0.0)))
        first = (level + 1) * 2 * (cols // block + 1) - 2
        whole_out[...] = jnp.zeros_like(whole_out)
        whole_out[2 * level : 2 * level + 2, :] = turned[first : first + 2, :]
    else:
        value = work_rows(members, forcing, level)
        live = jnp.where(lax.axis_index("col") == 0, 1.0, 0.0)
        entering = jnp.where(whole, received[...] * live, columns[...])
        entering = jnp.where(mine, entering, 0.0)
    entering = packed(entering)
    weights = table.matrix(level)
    spans = [slice(at, at + block) for at in range(0, cols, block)]
    for near in spans:
        between[:, near] = dot_right(value[:, near], weights, (entering, table.reach(near)))
    for near in spans:
        scratch[:, near] = dot_left(left, between[:, near])
    if forward:
        total = None
        for m in range(count):
            term = members[m, level].astype(F32) * scratch[m * rows : (m + 1) * rows, :]
            total = term if total is None else total + term
        out[...] = total
    else:
        for m in range(count):
            out[m] = control[m, level] + scratch[m * rows : (m + 1) * rows, :]


def bulk_fields(table, cols, weights, places):
    sources = table.shape[0] // FIELDS
    fields = [table[pl.ds(f, sources, stride=FIELDS), :] for f in range(FIELDS)]
    corner = fields[0].astype(jnp.int32)
    row_at = lax.div(corner, cols)
    col_at = corner - row_at * cols
    values = col_weights(col_at, fields[2]) + [fields[1]] + fields[3:]
    for i, value in enumerate(values):
        weights[i] = value
    places[0] = row_at
    places[1] = lax.div(col_at, GROUP)


def source_row(ref, i, chunk, wide):
    rows = [ref[i, pl.ds(chunk * wide + j, 1), :] for j in range(wide)]
    return jnp.concatenate(rows, axis=1)


def row_weights(row_at, frac, rows):
    places = lax.broadcasted_iota(jnp.int32, (rows, row_at.shape[1]), 0)
    near = jnp.where(places == row_at, 1.0 - frac, 0.0)
    return near + jnp.where(places == row_at + 1, frac, 0.0)


def one_hot(col_at, cols):
    places = lax.broadcasted_iota(jnp.int32, (cols, col_at.shape[1]), 0)
    return jnp.where(places == col_at, 1.0, 0.0).astype(BF16)


def spread_matrix(size, back):
    one = lax.broadcasted_iota(jnp.int32, (size, size), 1 if back else 0)
    two = lax.broadcasted_iota(jnp.int32, (size, size), 0 if back else 1)
    at = (one & (GROUP - 1)) * (size // GROUP) + lax.div(one, GROUP)
    return jnp.where(at == two, 1.0, 0.0).astype(BF16)


def col_weights(col_at, frac):
    within = col_at & (GROUP - 1)
    weights = []
    for j in range(GROUP + 1):
        weight = jnp.where(within == j, 1.0 - frac, 0.0)
        weights.append(weight + jnp.where(within == j - 1, frac, 0.0))
    return weights


def observe_kernel(scale, wide, group, rates, states, columns, members, reach, table, *refs):
    count, levels, rows, cols = members.shape
    partial, (images, field, stack, weights, places) = refs[:levels], refs[levels:]
    bulk_fields(table, cols, weights, places)
    chunks = cols // LANES
    for level in range(levels):
        reach1, reach2 = reach[level, 0], reach[level, 1]
        ones, twos = entering_rows(True, rates, level, cols)
        spans = [slice(t * LANES, (t + 1) * LANES) for t in range(chunks)]
        totals = [partial[level][:, near] for near in spans]
        for m in range(count):
            across = columns[m * rows : (m + 1) * rows, :]
            one = jnp.broadcast_to(across[:, 2 * level : 2 * level + 1], (rows, LANES))
            two = jnp.broadcast_to(across[:, 2 * level + 1 : 2 * level + 2], (rows, LANES))
            for t, near in enumerate(spans):
                at = (2 * level * chunks + t) * count + m
                later = at + chunks * count
                entered = reach1 * states[at : at + 1, :] + reach2 * states[later : later + 1, :]
                entered = entered + one * ones[:, near] + two * twos[:, near]
                totals[t] = totals[t] + members[m, level, :, near].astype(F32) * entered
        for t, near in enumerate(spans):
            field[level * rows : (level + 1) * rows, near] = totals[t] * scale
    flat = levels * rows
    high, low = split(field[...])
    both = jnp.concatenate([high, low], axis=0)
    spread = spread_matrix(PIECE, False)
    each = PIECE // GROUP
    pieces = [dot(both[:, at : at + PIECE], spread) for at in range(0, cols, PIECE)]
    wide_k = cols // GROUP
    for j in range(GROUP):
        value = jnp.concatenate([p[:, j * each : (j + 1) * each] for p in pieces], axis=1)
        stack[2 * flat * j : 2 * flat * (j + 1), :] = value.astype(BF16)
        if j == 0:
            moved = pltpu.roll(value, wide_k - 1, 1)
            stack[2 * flat * GROUP : 2 * flat * (GROUP + 1), :] = moved.astype(BF16)
    sources = table.shape[0] // FIELDS // wide

    def work(chunk):
        row_at, group_at = (source_row(places, i, chunk, wide) for i in range(2))
        *near, frac_y, frac_z = (source_row(weights, i, chunk, wide) for i in range(GROUP + 3))
        seen = dot(stack[...], one_hot(group_at, cols // GROUP))
        mixed = None
        for j, weight in enumerate(near):
            at = 2 * flat * j
            term = (seen[at : at + flat] + seen[at + flat : at + 2 * flat]) * weight
            mixed = term if mixed is None else mixed + term
        weight = row_weights(row_at, frac_y, rows)
        low_level = jnp.sum(mixed[0:rows] * weight, axis=0, keepdims=True)
        high_level = jnp.sum(mixed[rows : 2 * rows] * weight, axis=0, keepdims=True)
        image = (1.0 - frac_z) * low_level + frac_z * high_level
        for i in range(wide):
            images[pl.ds(chunk * wide + i, 1), :] = image[:, i * LANES : (i + 1) * LANES]

    if sources == group:
        for chunk in range(sources):
            work(chunk)
    else:

        @pl.loop(0, sources // group)
        def _(turn):
            for i in range(group):
                work(turn * group + i)


def force_kernel(
    scale, wide, group, rates, images, others, table, members, *refs
):
    forcing, message, keep, hot, load, total, misfits, weights, places = refs
    bulk_fields(table, members.shape[3], weights, places)
    count, levels, rows, cols = members.shape
    flat = levels * rows
    sources = table.shape[0] // FIELDS
    half = sources // 2
    span = wide * LANES
    total[...] = jnp.zeros_like(total)

    @pl.loop(0, sources // wide // group)
    def _(turn):
        for i in range(group):
            chunk = turn * group + i
            row_at, group_at = (source_row(places, i, chunk, wide) for i in range(2))
            *near_weights, frac_y, frac_z, innovation, precision = (
                source_row(weights, i, chunk, wide) for i in range(GROUP + 5)
            )
            parts = []
            for j in range(wide):
                source = chunk * wide + j
                swapped = jnp.where(source < half, source + half, source - half)
                parts.append(images[pl.ds(source, 1), :] + others[pl.ds(swapped, 1), :])
            misfit = precision * (jnp.concatenate(parts, axis=1) - innovation)
            for j in range(wide):
                misfits[pl.ds(chunk * wide + j, 1), :] = misfit[:, j * LANES : (j + 1) * LANES]
            weight = row_weights(row_at, frac_y, rows) * misfit
            stack = jnp.concatenate([weight * (1.0 - frac_z), weight * frac_z], axis=0)
            near = slice(i * span, (i + 1) * span)
            for j, weight in enumerate(near_weights):
                at = 2 * flat * j
                load[at : at + flat, near], load[at + flat : at + 2 * flat, near] = split(stack * weight)
            hot[:, near] = one_hot(group_at, cols // GROUP)
        total[...] += lax.dot_general(
            load[...], hot[...], (((1,), (1,)), ((), ())), preferred_element_type=F32
        )

    groups = []
    for j in range(GROUP + 1):
        at = 2 * flat * j
        groups.append(total[at : at + flat, :] + total[at + flat : at + 2 * flat, :])
    groups[0] = groups[0] + pltpu.roll(groups[GROUP], 1, 1)
    spread = spread_matrix(PIECE, True)
    each = PIECE // GROUP
    for t in range(cols // PIECE):
        value = jnp.concatenate([g[:, t * each : (t + 1) * each] for g in groups[:GROUP]], axis=1)
        high, low = split(value * scale)
        force = dot(high, spread) + dot(low, spread)
        for level in range(levels):
            forcing[level, :, t * PIECE : (t + 1) * PIECE] = force[level * rows : (level + 1) * rows]
    values = ((level, work_rows(members, forcing, level)) for level in range(levels))
    put_row_edges(False, rates, count, values, message)
    bit = lax.axis_index("row") & 1
    base = message.shape[0] - keep.shape[0]
    steps = (half // 2).bit_length() - 1

    def of_row(row):
        at = 2 * block_place(True, steps, row)
        return misfits[at : at + 2, :]

    for h in range(half // 4):
        zero, one = of_row(2 * h), of_row(2 * h + 1)
        message[base + 2 * h : base + 2 * h + 2, :], keep[2 * h : 2 * h + 2, :] = join(bit, one, zero)


def finish_kernel(rates, per_level, reach, part, received, keep, *refs):
    levels = reach.shape[0]
    bases, (out, returned, states, buffer, sems) = refs[:levels], refs[levels:]
    half = buffer.shape[0]
    outer_states(False, rates, per_level, half, part, received, states)
    members, _, _, cols = buffer.shape
    chunks = cols // LANES
    copies = []
    for m in range(members):
        for level in range(levels):
            for t in range(chunks):
                near = slice(t * LANES, (t + 1) * LANES)
                at = (2 * level * chunks + t) * members + m
                later = at + chunks * members
                entered = reach[level, 0] * states[at : at + 1, :] + reach[level, 1] * states[later : later + 1, :]
                buffer[m, level, :, near] = bases[level][m, :, near] + entered
        copies.append(pltpu.make_async_copy(buffer.at[m], out.at[m], sems.at[m]))
        copies[-1].start()
    at = 0
    for value in join_columns(1, keep, received, 2 * levels * half):
        returned[:, at : at + LANES] = value
        at += LANES
    for copy in copies:
        copy.wait()


def body(
    control, members, obs_corner, obs_count, offset_y, offset_x, offset_z, innovation, precision
):
    count, levels, rows, cols = control.shape
    n_mem, n_row, n_col = (lax.axis_size(name) for name in ("mem", "row", "col"))
    if n_mem != 2 or n_col != 2 or n_row & (n_row - 1):
        raise ValueError("unsupported mesh")
    grid_rows = rows * n_row
    block = min(256, cols)
    rates_x = filter_rates([cols / 16.0, cols / 64.0])
    rates_y = filter_rates([grid_rows / 2.0, rows / 2.0])
    scale = float(count * n_mem) ** -0.5
    flat = count * rows
    state_rows = levels * 2 * count * cols // LANES
    blocks = cols // block
    last = n_row.bit_length() - 2
    if levels * 2 * (blocks + 1) > HALF or last < 1:
        raise ValueError("unsupported sizes")

    per_level = 2 * (blocks + 1)
    corners = levels * 2 * count

    def tables(forward, *after):
        return call(
            functools.partial(table_kernel, forward, rates_x, rates_y, count, block),
            [((4 * HALF + block + LANES, cols), BF16), ((2, levels, flat, flat), BF16)]
            + [(a.shape, a.dtype) for a in after[1:]],
            after,
            8 * MIB,
            1.0,
        )

    def local(forward, level, *args):
        outs = [((rows, cols), F32), ((TURNED, flat), F32)] if forward else [((count, rows, cols), F32)]
        return call(
            functools.partial(local_kernel, forward, level, block),
            outs,
            args,
            16 * MIB,
            2.5,
            apart=() if forward else (len(args) - 1,),
            scratch=[pltpu.VMEM((flat, cols), F32)] * 2,
        )

    def close(forward, unit, edges, states, received, keep, after, more=()):
        moving = keep.shape[0] * 2 // unit * (unit // 2) * (1 + len(more) // 2)
        turned = TURNED * flat // LANES if forward else 0
        states, message, keep = call(
            functools.partial(
                corner_kernel, forward, rates_y, last, n_row, rows, unit, count, block, len(after)
            ),
            [((state_rows, LANES), F32), ((corners + moving + turned, LANES), F32), ((moving, LANES), F32)],
            (*after, *more, edges, states, received, keep),
            8 * MIB,
            0.4,
            apart=() if forward else range(len(after)),
        )
        received = swap(message, "col", n_col, 0)
        (part,) = call(
            functools.partial(inner_kernel, levels, count, block),
            [((state_rows, LANES), F32)],
            (edges, states, message),
            8 * MIB,
            0.4,
        )
        return part, received, keep

    row_reach = row_reach_of(rates_y, rows, True)
    args = (control, obs_count, obs_corner, offset_y, offset_x, offset_z, innovation, precision)
    moving = n_row * FIELDS
    message, *blocks_out = call(
        functools.partial(first_kernel, rates_y),
        [((state_rows, LANES), F32)] + [((moving, LANES), F32)] * 2,
        args,
        OBS * MIB,
        2.0,
        apart=range(len(args)),
        scratch=[pltpu.VMEM(a.shape, a.dtype) for a in args]
        + [pltpu.SemaphoreType.DMA((len(args) + levels - 1,))],
    )
    edges, row_matrix, blocks_out[1] = tables(True, message, blocks_out[1])
    partial = []
    turned = []

    def beside(step, message):
        now = [row_matrix] if step == 0 else []
        while step and len(partial) < levels and (len(partial) < levels - 1 or step == last):
            one, two = local(True, len(partial), control, members, edges, row_matrix)
            partial.append(one)
            turned.append(two)
            now.append(two)
        return now

    states, received, (send,), keep = scan_rows(
        True, rates_y, rows, n_col * FIELDS, message, blocks_out, beside
    )
    last_bit = block_bits(True, last + 1)[last]
    pairs = []
    for m in range(n_mem):
        for r in range(n_row):
            pairs.append((m * n_row + r, (1 - m) * n_row + (r ^ (1 << last_bit))))
    row_other = swap(send, "row", n_row, last_bit)
    mem_keep = swap(keep, "mem", n_mem, 0)
    mem_other = lax.ppermute(send, ("mem", "row"), pairs)
    part, received, keep = close(
        True, n_col * FIELDS, edges, states, received, keep, turned, (row_other, mem_keep, mem_other)
    )
    sources = 4 * moving // FIELDS
    states, table, columns = call(
        functools.partial(collect_kernel, rates_x, per_level, count),
        [((state_rows, LANES), F32), ((4 * moving, LANES), F32), ((flat, LANES), F32)],
        (part, received, keep),
        4 * MIB,
        0.1,
    )
    wide = 2
    group = 8
    unpacked = [
        pltpu.VMEM((GROUP + 5, sources, LANES), F32),
        pltpu.VMEM((2, sources, LANES), jnp.int32),
    ]
    (images,) = call(
        functools.partial(observe_kernel, scale, wide, 2 * group, rates_x),
        [((sources, LANES), F32)],
        (states, columns, members, row_reach, table, *partial),
        16 * MIB,
        2.8,
        scratch=[
            pltpu.VMEM((levels * rows, cols), F32),
            pltpu.VMEM((2 * levels * rows * (GROUP + 1), cols // GROUP), BF16),
            *unpacked,
        ],
    )
    others = swap(images, "mem", n_mem, 0)

    row_reach = row_reach_of(rates_y, rows, False)
    edges, row_matrix = tables(False)
    forcing, message, keep = call(
        functools.partial(force_kernel, scale, wide, group, rates_y),
        [
            ((levels, rows, cols), F32),
            ((state_rows + n_row, LANES), F32),
            ((n_row, LANES), F32),
        ],
        (images, others, table, members),
        24 * MIB,
        4.0,
        scratch=[
            pltpu.VMEM((cols // GROUP, group * wide * LANES), BF16),
            pltpu.VMEM((2 * levels * rows * (GROUP + 1), group * wide * LANES), BF16),
            pltpu.VMEM((2 * levels * rows * (GROUP + 1), cols // GROUP), F32),
            pltpu.VMEM((sources, LANES), F32),
            *unpacked,
        ],
    )
    bases = []
    sent = []

    def back_beside(step, message):
        if step == 0:
            sent.extend(
                call(
                    functools.partial(columns_kernel, block),
                    [((flat, LANES), F32)],
                    (members, forcing, edges, message),
                    16 * MIB,
                    1.0,
                    apart=(3,),
                )
            )
            sent.append(swap(sent[0], "col", n_col, 0))
            return sent[1:]
        now = []
        if step == 1 or step == last:
            for level in range(len(bases), levels if step == last else levels - 1):
                now += local(False, level, control, members, forcing, *sent, edges, row_matrix, message)
        bases.extend(now)
        return now

    states, received, _, keep = scan_rows(False, rates_y, rows, n_col, message, (keep,), back_beside)
    part, received, keep = close(False, n_col, edges, states, received, keep, bases)
    return pl.pallas_call(
        functools.partial(finish_kernel, rates_x, per_level),
        out_shape=[
            jax.ShapeDtypeStruct(control.shape, F32),
            jax.ShapeDtypeStruct(precision.shape, F32),
        ],
        in_specs=[pl.BlockSpec(memory_space=pltpu.VMEM)] * (4 + levels),
        out_specs=[pl.BlockSpec(memory_space=pl.ANY), pl.BlockSpec(memory_space=pltpu.VMEM)],
        scratch_shapes=[
            pltpu.VMEM((state_rows, LANES), F32),
            pltpu.VMEM(control.shape, F32),
            pltpu.SemaphoreType.DMA((count,)),
        ],
        compiler_params=pltpu.CompilerParams(vmem_limit_bytes=8 * MIB),
        cost_estimate=cost(2.0),
    )(row_reach, part, received, keep, *bases)


def solution(mesh):
    spread = P(("mem", "row", "col"), None)
    grid = P("mem", None, "row", "col")
    return jax.shard_map(
        body,
        mesh=mesh,
        in_specs=(grid, grid) + (spread,) * 7,
        out_specs=(grid, spread),
        check_vma=False,
    )
```

```python
import functools

import jax
import jax.numpy as jnp
import numpy as np
from jax import lax
from jax.experimental import pallas as pl
from jax.experimental.pallas import tpu as pltpu
from jax.sharding import PartitionSpec as P

LANES = 128
HALF = LANES // 2
FIELDS = 6
TURNED = 8
GROUP = 4
PIECE = 256
F32 = jnp.float32
BF16 = jnp.bfloat16
MIB = 1 << 20
OBS = 57


def filter_rates(lengths):
    decay = np.exp(-1.0 / np.asarray(lengths, np.float64))
    weight = ((1.0 - decay**2) ** 3 / (1.0 + decay**2)) ** 0.25
    return decay, weight


def row_reach_of(rates, size, forward):
    places = np.arange(size)
    steps = places + 1 if forward else size - places
    reach = np.zeros((len(rates[0]), 2, size, LANES), np.float32)
    for level, (a, b) in enumerate(zip(*rates)):
        reach[level, 0] = (b * steps * a**steps)[:, None]
        reach[level, 1] = (a**steps)[:, None]
    return reach


def by_level(level, values):
    chosen = jnp.full(level.shape, float(values[0]), F32)
    for i in range(1, len(values)):
        chosen = jnp.where(level == i, float(values[i]), chosen)
    return chosen


def two_pass(a, b, lag):
    steps = jnp.maximum(lag, 0).astype(F32)
    return jnp.where(lag >= 0, float(b**2) * (steps + 1.0) * jnp.exp(steps * float(np.log(a))), 0.0)


def table_kernel(forward, rates_x, rates_y, members, block, *refs):
    edges, row_matrix, *passed = refs[len(refs) // 2 if len(refs) > 2 else 0 :]
    for out, ref in zip(passed, refs[1:]):
        out[...] = ref[...]
    levels = len(rates_x[0])
    size = edges.shape[1]
    blocks = size // block
    per_level = 2 * (blocks + 1)
    logs = [float(np.log(a)) for a in rates_x[0]]

    def lanes_of(lane):
        level = lax.div(lane, per_level)
        inner = lax.rem(lane, per_level)
        k = lax.div(inner, 2)
        return level, k, (inner & 1) == 1, (lane < levels * per_level)

    def place_of_column(column):
        return column if forward else size - 1 - column

    filled = min(HALF, -(-levels * per_level // 16) * 16)
    shape = (filled, size)
    level, k, second, used = lanes_of(lax.broadcasted_iota(jnp.int32, shape, 0))
    place = place_of_column(lax.broadcasted_iota(jnp.int32, shape, 1))
    steps = place + 1 - jnp.where(k == blocks, 0, (k + 1) * block)
    used = used & (steps > 0)
    steps = jnp.maximum(steps, 0).astype(F32)
    power = jnp.exp(steps * by_level(level, logs))
    value = jnp.where(second, power, by_level(level, rates_x[1]) * steps * power)
    high, low = split(jnp.where(used, value, 0.0))
    for i, part in enumerate((high, high, low, jnp.zeros(shape, BF16))):
        edges[i * HALF : i * HALF + filled, :] = part
        if filled < HALF:
            edges[i * HALF + filled : (i + 1) * HALF, :] = jnp.zeros((HALF - filled, size), BF16)

    first = 4 * HALF
    row = lax.broadcasted_iota(jnp.int32, (block, block), 0)
    column = lax.broadcasted_iota(jnp.int32, (block, block), 1)
    lag = column - row if forward else row - column
    for i, (a, b) in enumerate(zip(*rates_x)):
        for h, value in enumerate(split(two_pass(a, b, lag))):
            at = (h * levels + i) * block
            edges[first : first + block, at : at + block] = value
    at = 2 * levels * block
    if at < size:
        edges[first : first + block, at:] = jnp.zeros((block, size - at), BF16)

    first += block
    shape = (LANES, LANES)
    lane = lax.broadcasted_iota(jnp.int32, shape, 1)
    level, k, second, used = lanes_of(lane & (HALF - 1))
    stop = jnp.where(k == blocks, size, (k + 1) * block)
    begin = jnp.where(k == blocks, 0, k * block)
    log, weight = by_level(level, logs), by_level(level, rates_x[1])
    for t in range(size // LANES):
        place = place_of_column(t * LANES + lax.broadcasted_iota(jnp.int32, shape, 0))
        left = stop - 1 - place
        inside = used & (place >= begin) & (left >= 0)
        left = jnp.maximum(left, 0).astype(F32)
        value = weight * jnp.exp(left * log)
        value = jnp.where(inside, jnp.where(second, weight * (left + 1.0) * value, value), 0.0)
        high = value.astype(BF16)
        near = slice(t * LANES, (t + 1) * LANES)
        edges[first : first + LANES, near] = jnp.where(lane < HALF, high.astype(F32), value - high.astype(F32)).astype(BF16)

    flat = row_matrix.shape[2]
    height = flat // members
    row = lax.broadcasted_iota(jnp.int32, (height, flat), 0)
    column = lax.broadcasted_iota(jnp.int32, (height, flat), 1)
    member = lax.div(column, height)
    lag = row - lax.rem(column, height)
    lag = lag if forward else -lag
    for i, (a, b) in enumerate(zip(*rates_y)):
        value = two_pass(a, b, lag)
        for m in range(members):
            near = slice(m * height, (m + 1) * height)
            row_matrix[0, i, near, :], row_matrix[1, i, near, :] = split(jnp.where(member == m, value, 0.0))


class EdgeTable:
    def __init__(self, ref, levels, block):
        self.ref, self.levels, self.block = ref, levels, block
        self.size = ref.shape[1]
        self.first = 4 * HALF

    def reach(self, near=slice(None)):
        return self.ref[0 : self.first, near]

    def matrix(self, level):
        return jnp.concatenate([self.square(level), self.square(self.levels + level), self.square(level)], axis=0)

    def square(self, index):
        return self.ref[self.first : self.first + self.block, index * self.block : (index + 1) * self.block]

    def edge(self):
        at = self.first + self.block
        rows = [self.ref[at : at + LANES, t : t + LANES] for t in range(0, self.size, LANES)]
        return jnp.concatenate(rows, axis=0)


def split(value):
    high = value.astype(BF16)
    return high, (value - high.astype(F32)).astype(BF16)


def dot(left, right):
    return jnp.dot(left, right, preferred_element_type=F32)


def lane_kinds(shape, blocks, level):
    lane = lax.broadcasted_iota(jnp.int32, shape, 1)
    per_level = 2 * (blocks + 1)
    mine = (lane >= level * per_level) & (lane < (level + 1) * per_level)
    return mine, lax.rem(lane, per_level) >= 2 * blocks


def edge_states(value, table, blocks, level):
    high, low = split(value)
    weights = table.edge()
    both = dot(high, weights) + dot(low, weights)
    mine, _ = lane_kinds(both.shape, blocks, level)
    return jnp.where(mine, both + pltpu.roll(both, HALF, 1), 0.0)


def packed(states):
    lane = lax.broadcasted_iota(jnp.int32, states.shape, 1)
    high = states.astype(BF16).astype(F32)
    low = states - high
    first = jnp.where(lane < HALF, high, pltpu.roll(low, HALF, 1))
    second = jnp.where(lane < HALF, high, 0.0)
    return jnp.concatenate([first.astype(BF16), second.astype(BF16)], axis=1)


def dot_left(left, value):
    high, low = split(value)
    return dot(left, jnp.concatenate([high, high, low], axis=0))


def dot_right(value, right, *more):
    high, low = split(value)
    left = jnp.concatenate([high, high, low] + [x for x, _ in more], axis=1)
    return dot(left, jnp.concatenate([right] + [x for _, x in more], axis=0))


def cost(micros):
    return pl.CostEstimate(flops=0, bytes_accessed=int(micros * 3.6e6), transcendentals=0)


def call(kernel, outs, args, limit, micros, apart=(), scratch=()):
    return pl.pallas_call(
        kernel,
        out_shape=[jax.ShapeDtypeStruct(shape, dtype) for shape, dtype in outs],
        in_specs=[
            pl.BlockSpec(memory_space=pl.ANY if i in apart else pltpu.VMEM) for i in range(len(args))
        ],
        out_specs=[pl.BlockSpec(memory_space=pltpu.VMEM) for _ in outs],
        scratch_shapes=list(scratch),
        compiler_params=pltpu.CompilerParams(vmem_limit_bytes=limit),
        cost_estimate=cost(micros),
    )(*args)


def level_rows(ref, level):
    value = ref[:, level]
    return value.reshape(value.shape[0] * value.shape[1], value.shape[2])


def work_rows(members_ref, forcing_ref, level):
    value = members_ref[:, level].astype(F32) * forcing_ref[level][None]
    return value.reshape(value.shape[0] * value.shape[1], value.shape[2])


def row_weights_at_edge(forward, rates, level, members, size):
    a, b = rates[0][level], rates[1][level]
    shape = (members, members * size)
    member = lax.broadcasted_iota(jnp.int32, shape, 0)
    place = lax.broadcasted_iota(jnp.int32, shape, 1)
    row = lax.rem(place, size)
    left = (size - 1 - row if forward else row).astype(F32)
    power = jnp.where(lax.div(place, size) == member, float(b) * jnp.exp(left * float(np.log(a))), 0.0)
    high, low = split(jnp.concatenate([power, float(b) * (left + 1.0) * power], axis=0))
    return jnp.concatenate([high, low], axis=0)


def put_row_edges(forward, rates, members, values, message):
    for level, value in values:
        weights = row_weights_at_edge(forward, rates, level, members, value.shape[0] // members)
        pairs = weights.shape[0] // 2
        high, low = split(value)
        both = dot(weights, high)
        lay_states(message, level, both[0:pairs] + both[pairs:] + dot(weights[0:pairs], low))


def lay_states(message, level, states):
    half = states.shape[0] // 2
    chunks = states.shape[1] // LANES
    for s in range(2):
        for t in range(chunks):
            at = ((2 * level + s) * chunks + t) * half
            message[at : at + half, :] = states[s * half : (s + 1) * half, t * LANES : (t + 1) * LANES]


def take_states(states, level, half, chunks):
    rows = []
    for s in range(2):
        at = (2 * level + s) * chunks * half
        rows.append(
            jnp.concatenate([states[at + t * half : at + (t + 1) * half, :] for t in range(chunks)], axis=1)
        )
    return jnp.concatenate(rows, axis=0)


def first_kernel(rates, *refs):
    sources, (message, send), places, sems = refs[:8], refs[8:10], refs[10:18], refs[18]
    base = message.shape[0] - send.shape[0]
    control, counts, *fields = places
    levels = control.shape[1]
    pairs = list(zip(sources[1:], places[1:]))
    pairs += [(sources[0].at[:, level], control.at[:, level]) for level in range(levels)]
    copies = [pltpu.make_async_copy(*pair, sems.at[i]) for i, pair in enumerate(pairs)]
    for copy in copies:
        copy.start()
    for copy in copies[:-levels]:
        copy.wait()
    rows = counts.shape[1] // 2
    steps = rows.bit_length() - 1
    order = sorted(range(rows), key=lambda row: block_place(True, steps, row))
    bit = (lax.axis_index("row") >> block_bits(True, steps)[0]) & 1
    slot = lax.broadcasted_iota(jnp.int32, (1, LANES), 1)

    def read(tile, f):
        value = fields[f][:, tile * LANES : (tile + 1) * LANES].astype(F32)
        if f == FIELDS - 1:
            value = jnp.where(slot < counts[:, tile : tile + 1], value, 0.0)
        return value

    at = 0
    for h in range(0, rows, 2):
        for tile_col in range(2):
            for f in range(FIELDS):
                zero, one = read(2 * order[h] + tile_col, f), read(2 * order[h + 1] + tile_col, f)
                send[at : at + 1, :], message[base + at : base + at + 1, :] = join(bit, one, zero)
                at += 1

    def values():
        for level in range(levels):
            copies[level - levels].wait()
            yield level, level_rows(control, level)

    put_row_edges(True, rates, control.shape[0], values(), message)


def columns_kernel(block, members, forcing, edges, _, out):
    levels = members.shape[1]
    table = EdgeTable(edges, levels, block)
    total = None
    for level in range(levels):
        states = edge_states(work_rows(members, forcing, level), table, table.size // block, level)
        total = states if total is None else total + states
    out[...] = total


def entering_rows(forward, rates, level, size):
    a, b = rates[0][level], rates[1][level]
    place = lax.broadcasted_iota(jnp.int32, (1, size), 1)
    steps = (place + 1 if forward else size - place).astype(F32)
    power = jnp.exp(steps * float(np.log(a)))
    return float(b) * steps * power, power


def corner_kernel(forward, rates, step, count, tile, unit, half, block, after, *refs):
    *refs, edges, before, received, keep_in, states, message, keep = refs
    more, refs = refs[:after], refs[after:]
    last_states(forward, rates, step, count, tile, before, received, states)
    levels = len(rates[0])
    table = EdgeTable(edges, levels, block)
    chunks = table.size // LANES
    rows = [take_states(states, level, half, chunks) for level in range(levels)]
    high, low = split(jnp.concatenate(rows, axis=0))
    at = high.shape[0]
    both = dot(jnp.concatenate([high, low], axis=0), table.edge())
    both = both[0:at] + both[at:]
    both = both + pltpu.roll(both, HALF, 1)
    for level in range(levels):
        near = slice(2 * half * level, 2 * half * (level + 1))
        mine, _ = lane_kinds((2 * half, LANES), table.size // block, level)
        message[near, :] = jnp.where(mine, both[near], 0.0)
    bit = (lax.axis_index("row") >> block_bits(forward, step + 1)[step]) & 1
    place = lax.axis_index("col")
    base, size = before.shape[0], keep_in.shape[0]
    each = unit // 2
    if refs:
        pairs = [(keep_in[...], refs[0][...]), (refs[1][...], refs[2][...])]
    else:
        pairs = [(keep_in[...], received[base : base + size, :])]
    start, at = at, 0
    for mine, other in pairs:
        for value in join(bit, mine, other):
            for i in range(0, size, unit):
                send, stay = join(place, value[i + each : i + unit], value[i : i + each])
                message[start + at : start + at + each, :] = send
                keep[at : at + each, :] = stay
                at += each
    if forward:
        turned = more[0][...]
        for ref in more[1:]:
            turned = turned + ref[...]
        for t in range(turned.shape[1] // LANES):
            first = start + at + t * turned.shape[0]
            message[first : first + turned.shape[0], :] = turned[:, t * LANES : (t + 1) * LANES]


def inner_kernel(levels, half, block, edges, states, message, part):
    table = EdgeTable(edges, levels, block)
    size = table.size
    blocks = size // block
    for level in range(levels):
        value = take_states(states, level, half, size // LANES)
        pairs = value.shape[0]
        corner = message[level * pairs : (level + 1) * pairs, :]
        _, whole = lane_kinds(corner.shape, blocks, level)
        carry = dot(packed(jnp.where(whole, 0.0, corner)), table.reach())
        stack = jnp.concatenate([value[:, at : at + block] for at in range(0, size, block)], axis=0)
        stack = dot_right(stack, table.matrix(level))
        rows = [stack[n * pairs : (n + 1) * pairs] for n in range(blocks)]
        lay_states(part, level, jnp.concatenate(rows, axis=1) + carry)


def outer_states(forward, rates, per_level, half, part, received, states):
    place = lax.axis_index("col")
    live = jnp.where(place == (1 if forward else 0), 1.0, 0.0)
    levels = len(rates[0])
    chunks = part.shape[0] // (2 * levels * half)
    for level in range(levels):
        lane = (level + 1) * per_level - 2
        ones, twos = entering_rows(forward, rates, level, chunks * LANES)
        for s in range(2):
            at = (2 * level + s) * half
            corner = received[at : at + half, :] * live
            one, two = corner[:, lane : lane + 1], corner[:, lane + 1 : lane + 2]
            for t in range(chunks):
                at = ((2 * level + s) * chunks + t) * half
                near = slice(t * LANES, (t + 1) * LANES)
                states[at : at + half, :] = part[at : at + half, :] + one * ones[:, near] + two * twos[:, near]


def join_columns(each, keep, received, base):
    place = lax.axis_index("col")
    for i in range(0, keep.shape[0], each):
        yield from join(place, keep[i : i + each, :], received[base + i : base + i + each, :])


def collect_kernel(rates, per_level, half, part, received, keep, states, table, columns):
    outer_states(True, rates, per_level, half, part, received, states)
    at = 0
    for value in join_columns(FIELDS, keep, received, 2 * len(rates[0]) * half):
        table[at : at + FIELDS, :] = value
        at += FIELDS
    live = jnp.where(lax.axis_index("col") == 1, 1.0, 0.0)
    start = 2 * len(rates[0]) * half + keep.shape[0]
    for t in range(columns.shape[0] // LANES):
        turned = received[start + t * TURNED : start + (t + 1) * TURNED, :] * live
        turned = jnp.concatenate([turned, jnp.zeros((LANES - TURNED, LANES), F32)], axis=0)
        columns[t * LANES : (t + 1) * LANES, :] = jnp.transpose(turned)


def block_bits(forward, steps):
    bits = list(range(steps))
    if forward:
        bits[0], bits[-1] = bits[-1], bits[0]
    return bits


def block_place(forward, steps, row):
    return sum(((row >> bit) & 1) << i for i, bit in enumerate(block_bits(forward, steps)))


def transfer(rates, level, steps):
    a, b = rates[0][level], rates[1][level]
    return float(a**steps), float(b * steps * a**steps)


def pick(index, values):
    chosen = jnp.float32(values[0])
    for i in range(1, len(values)):
        chosen = jnp.where(index == i, jnp.float32(values[i]), chosen)
    return chosen


def reach_of(forward, rates, step, count, tile, level):
    row = lax.axis_index("row")
    line = row if forward else count - 1 - row
    upper = ((line >> step) & 1) == 1
    inside = line & ((1 << step) - 1)
    table = [transfer(rates, level, q * tile) for q in range(1 << step)]
    near1 = jnp.where(upper, pick(inside, [x[0] for x in table]), 0.0)
    near2 = jnp.where(upper, pick(inside, [x[1] for x in table]), 0.0)
    return near1, near2, upper


def join(bit, mine, other):
    return jnp.where(bit == 1, other, mine), jnp.where(bit == 1, mine, other)


def new_states(forward, rates, step, count, tile, level, before, received, first, second):
    near1, near2, upper = reach_of(forward, rates, step, count, tile, level)
    got1, got2 = received[first, :], received[second, :]
    new1 = near1 * got1
    new2 = near1 * got2 + near2 * got1
    if before is not None:
        new1 = before[first, :] + new1
        new2 = before[second, :] + new2
    return new1, new2, got1, got2, upper


def round_kernel(forward, rates, step, count, tile, unit, spans, apart, after, *refs):
    sent, received, *refs = refs
    keep_in = sent if apart else refs.pop(0)
    before = refs.pop(0) if step else None
    blocks = refs.pop(0) if apart else received
    message, keep, states, *send = refs[after:]
    levels = len(rates[0])
    base = states.shape[0]
    start, own = (0, base) if apart else (base, 0)
    part = base // (2 * levels)
    for level in range(levels):
        at = 2 * level * part
        first, second = slice(at, at + part), slice(at + part, at + 2 * part)
        new1, new2, got1, got2, upper = new_states(
            forward, rates, step, count, tile, level, before, received, first, second
        )
        states[first, :] = new1
        states[second, :] = new2
        far1, far2 = transfer(rates, level, tile << step)
        own1 = jnp.where(upper, 1.0, far1)
        own2 = jnp.where(upper, 0.0, far2)
        his1 = jnp.where(upper, far1, 1.0)
        his2 = jnp.where(upper, far2, 0.0)
        all1, all2 = sent[first, :], sent[second, :]
        message[first, :] = own1 * all1 + his1 * got1
        message[second, :] = own1 * all2 + own2 * all1 + his1 * got2 + his2 * got1
    row = lax.axis_index("row")
    bits = block_bits(forward, count.bit_length() - 1)
    bit = (row >> bits[step]) & 1
    next_bit = (row >> bits[step + 1]) & 1
    size = unit << step
    place, first = (send[0], 0) if send else (message, base)

    def span(h):
        near = slice(own + h * size, own + (h + 1) * size)
        other = blocks[start + h * size : start + (h + 1) * size, :]
        return jnp.concatenate(join(bit, keep_in[near, :], other), axis=0)

    at = 0
    for h in range(0, spans // 2, 2):
        moved, stay = join(next_bit, span(h + 1), span(h))
        place[first + at : first + at + 2 * size, :] = moved
        keep[at : at + 2 * size, :] = stay
        at += 2 * size


def last_states(forward, rates, step, count, tile, before, received, states):
    levels = len(rates[0])
    part = before.shape[0] // (2 * levels)
    for level in range(levels):
        at = 2 * level * part
        first, second = slice(at, at + part), slice(at + part, at + 2 * part)
        states[first, :], states[second, :], *_ = new_states(
            forward, rates, step, count, tile, level, before, received, first, second
        )


def swap(value, axis, size, step):
    return lax.ppermute(value, axis, [(i, i ^ (1 << step)) for i in range(size)])


def scan_rows(forward, rates, tile, unit, message, blocks, beside):
    count = lax.axis_size("row")
    steps = count.bit_length() - 1
    spans = count
    apart = forward
    keep = blocks[0]
    moving = keep.shape[0]
    state_rows = message.shape[0] - moving
    states = None
    for step in range(steps - 1):
        received = swap(message, "row", count, step)
        args = (message, received) + (() if apart else (keep,)) + (() if step == 0 else (states,))
        if apart:
            args += (swap(blocks[0], "row", count, block_bits(forward, steps)[step]),)
        after = beside(step, message)
        first = len(args)
        args = args + tuple(after)
        kernel = functools.partial(
            round_kernel, forward, rates, step, count, tile, unit, spans, apart, len(after)
        )
        outs = [state_rows + moving, moving, state_rows]
        if forward and step == steps - 2:
            outs = [state_rows, moving, state_rows, moving]
        outs = [((rows, LANES), F32) for rows in outs]
        message, keep, states, *send = call(kernel, outs, args, 4 * MIB, 0.1, apart=range(first, len(args)))
        spans //= 2
        apart = False
    received = swap(message, "row", count, steps - 1)
    beside(steps - 1, message)
    return states, received, send, keep


def local_kernel(forward, level, block, *refs):
    if forward:
        control, members, edges, row_matrix, out, whole_out, between, scratch = refs
    else:
        control, members, forcing, columns, received, edges, row_matrix, _, out, between, scratch = refs
    count, levels, rows, cols = control.shape
    table = EdgeTable(edges, levels, block)
    high = row_matrix[0, level]
    left = jnp.concatenate([high, row_matrix[1, level], high], axis=1)
    mine, whole = lane_kinds((count * rows, LANES), cols // block, level)
    if forward:
        value = level_rows(control, level)
        states = edge_states(value, table, cols // block, level)
        entering = jnp.where(whole, 0.0, states)
        turned = jnp.transpose(dot_left(left, jnp.where(whole, states, 0.0)))
        first = (level + 1) * 2 * (cols // block + 1) - 2
        whole_out[...] = jnp.zeros_like(whole_out)
        whole_out[2 * level : 2 * level + 2, :] = turned[first : first + 2, :]
    else:
        value = work_rows(members, forcing, level)
        live = jnp.where(lax.axis_index("col") == 0, 1.0, 0.0)
        entering = jnp.where(whole, received[...] * live, columns[...])
        entering = jnp.where(mine, entering, 0.0)
    entering = packed(entering)
    weights = table.matrix(level)
    spans = [slice(at, at + block) for at in range(0, cols, block)]
    for near in spans:
        between[:, near] = dot_right(value[:, near], weights, (entering, table.reach(near)))
    for near in spans:
        scratch[:, near] = dot_left(left, between[:, near])
    if forward:
        total = None
        for m in range(count):
            term = members[m, level].astype(F32) * scratch[m * rows : (m + 1) * rows, :]
            total = term if total is None else total + term
        out[...] = total
    else:
        for m in range(count):
            out[m] = control[m, level] + scratch[m * rows : (m + 1) * rows, :]


def bulk_fields(table, cols, weights, places):
    sources = table.shape[0] // FIELDS
    fields = [table[pl.ds(f, sources, stride=FIELDS), :] for f in range(FIELDS)]
    corner = fields[0].astype(jnp.int32)
    row_at = lax.div(corner, cols)
    col_at = corner - row_at * cols
    values = col_weights(col_at, fields[2]) + [fields[1]] + fields[3:]
    for i, value in enumerate(values):
        weights[i] = value
    places[0] = row_at
    places[1] = lax.div(col_at, GROUP)


def source_row(ref, i, chunk, wide):
    rows = [ref[i, pl.ds(chunk * wide + j, 1), :] for j in range(wide)]
    return jnp.concatenate(rows, axis=1)


def row_weights(row_at, frac, rows):
    places = lax.broadcasted_iota(jnp.int32, (rows, row_at.shape[1]), 0)
    near = jnp.where(places == row_at, 1.0 - frac, 0.0)
    return near + jnp.where(places == row_at + 1, frac, 0.0)


def one_hot(col_at, cols):
    places = lax.broadcasted_iota(jnp.int32, (cols, col_at.shape[1]), 0)
    return jnp.where(places == col_at, 1.0, 0.0).astype(BF16)


def spread_matrix(size, back):
    one = lax.broadcasted_iota(jnp.int32, (size, size), 1 if back else 0)
    two = lax.broadcasted_iota(jnp.int32, (size, size), 0 if back else 1)
    at = (one & (GROUP - 1)) * (size // GROUP) + lax.div(one, GROUP)
    return jnp.where(at == two, 1.0, 0.0).astype(BF16)


def col_weights(col_at, frac):
    within = col_at & (GROUP - 1)
    weights = []
    for j in range(GROUP + 1):
        weight = jnp.where(within == j, 1.0 - frac, 0.0)
        weights.append(weight + jnp.where(within == j - 1, frac, 0.0))
    return weights


def observe_kernel(scale, wide, group, rates, states, columns, members, reach, table, *refs):
    count, levels, rows, cols = members.shape
    partial, (images, field, stack, weights, places) = refs[:levels], refs[levels:]
    bulk_fields(table, cols, weights, places)
    chunks = cols // LANES
    for level in range(levels):
        reach1, reach2 = reach[level, 0], reach[level, 1]
        ones, twos = entering_rows(True, rates, level, cols)
        spans = [slice(t * LANES, (t + 1) * LANES) for t in range(chunks)]
        totals = [partial[level][:, near] for near in spans]
        for m in range(count):
            across = columns[m * rows : (m + 1) * rows, :]
            one = jnp.broadcast_to(across[:, 2 * level : 2 * level + 1], (rows, LANES))
            two = jnp.broadcast_to(across[:, 2 * level + 1 : 2 * level + 2], (rows, LANES))
            for t, near in enumerate(spans):
                at = (2 * level * chunks + t) * count + m
                later = at + chunks * count
                entered = reach1 * states[at : at + 1, :] + reach2 * states[later : later + 1, :]
                entered = entered + one * ones[:, near] + two * twos[:, near]
                totals[t] = totals[t] + members[m, level, :, near].astype(F32) * entered
        for t, near in enumerate(spans):
            field[level * rows : (level + 1) * rows, near] = totals[t] * scale
    flat = levels * rows
    high, low = split(field[...])
    both = jnp.concatenate([high, low], axis=0)
    spread = spread_matrix(PIECE, False)
    each = PIECE // GROUP
    pieces = [dot(both[:, at : at + PIECE], spread) for at in range(0, cols, PIECE)]
    wide_k = cols // GROUP
    for j in range(GROUP):
        value = jnp.concatenate([p[:, j * each : (j + 1) * each] for p in pieces], axis=1)
        stack[2 * flat * j : 2 * flat * (j + 1), :] = value.astype(BF16)
        if j == 0:
            moved = pltpu.roll(value, wide_k - 1, 1)
            stack[2 * flat * GROUP : 2 * flat * (GROUP + 1), :] = moved.astype(BF16)
    sources = table.shape[0] // FIELDS // wide

    def work(chunk):
        row_at, group_at = (source_row(places, i, chunk, wide) for i in range(2))
        *near, frac_y, frac_z = (source_row(weights, i, chunk, wide) for i in range(GROUP + 3))
        seen = dot(stack[...], one_hot(group_at, cols // GROUP))
        mixed = None
        for j, weight in enumerate(near):
            at = 2 * flat * j
            term = (seen[at : at + flat] + seen[at + flat : at + 2 * flat]) * weight
            mixed = term if mixed is None else mixed + term
        weight = row_weights(row_at, frac_y, rows)
        low_level = jnp.sum(mixed[0:rows] * weight, axis=0, keepdims=True)
        high_level = jnp.sum(mixed[rows : 2 * rows] * weight, axis=0, keepdims=True)
        image = (1.0 - frac_z) * low_level + frac_z * high_level
        for i in range(wide):
            images[pl.ds(chunk * wide + i, 1), :] = image[:, i * LANES : (i + 1) * LANES]

    if sources == group:
        for chunk in range(sources):
            work(chunk)
    else:

        @pl.loop(0, sources // group)
        def _(turn):
            for i in range(group):
                work(turn * group + i)


def force_kernel(
    scale, wide, group, rates, images, others, table, members, *refs
):
    forcing, message, keep, hot, load, total, misfits, weights, places = refs
    bulk_fields(table, members.shape[3], weights, places)
    count, levels, rows, cols = members.shape
    flat = levels * rows
    sources = table.shape[0] // FIELDS
    half = sources // 2
    span = wide * LANES
    total[...] = jnp.zeros_like(total)

    @pl.loop(0, sources // wide // group)
    def _(turn):
        for i in range(group):
            chunk = turn * group + i
            row_at, group_at = (source_row(places, i, chunk, wide) for i in range(2))
            *near_weights, frac_y, frac_z, innovation, precision = (
                source_row(weights, i, chunk, wide) for i in range(GROUP + 5)
            )
            parts = []
            for j in range(wide):
                source = chunk * wide + j
                swapped = jnp.where(source < half, source + half, source - half)
                parts.append(images[pl.ds(source, 1), :] + others[pl.ds(swapped, 1), :])
            misfit = precision * (jnp.concatenate(parts, axis=1) - innovation)
            for j in range(wide):
                misfits[pl.ds(chunk * wide + j, 1), :] = misfit[:, j * LANES : (j + 1) * LANES]
            weight = row_weights(row_at, frac_y, rows) * misfit
            stack = jnp.concatenate([weight * (1.0 - frac_z), weight * frac_z], axis=0)
            near = slice(i * span, (i + 1) * span)
            for j, weight in enumerate(near_weights):
                at = 2 * flat * j
                load[at : at + flat, near], load[at + flat : at + 2 * flat, near] = split(stack * weight)
            hot[:, near] = one_hot(group_at, cols // GROUP)
        total[...] += lax.dot_general(
            load[...], hot[...], (((1,), (1,)), ((), ())), preferred_element_type=F32
        )

    groups = []
    for j in range(GROUP + 1):
        at = 2 * flat * j
        groups.append(total[at : at + flat, :] + total[at + flat : at + 2 * flat, :])
    groups[0] = groups[0] + pltpu.roll(groups[GROUP], 1, 1)
    spread = spread_matrix(PIECE, True)
    each = PIECE // GROUP
    for t in range(cols // PIECE):
        value = jnp.concatenate([g[:, t * each : (t + 1) * each] for g in groups[:GROUP]], axis=1)
        high, low = split(value * scale)
        force = dot(high, spread) + dot(low, spread)
        for level in range(levels):
            forcing[level, :, t * PIECE : (t + 1) * PIECE] = force[level * rows : (level + 1) * rows]
    values = ((level, work_rows(members, forcing, level)) for level in range(levels))
    put_row_edges(False, rates, count, values, message)
    bit = lax.axis_index("row") & 1
    base = message.shape[0] - keep.shape[0]
    steps = (half // 2).bit_length() - 1

    def of_row(row):
        at = 2 * block_place(True, steps, row)
        return misfits[at : at + 2, :]

    for h in range(half // 4):
        zero, one = of_row(2 * h), of_row(2 * h + 1)
        message[base + 2 * h : base + 2 * h + 2, :], keep[2 * h : 2 * h + 2, :] = join(bit, one, zero)


def finish_kernel(rates, per_level, reach, part, received, keep, *refs):
    levels = reach.shape[0]
    bases, (out, returned, states, buffer, sems) = refs[:levels], refs[levels:]
    half = buffer.shape[0]
    outer_states(False, rates, per_level, half, part, received, states)
    members, _, _, cols = buffer.shape
    chunks = cols // LANES
    copies = []
    for m in range(members):
        for level in range(levels):
            for t in range(chunks):
                near = slice(t * LANES, (t + 1) * LANES)
                at = (2 * level * chunks + t) * members + m
                later = at + chunks * members
                entered = reach[level, 0] * states[at : at + 1, :] + reach[level, 1] * states[later : later + 1, :]
                buffer[m, level, :, near] = bases[level][m, :, near] + entered
        copies.append(pltpu.make_async_copy(buffer.at[m], out.at[m], sems.at[m]))
        copies[-1].start()
    at = 0
    for value in join_columns(1, keep, received, 2 * levels * half):
        returned[:, at : at + LANES] = value
        at += LANES
    for copy in copies:
        copy.wait()


def body(
    control, members, obs_corner, obs_count, offset_y, offset_x, offset_z, innovation, precision
):
    count, levels, rows, cols = control.shape
    n_mem, n_row, n_col = (lax.axis_size(name) for name in ("mem", "row", "col"))
    if n_mem != 2 or n_col != 2 or n_row & (n_row - 1):
        raise ValueError("unsupported mesh")
    grid_rows = rows * n_row
    block = min(256, cols)
    rates_x = filter_rates([cols / 16.0, cols / 64.0])
    rates_y = filter_rates([grid_rows / 2.0, rows / 2.0])
    scale = float(count * n_mem) ** -0.5
    flat = count * rows
    state_rows = levels * 2 * count * cols // LANES
    blocks = cols // block
    last = n_row.bit_length() - 2
    if levels * 2 * (blocks + 1) > HALF or last < 1:
        raise ValueError("unsupported sizes")

    per_level = 2 * (blocks + 1)
    corners = levels * 2 * count

    def tables(forward, *after):
        return call(
            functools.partial(table_kernel, forward, rates_x, rates_y, count, block),
            [((4 * HALF + block + LANES, cols), BF16), ((2, levels, flat, flat), BF16)]
            + [(a.shape, a.dtype) for a in after[1:]],
            after,
            8 * MIB,
            1.0,
        )

    def local(forward, level, *args):
        outs = [((rows, cols), F32), ((TURNED, flat), F32)] if forward else [((count, rows, cols), F32)]
        return call(
            functools.partial(local_kernel, forward, level, block),
            outs,
            args,
            16 * MIB,
            2.5,
            apart=() if forward else (len(args) - 1,),
            scratch=[pltpu.VMEM((flat, cols), F32)] * 2,
        )

    def close(forward, unit, edges, states, received, keep, after, more=()):
        moving = keep.shape[0] * 2 // unit * (unit // 2) * (1 + len(more) // 2)
        turned = TURNED * flat // LANES if forward else 0
        states, message, keep = call(
            functools.partial(
                corner_kernel, forward, rates_y, last, n_row, rows, unit, count, block, len(after)
            ),
            [((state_rows, LANES), F32), ((corners + moving + turned, LANES), F32), ((moving, LANES), F32)],
            (*after, *more, edges, states, received, keep),
            8 * MIB,
            0.4,
            apart=() if forward else range(len(after)),
        )
        received = swap(message, "col", n_col, 0)
        (part,) = call(
            functools.partial(inner_kernel, levels, count, block),
            [((state_rows, LANES), F32)],
            (edges, states, message),
            8 * MIB,
            0.4,
        )
        return part, received, keep

    row_reach = row_reach_of(rates_y, rows, True)
    args = (control, obs_count, obs_corner, offset_y, offset_x, offset_z, innovation, precision)
    moving = n_row * FIELDS
    message, blocks_out = call(
        functools.partial(first_kernel, rates_y),
        [((state_rows + moving, LANES), F32), ((moving, LANES), F32)],
        args,
        OBS * MIB,
        2.0,
        apart=range(len(args)),
        scratch=[pltpu.VMEM(a.shape, a.dtype) for a in args]
        + [pltpu.SemaphoreType.DMA((len(args) + levels - 1,))],
    )
    edges, row_matrix = tables(True, message)
    partial = []
    turned = []

    def beside(step, message):
        now = [row_matrix] if step == 0 else []
        while step and len(partial) < levels and (len(partial) < levels - 1 or step == last):
            one, two = local(True, len(partial), control, members, edges, row_matrix)
            partial.append(one)
            turned.append(two)
            now.append(two)
        return now

    states, received, (send,), keep = scan_rows(
        True, rates_y, rows, n_col * FIELDS, message, (blocks_out,), beside
    )
    last_bit = block_bits(True, last + 1)[last]
    pairs = []
    for m in range(n_mem):
        for r in range(n_row):
            pairs.append((m * n_row + r, (1 - m) * n_row + (r ^ (1 << last_bit))))
    row_other = swap(send, "row", n_row, last_bit)
    mem_keep = swap(keep, "mem", n_mem, 0)
    mem_other = lax.ppermute(send, ("mem", "row"), pairs)
    part, received, keep = close(
        True, n_col * FIELDS, edges, states, received, keep, turned, (row_other, mem_keep, mem_other)
    )
    sources = 4 * moving // FIELDS
    states, table, columns = call(
        functools.partial(collect_kernel, rates_x, per_level, count),
        [((state_rows, LANES), F32), ((4 * moving, LANES), F32), ((flat, LANES), F32)],
        (part, received, keep),
        4 * MIB,
        0.1,
    )
    wide = 2
    group = 8
    unpacked = [
        pltpu.VMEM((GROUP + 5, sources, LANES), F32),
        pltpu.VMEM((2, sources, LANES), jnp.int32),
    ]
    (images,) = call(
        functools.partial(observe_kernel, scale, wide, 2 * group, rates_x),
        [((sources, LANES), F32)],
        (states, columns, members, row_reach, table, *partial),
        16 * MIB,
        2.8,
        scratch=[
            pltpu.VMEM((levels * rows, cols), F32),
            pltpu.VMEM((2 * levels * rows * (GROUP + 1), cols // GROUP), BF16),
            *unpacked,
        ],
    )
    others = swap(images, "mem", n_mem, 0)

    row_reach = row_reach_of(rates_y, rows, False)
    edges, row_matrix = tables(False)
    forcing, message, keep = call(
        functools.partial(force_kernel, scale, wide, group, rates_y),
        [
            ((levels, rows, cols), F32),
            ((state_rows + n_row, LANES), F32),
            ((n_row, LANES), F32),
        ],
        (images, others, table, members),
        24 * MIB,
        4.0,
        scratch=[
            pltpu.VMEM((cols // GROUP, group * wide * LANES), BF16),
            pltpu.VMEM((2 * levels * rows * (GROUP + 1), group * wide * LANES), BF16),
            pltpu.VMEM((2 * levels * rows * (GROUP + 1), cols // GROUP), F32),
            pltpu.VMEM((sources, LANES), F32),
            *unpacked,
        ],
    )
    bases = []
    sent = []

    def back_beside(step, message):
        if step == 0:
            sent.extend(
                call(
                    functools.partial(columns_kernel, block),
                    [((flat, LANES), F32)],
                    (members, forcing, edges, message),
                    16 * MIB,
                    1.0,
                    apart=(3,),
                )
            )
            sent.append(swap(sent[0], "col", n_col, 0))
            return sent[1:]
        now = []
        if step == 1 or step == last:
            for level in range(len(bases), levels if step == last else levels - 1):
                now += local(False, level, control, members, forcing, *sent, edges, row_matrix, message)
        bases.extend(now)
        return now

    states, received, _, keep = scan_rows(False, rates_y, rows, n_col, message, (keep,), back_beside)
    part, received, keep = close(False, n_col, edges, states, received, keep, bases)
    return pl.pallas_call(
        functools.partial(finish_kernel, rates_x, per_level),
        out_shape=[
            jax.ShapeDtypeStruct(control.shape, F32),
            jax.ShapeDtypeStruct(precision.shape, F32),
        ],
        in_specs=[pl.BlockSpec(memory_space=pltpu.VMEM)] * (4 + levels),
        out_specs=[pl.BlockSpec(memory_space=pl.ANY), pl.BlockSpec(memory_space=pltpu.VMEM)],
        scratch_shapes=[
            pltpu.VMEM((state_rows, LANES), F32),
            pltpu.VMEM(control.shape, F32),
            pltpu.SemaphoreType.DMA((count,)),
        ],
        compiler_params=pltpu.CompilerParams(vmem_limit_bytes=8 * MIB),
        cost_estimate=cost(2.0),
    )(row_reach, part, received, keep, *bases)


def solution(mesh):
    spread = P(("mem", "row", "col"), None)
    grid = P("mem", None, "row", "col")
    return jax.shard_map(
        body,
        mesh=mesh,
        in_specs=(grid, grid) + (spread,) * 7,
        out_specs=(grid, spread),
        check_vma=False,
    )
```

```python
import functools

import jax
import jax.numpy as jnp
import numpy as np
from jax import lax
from jax.experimental import pallas as pl
from jax.experimental.pallas import tpu as pltpu
from jax.sharding import PartitionSpec as P

LANES = 128
HALF = LANES // 2
FIELDS = 6
TURNED = 8
GROUP = 4
PIECE = 256
F32 = jnp.float32
BF16 = jnp.bfloat16
MIB = 1 << 20
OBS = 57


def filter_rates(lengths):
    decay = np.exp(-1.0 / np.asarray(lengths, np.float64))
    weight = ((1.0 - decay**2) ** 3 / (1.0 + decay**2)) ** 0.25
    return decay, weight


def row_reach_of(rates, size, forward):
    places = np.arange(size)
    steps = places + 1 if forward else size - places
    reach = np.zeros((len(rates[0]), 2, size, LANES), np.float32)
    for level, (a, b) in enumerate(zip(*rates)):
        reach[level, 0] = (b * steps * a**steps)[:, None]
        reach[level, 1] = (a**steps)[:, None]
    return reach


def by_level(level, values):
    chosen = jnp.full(level.shape, float(values[0]), F32)
    for i in range(1, len(values)):
        chosen = jnp.where(level == i, float(values[i]), chosen)
    return chosen


def two_pass(a, b, lag):
    steps = jnp.maximum(lag, 0).astype(F32)
    return jnp.where(lag >= 0, float(b**2) * (steps + 1.0) * jnp.exp(steps * float(np.log(a))), 0.0)


def table_kernel(forward, rates_x, rates_y, members, block, *refs):
    edges, row_matrix, *passed = refs[len(refs) // 2 if len(refs) > 2 else 0 :]
    for out, ref in zip(passed, refs[1:]):
        out[...] = ref[...]
    levels = len(rates_x[0])
    size = edges.shape[1]
    blocks = size // block
    per_level = 2 * (blocks + 1)
    logs = [float(np.log(a)) for a in rates_x[0]]

    def lanes_of(lane):
        level = lax.div(lane, per_level)
        inner = lax.rem(lane, per_level)
        k = lax.div(inner, 2)
        return level, k, (inner & 1) == 1, (lane < levels * per_level)

    def place_of_column(column):
        return column if forward else size - 1 - column

    filled = min(HALF, -(-levels * per_level // 16) * 16)
    shape = (filled, size)
    level, k, second, used = lanes_of(lax.broadcasted_iota(jnp.int32, shape, 0))
    place = place_of_column(lax.broadcasted_iota(jnp.int32, shape, 1))
    steps = place + 1 - jnp.where(k == blocks, 0, (k + 1) * block)
    used = used & (steps > 0)
    steps = jnp.maximum(steps, 0).astype(F32)
    power = jnp.exp(steps * by_level(level, logs))
    value = jnp.where(second, power, by_level(level, rates_x[1]) * steps * power)
    high, low = split(jnp.where(used, value, 0.0))
    for i, part in enumerate((high, high, low, jnp.zeros(shape, BF16))):
        edges[i * HALF : i * HALF + filled, :] = part
        if filled < HALF:
            edges[i * HALF + filled : (i + 1) * HALF, :] = jnp.zeros((HALF - filled, size), BF16)

    first = 4 * HALF
    row = lax.broadcasted_iota(jnp.int32, (block, block), 0)
    column = lax.broadcasted_iota(jnp.int32, (block, block), 1)
    lag = column - row if forward else row - column
    for i, (a, b) in enumerate(zip(*rates_x)):
        for h, value in enumerate(split(two_pass(a, b, lag))):
            at = (h * levels + i) * block
            edges[first : first + block, at : at + block] = value
    at = 2 * levels * block
    if at < size:
        edges[first : first + block, at:] = jnp.zeros((block, size - at), BF16)

    first += block
    shape = (LANES, LANES)
    lane = lax.broadcasted_iota(jnp.int32, shape, 1)
    level, k, second, used = lanes_of(lane & (HALF - 1))
    stop = jnp.where(k == blocks, size, (k + 1) * block)
    begin = jnp.where(k == blocks, 0, k * block)
    log, weight = by_level(level, logs), by_level(level, rates_x[1])
    for t in range(size // LANES):
        place = place_of_column(t * LANES + lax.broadcasted_iota(jnp.int32, shape, 0))
        left = stop - 1 - place
        inside = used & (place >= begin) & (left >= 0)
        left = jnp.maximum(left, 0).astype(F32)
        value = weight * jnp.exp(left * log)
        value = jnp.where(inside, jnp.where(second, weight * (left + 1.0) * value, value), 0.0)
        high = value.astype(BF16)
        near = slice(t * LANES, (t + 1) * LANES)
        edges[first : first + LANES, near] = jnp.where(lane < HALF, high.astype(F32), value - high.astype(F32)).astype(BF16)

    flat = row_matrix.shape[2]
    height = flat // members
    row = lax.broadcasted_iota(jnp.int32, (height, flat), 0)
    column = lax.broadcasted_iota(jnp.int32, (height, flat), 1)
    member = lax.div(column, height)
    lag = row - lax.rem(column, height)
    lag = lag if forward else -lag
    for i, (a, b) in enumerate(zip(*rates_y)):
        value = two_pass(a, b, lag)
        for m in range(members):
            near = slice(m * height, (m + 1) * height)
            row_matrix[0, i, near, :], row_matrix[1, i, near, :] = split(jnp.where(member == m, value, 0.0))


class EdgeTable:
    def __init__(self, ref, levels, block):
        self.ref, self.levels, self.block = ref, levels, block
        self.size = ref.shape[1]
        self.first = 4 * HALF

    def reach(self, near=slice(None)):
        return self.ref[0 : self.first, near]

    def matrix(self, level):
        return jnp.concatenate([self.square(level), self.square(self.levels + level), self.square(level)], axis=0)

    def square(self, index):
        return self.ref[self.first : self.first + self.block, index * self.block : (index + 1) * self.block]

    def edge(self):
        at = self.first + self.block
        rows = [self.ref[at : at + LANES, t : t + LANES] for t in range(0, self.size, LANES)]
        return jnp.concatenate(rows, axis=0)


def split(value):
    high = value.astype(BF16)
    return high, (value - high.astype(F32)).astype(BF16)


def dot(left, right):
    return jnp.dot(left, right, preferred_element_type=F32)


def lane_kinds(shape, blocks, level):
    lane = lax.broadcasted_iota(jnp.int32, shape, 1)
    per_level = 2 * (blocks + 1)
    mine = (lane >= level * per_level) & (lane < (level + 1) * per_level)
    return mine, lax.rem(lane, per_level) >= 2 * blocks


def edge_states(value, table, blocks, level):
    high, low = split(value)
    weights = table.edge()
    both = dot(high, weights) + dot(low, weights)
    mine, _ = lane_kinds(both.shape, blocks, level)
    return jnp.where(mine, both + pltpu.roll(both, HALF, 1), 0.0)


def packed(states):
    lane = lax.broadcasted_iota(jnp.int32, states.shape, 1)
    high = states.astype(BF16).astype(F32)
    low = states - high
    first = jnp.where(lane < HALF, high, pltpu.roll(low, HALF, 1))
    second = jnp.where(lane < HALF, high, 0.0)
    return jnp.concatenate([first.astype(BF16), second.astype(BF16)], axis=1)


def dot_left(left, value):
    high, low = split(value)
    return dot(left, jnp.concatenate([high, high, low], axis=0))


def dot_right(value, right, *more):
    high, low = split(value)
    left = jnp.concatenate([high, high, low] + [x for x, _ in more], axis=1)
    return dot(left, jnp.concatenate([right] + [x for _, x in more], axis=0))


def cost(micros):
    return pl.CostEstimate(flops=0, bytes_accessed=int(micros * 3.6e6), transcendentals=0)


def call(kernel, outs, args, limit, micros, apart=(), scratch=()):
    return pl.pallas_call(
        kernel,
        out_shape=[jax.ShapeDtypeStruct(shape, dtype) for shape, dtype in outs],
        in_specs=[
            pl.BlockSpec(memory_space=pl.ANY if i in apart else pltpu.VMEM) for i in range(len(args))
        ],
        out_specs=[pl.BlockSpec(memory_space=pltpu.VMEM) for _ in outs],
        scratch_shapes=list(scratch),
        compiler_params=pltpu.CompilerParams(vmem_limit_bytes=limit),
        cost_estimate=cost(micros),
    )(*args)


def level_rows(ref, level):
    value = ref[:, level]
    return value.reshape(value.shape[0] * value.shape[1], value.shape[2])


def work_rows(members_ref, forcing_ref, level):
    value = members_ref[:, level].astype(F32) * forcing_ref[level][None]
    return value.reshape(value.shape[0] * value.shape[1], value.shape[2])


def row_weights_at_edge(forward, rates, level, members, size):
    a, b = rates[0][level], rates[1][level]
    shape = (members, members * size)
    member = lax.broadcasted_iota(jnp.int32, shape, 0)
    place = lax.broadcasted_iota(jnp.int32, shape, 1)
    row = lax.rem(place, size)
    left = (size - 1 - row if forward else row).astype(F32)
    power = jnp.where(lax.div(place, size) == member, float(b) * jnp.exp(left * float(np.log(a))), 0.0)
    high, low = split(jnp.concatenate([power, float(b) * (left + 1.0) * power], axis=0))
    return jnp.concatenate([high, low], axis=0)


def put_row_edges(forward, rates, members, size, values, message):
    levels = len(rates[0])
    tables = [row_weights_at_edge(forward, rates, level, members, size) for level in range(levels)]
    for level, value in values:
        weights = tables[level]
        pairs = weights.shape[0] // 2
        high, low = split(value)
        both = dot(weights, high)
        lay_states(message, level, both[0:pairs] + both[pairs:] + dot(weights[0:pairs], low))


def lay_states(message, level, states):
    half = states.shape[0] // 2
    chunks = states.shape[1] // LANES
    for s in range(2):
        for t in range(chunks):
            at = ((2 * level + s) * chunks + t) * half
            message[at : at + half, :] = states[s * half : (s + 1) * half, t * LANES : (t + 1) * LANES]


def take_states(states, level, half, chunks):
    rows = []
    for s in range(2):
        at = (2 * level + s) * chunks * half
        rows.append(
            jnp.concatenate([states[at + t * half : at + (t + 1) * half, :] for t in range(chunks)], axis=1)
        )
    return jnp.concatenate(rows, axis=0)


def first_kernel(rates, *refs):
    sources, (message, send), places, sems = refs[:8], refs[8:10], refs[10:18], refs[18]
    base = message.shape[0] - send.shape[0]
    control, counts, *fields = places
    levels = control.shape[1]
    pairs = list(zip(sources[1:], places[1:]))
    pairs += [(sources[0].at[:, level], control.at[:, level]) for level in range(levels)]
    copies = [pltpu.make_async_copy(*pair, sems.at[i]) for i, pair in enumerate(pairs)]
    for copy in copies:
        copy.start()
    for copy in copies[:-levels]:
        copy.wait()
    rows = counts.shape[1] // 2
    steps = rows.bit_length() - 1
    order = sorted(range(rows), key=lambda row: block_place(True, steps, row))
    bit = (lax.axis_index("row") >> block_bits(True, steps)[0]) & 1
    slot = lax.broadcasted_iota(jnp.int32, (1, LANES), 1)

    def read(tile, f):
        value = fields[f][:, tile * LANES : (tile + 1) * LANES].astype(F32)
        if f == FIELDS - 1:
            value = jnp.where(slot < counts[:, tile : tile + 1], value, 0.0)
        return value

    at = 0
    for h in range(0, rows, 2):
        for tile_col in range(2):
            for f in range(FIELDS):
                zero, one = read(2 * order[h] + tile_col, f), read(2 * order[h + 1] + tile_col, f)
                send[at : at + 1, :], message[base + at : base + at + 1, :] = join(bit, one, zero)
                at += 1

    def values():
        for level in range(levels):
            copies[level - levels].wait()
            yield level, level_rows(control, level)

    put_row_edges(True, rates, control.shape[0], control.shape[2], values(), message)


def columns_kernel(block, members, forcing, edges, _, out):
    levels = members.shape[1]
    table = EdgeTable(edges, levels, block)
    total = None
    for level in range(levels):
        states = edge_states(work_rows(members, forcing, level), table, table.size // block, level)
        total = states if total is None else total + states
    out[...] = total


def entering_rows(forward, rates, level, size):
    a, b = rates[0][level], rates[1][level]
    place = lax.broadcasted_iota(jnp.int32, (1, size), 1)
    steps = (place + 1 if forward else size - place).astype(F32)
    power = jnp.exp(steps * float(np.log(a)))
    return float(b) * steps * power, power


def corner_kernel(forward, rates, step, count, tile, unit, half, block, after, *refs):
    *refs, edges, before, received, keep_in, states, message, keep = refs
    more, refs = refs[:after], refs[after:]
    last_states(forward, rates, step, count, tile, before, received, states)
    levels = len(rates[0])
    table = EdgeTable(edges, levels, block)
    chunks = table.size // LANES
    rows = [take_states(states, level, half, chunks) for level in range(levels)]
    high, low = split(jnp.concatenate(rows, axis=0))
    at = high.shape[0]
    both = dot(jnp.concatenate([high, low], axis=0), table.edge())
    both = both[0:at] + both[at:]
    both = both + pltpu.roll(both, HALF, 1)
    for level in range(levels):
        near = slice(2 * half * level, 2 * half * (level + 1))
        mine, _ = lane_kinds((2 * half, LANES), table.size // block, level)
        message[near, :] = jnp.where(mine, both[near], 0.0)
    bit = (lax.axis_index("row") >> block_bits(forward, step + 1)[step]) & 1
    place = lax.axis_index("col")
    base, size = before.shape[0], keep_in.shape[0]
    each = unit // 2
    if refs:
        pairs = [(keep_in[...], refs[0][...]), (refs[1][...], refs[2][...])]
    else:
        pairs = [(keep_in[...], received[base : base + size, :])]
    start, at = at, 0
    for mine, other in pairs:
        for value in join(bit, mine, other):
            for i in range(0, size, unit):
                send, stay = join(place, value[i + each : i + unit], value[i : i + each])
                message[start + at : start + at + each, :] = send
                keep[at : at + each, :] = stay
                at += each
    if forward:
        turned = more[0][...]
        for ref in more[1:]:
            turned = turned + ref[...]
        for t in range(turned.shape[1] // LANES):
            first = start + at + t * turned.shape[0]
            message[first : first + turned.shape[0], :] = turned[:, t * LANES : (t + 1) * LANES]


def inner_kernel(levels, half, block, edges, states, message, part):
    table = EdgeTable(edges, levels, block)
    size = table.size
    blocks = size // block
    for level in range(levels):
        value = take_states(states, level, half, size // LANES)
        pairs = value.shape[0]
        corner = message[level * pairs : (level + 1) * pairs, :]
        _, whole = lane_kinds(corner.shape, blocks, level)
        carry = dot(packed(jnp.where(whole, 0.0, corner)), table.reach())
        stack = jnp.concatenate([value[:, at : at + block] for at in range(0, size, block)], axis=0)
        stack = dot_right(stack, table.matrix(level))
        rows = [stack[n * pairs : (n + 1) * pairs] for n in range(blocks)]
        lay_states(part, level, jnp.concatenate(rows, axis=1) + carry)


def outer_states(forward, rates, per_level, half, part, received, states):
    place = lax.axis_index("col")
    live = jnp.where(place == (1 if forward else 0), 1.0, 0.0)
    levels = len(rates[0])
    chunks = part.shape[0] // (2 * levels * half)
    for level in range(levels):
        lane = (level + 1) * per_level - 2
        ones, twos = entering_rows(forward, rates, level, chunks * LANES)
        for s in range(2):
            at = (2 * level + s) * half
            corner = received[at : at + half, :] * live
            one, two = corner[:, lane : lane + 1], corner[:, lane + 1 : lane + 2]
            for t in range(chunks):
                at = ((2 * level + s) * chunks + t) * half
                near = slice(t * LANES, (t + 1) * LANES)
                states[at : at + half, :] = part[at : at + half, :] + one * ones[:, near] + two * twos[:, near]


def join_columns(each, keep, received, base):
    place = lax.axis_index("col")
    for i in range(0, keep.shape[0], each):
        yield from join(place, keep[i : i + each, :], received[base + i : base + i + each, :])


def collect_kernel(rates, per_level, half, part, received, keep, states, table, columns):
    outer_states(True, rates, per_level, half, part, received, states)
    at = 0
    for value in join_columns(FIELDS, keep, received, 2 * len(rates[0]) * half):
        table[at : at + FIELDS, :] = value
        at += FIELDS
    live = jnp.where(lax.axis_index("col") == 1, 1.0, 0.0)
    start = 2 * len(rates[0]) * half + keep.shape[0]
    for t in range(columns.shape[0] // LANES):
        turned = received[start + t * TURNED : start + (t + 1) * TURNED, :] * live
        turned = jnp.concatenate([turned, jnp.zeros((LANES - TURNED, LANES), F32)], axis=0)
        columns[t * LANES : (t + 1) * LANES, :] = jnp.transpose(turned)


def block_bits(forward, steps):
    bits = list(range(steps))
    if forward:
        bits[0], bits[-1] = bits[-1], bits[0]
    return bits


def block_place(forward, steps, row):
    return sum(((row >> bit) & 1) << i for i, bit in enumerate(block_bits(forward, steps)))


def transfer(rates, level, steps):
    a, b = rates[0][level], rates[1][level]
    return float(a**steps), float(b * steps * a**steps)


def pick(index, values):
    chosen = jnp.float32(values[0])
    for i in range(1, len(values)):
        chosen = jnp.where(index == i, jnp.float32(values[i]), chosen)
    return chosen


def reach_of(forward, rates, step, count, tile, level):
    row = lax.axis_index("row")
    line = row if forward else count - 1 - row
    upper = ((line >> step) & 1) == 1
    inside = line & ((1 << step) - 1)
    table = [transfer(rates, level, q * tile) for q in range(1 << step)]
    near1 = jnp.where(upper, pick(inside, [x[0] for x in table]), 0.0)
    near2 = jnp.where(upper, pick(inside, [x[1] for x in table]), 0.0)
    return near1, near2, upper


def join(bit, mine, other):
    return jnp.where(bit == 1, other, mine), jnp.where(bit == 1, mine, other)


def new_states(forward, rates, step, count, tile, level, before, received, first, second):
    near1, near2, upper = reach_of(forward, rates, step, count, tile, level)
    got1, got2 = received[first, :], received[second, :]
    new1 = near1 * got1
    new2 = near1 * got2 + near2 * got1
    if before is not None:
        new1 = before[first, :] + new1
        new2 = before[second, :] + new2
    return new1, new2, got1, got2, upper


def round_kernel(forward, rates, step, count, tile, unit, spans, apart, after, *refs):
    sent, received, *refs = refs
    keep_in = sent if apart else refs.pop(0)
    before = refs.pop(0) if step else None
    blocks = refs.pop(0) if apart else received
    message, keep, states, *send = refs[after:]
    levels = len(rates[0])
    base = states.shape[0]
    start, own = (0, base) if apart else (base, 0)
    part = base // (2 * levels)
    for level in range(levels):
        at = 2 * level * part
        first, second = slice(at, at + part), slice(at + part, at + 2 * part)
        new1, new2, got1, got2, upper = new_states(
            forward, rates, step, count, tile, level, before, received, first, second
        )
        states[first, :] = new1
        states[second, :] = new2
        far1, far2 = transfer(rates, level, tile << step)
        own1 = jnp.where(upper, 1.0, far1)
        own2 = jnp.where(upper, 0.0, far2)
        his1 = jnp.where(upper, far1, 1.0)
        his2 = jnp.where(upper, far2, 0.0)
        all1, all2 = sent[first, :], sent[second, :]
        message[first, :] = own1 * all1 + his1 * got1
        message[second, :] = own1 * all2 + own2 * all1 + his1 * got2 + his2 * got1
    row = lax.axis_index("row")
    bits = block_bits(forward, count.bit_length() - 1)
    bit = (row >> bits[step]) & 1
    next_bit = (row >> bits[step + 1]) & 1
    size = unit << step
    place, first = (send[0], 0) if send else (message, base)

    def span(h):
        near = slice(own + h * size, own + (h + 1) * size)
        other = blocks[start + h * size : start + (h + 1) * size, :]
        return jnp.concatenate(join(bit, keep_in[near, :], other), axis=0)

    at = 0
    for h in range(0, spans // 2, 2):
        moved, stay = join(next_bit, span(h + 1), span(h))
        place[first + at : first + at + 2 * size, :] = moved
        keep[at : at + 2 * size, :] = stay
        at += 2 * size


def last_states(forward, rates, step, count, tile, before, received, states):
    levels = len(rates[0])
    part = before.shape[0] // (2 * levels)
    for level in range(levels):
        at = 2 * level * part
        first, second = slice(at, at + part), slice(at + part, at + 2 * part)
        states[first, :], states[second, :], *_ = new_states(
            forward, rates, step, count, tile, level, before, received, first, second
        )


def swap(value, axis, size, step):
    return lax.ppermute(value, axis, [(i, i ^ (1 << step)) for i in range(size)])


def scan_rows(forward, rates, tile, unit, message, blocks, beside):
    count = lax.axis_size("row")
    steps = count.bit_length() - 1
    spans = count
    apart = forward
    keep = blocks[0]
    moving = keep.shape[0]
    state_rows = message.shape[0] - moving
    states = None
    for step in range(steps - 1):
        received = swap(message, "row", count, step)
        args = (message, received) + (() if apart else (keep,)) + (() if step == 0 else (states,))
        if apart:
            args += (swap(blocks[0], "row", count, block_bits(forward, steps)[step]),)
        after = beside(step, message)
        first = len(args)
        args = args + tuple(after)
        kernel = functools.partial(
            round_kernel, forward, rates, step, count, tile, unit, spans, apart, len(after)
        )
        outs = [state_rows + moving, moving, state_rows]
        if forward and step == steps - 2:
            outs = [state_rows, moving, state_rows, moving]
        outs = [((rows, LANES), F32) for rows in outs]
        message, keep, states, *send = call(kernel, outs, args, 4 * MIB, 0.1, apart=range(first, len(args)))
        spans //= 2
        apart = False
    received = swap(message, "row", count, steps - 1)
    beside(steps - 1, message)
    return states, received, send, keep


def local_kernel(forward, level, block, *refs):
    if forward:
        control, members, edges, row_matrix, out, whole_out, between, scratch = refs
    else:
        control, members, forcing, columns, received, edges, row_matrix, _, out, between, scratch = refs
    count, levels, rows, cols = control.shape
    table = EdgeTable(edges, levels, block)
    high = row_matrix[0, level]
    left = jnp.concatenate([high, row_matrix[1, level], high], axis=1)
    mine, whole = lane_kinds((count * rows, LANES), cols // block, level)
    if forward:
        value = level_rows(control, level)
        states = edge_states(value, table, cols // block, level)
        entering = jnp.where(whole, 0.0, states)
        turned = jnp.transpose(dot_left(left, jnp.where(whole, states, 0.0)))
        first = (level + 1) * 2 * (cols // block + 1) - 2
        whole_out[...] = jnp.zeros_like(whole_out)
        whole_out[2 * level : 2 * level + 2, :] = turned[first : first + 2, :]
    else:
        value = work_rows(members, forcing, level)
        live = jnp.where(lax.axis_index("col") == 0, 1.0, 0.0)
        entering = jnp.where(whole, received[...] * live, columns[...])
        entering = jnp.where(mine, entering, 0.0)
    entering = packed(entering)
    weights = table.matrix(level)
    spans = [slice(at, at + block) for at in range(0, cols, block)]
    for near in spans:
        between[:, near] = dot_right(value[:, near], weights, (entering, table.reach(near)))
    for near in spans:
        scratch[:, near] = dot_left(left, between[:, near])
    if forward:
        total = None
        for m in range(count):
            term = members[m, level].astype(F32) * scratch[m * rows : (m + 1) * rows, :]
            total = term if total is None else total + term
        out[...] = total
    else:
        for m in range(count):
            out[m] = control[m, level] + scratch[m * rows : (m + 1) * rows, :]


def bulk_fields(table, cols, weights, places):
    sources = table.shape[0] // FIELDS
    fields = [table[pl.ds(f, sources, stride=FIELDS), :] for f in range(FIELDS)]
    corner = fields[0].astype(jnp.int32)
    row_at = lax.div(corner, cols)
    col_at = corner - row_at * cols
    values = col_weights(col_at, fields[2]) + [fields[1]] + fields[3:]
    for i, value in enumerate(values):
        weights[i] = value
    places[0] = row_at
    places[1] = lax.div(col_at, GROUP)


def source_row(ref, i, chunk, wide):
    rows = [ref[i, pl.ds(chunk * wide + j, 1), :] for j in range(wide)]
    return jnp.concatenate(rows, axis=1)


def row_weights(row_at, frac, rows):
    places = lax.broadcasted_iota(jnp.int32, (rows, row_at.shape[1]), 0)
    near = jnp.where(places == row_at, 1.0 - frac, 0.0)
    return near + jnp.where(places == row_at + 1, frac, 0.0)


def one_hot(col_at, cols):
    places = lax.broadcasted_iota(jnp.int32, (cols, col_at.shape[1]), 0)
    return jnp.where(places == col_at, 1.0, 0.0).astype(BF16)


def spread_matrix(size, back):
    one = lax.broadcasted_iota(jnp.int32, (size, size), 1 if back else 0)
    two = lax.broadcasted_iota(jnp.int32, (size, size), 0 if back else 1)
    at = (one & (GROUP - 1)) * (size // GROUP) + lax.div(one, GROUP)
    return jnp.where(at == two, 1.0, 0.0).astype(BF16)


def col_weights(col_at, frac):
    within = col_at & (GROUP - 1)
    weights = []
    for j in range(GROUP + 1):
        weight = jnp.where(within == j, 1.0 - frac, 0.0)
        weights.append(weight + jnp.where(within == j - 1, frac, 0.0))
    return weights


def observe_kernel(scale, wide, group, rates, states, columns, members, reach, table, *refs):
    count, levels, rows, cols = members.shape
    partial, (images, field, stack, weights, places) = refs[:levels], refs[levels:]
    bulk_fields(table, cols, weights, places)
    chunks = cols // LANES
    for level in range(levels):
        reach1, reach2 = reach[level, 0], reach[level, 1]
        ones, twos = entering_rows(True, rates, level, cols)
        spans = [slice(t * LANES, (t + 1) * LANES) for t in range(chunks)]
        totals = [partial[level][:, near] for near in spans]
        for m in range(count):
            across = columns[m * rows : (m + 1) * rows, :]
            one = jnp.broadcast_to(across[:, 2 * level : 2 * level + 1], (rows, LANES))
            two = jnp.broadcast_to(across[:, 2 * level + 1 : 2 * level + 2], (rows, LANES))
            for t, near in enumerate(spans):
                at = (2 * level * chunks + t) * count + m
                later = at + chunks * count
                entered = reach1 * states[at : at + 1, :] + reach2 * states[later : later + 1, :]
                entered = entered + one * ones[:, near] + two * twos[:, near]
                totals[t] = totals[t] + members[m, level, :, near].astype(F32) * entered
        for t, near in enumerate(spans):
            field[level * rows : (level + 1) * rows, near] = totals[t] * scale
    flat = levels * rows
    high, low = split(field[...])
    both = jnp.concatenate([high, low], axis=0)
    spread = spread_matrix(PIECE, False)
    each = PIECE // GROUP
    pieces = [dot(both[:, at : at + PIECE], spread) for at in range(0, cols, PIECE)]
    wide_k = cols // GROUP
    for j in range(GROUP):
        value = jnp.concatenate([p[:, j * each : (j + 1) * each] for p in pieces], axis=1)
        stack[2 * flat * j : 2 * flat * (j + 1), :] = value.astype(BF16)
        if j == 0:
            moved = pltpu.roll(value, wide_k - 1, 1)
            stack[2 * flat * GROUP : 2 * flat * (GROUP + 1), :] = moved.astype(BF16)
    sources = table.shape[0] // FIELDS // wide

    def work(chunk):
        row_at, group_at = (source_row(places, i, chunk, wide) for i in range(2))
        *near, frac_y, frac_z = (source_row(weights, i, chunk, wide) for i in range(GROUP + 3))
        seen = dot(stack[...], one_hot(group_at, cols // GROUP))
        mixed = None
        for j, weight in enumerate(near):
            at = 2 * flat * j
            term = (seen[at : at + flat] + seen[at + flat : at + 2 * flat]) * weight
            mixed = term if mixed is None else mixed + term
        weight = row_weights(row_at, frac_y, rows)
        low_level = jnp.sum(mixed[0:rows] * weight, axis=0, keepdims=True)
        high_level = jnp.sum(mixed[rows : 2 * rows] * weight, axis=0, keepdims=True)
        image = (1.0 - frac_z) * low_level + frac_z * high_level
        for i in range(wide):
            images[pl.ds(chunk * wide + i, 1), :] = image[:, i * LANES : (i + 1) * LANES]

    if sources == group:
        for chunk in range(sources):
            work(chunk)
    else:

        @pl.loop(0, sources // group)
        def _(turn):
            for i in range(group):
                work(turn * group + i)


def force_kernel(
    scale, wide, group, rates, images, others, table, members, *refs
):
    forcing, message, keep, hot, load, total, misfits, weights, places = refs
    bulk_fields(table, members.shape[3], weights, places)
    count, levels, rows, cols = members.shape
    flat = levels * rows
    sources = table.shape[0] // FIELDS
    half = sources // 2
    span = wide * LANES
    total[...] = jnp.zeros_like(total)

    @pl.loop(0, sources // wide // group)
    def _(turn):
        for i in range(group):
            chunk = turn * group + i
            row_at, group_at = (source_row(places, i, chunk, wide) for i in range(2))
            *near_weights, frac_y, frac_z, innovation, precision = (
                source_row(weights, i, chunk, wide) for i in range(GROUP + 5)
            )
            parts = []
            for j in range(wide):
                source = chunk * wide + j
                swapped = jnp.where(source < half, source + half, source - half)
                parts.append(images[pl.ds(source, 1), :] + others[pl.ds(swapped, 1), :])
            misfit = precision * (jnp.concatenate(parts, axis=1) - innovation)
            for j in range(wide):
                misfits[pl.ds(chunk * wide + j, 1), :] = misfit[:, j * LANES : (j + 1) * LANES]
            weight = row_weights(row_at, frac_y, rows) * misfit
            stack = jnp.concatenate([weight * (1.0 - frac_z), weight * frac_z], axis=0)
            near = slice(i * span, (i + 1) * span)
            for j, weight in enumerate(near_weights):
                at = 2 * flat * j
                load[at : at + flat, near], load[at + flat : at + 2 * flat, near] = split(stack * weight)
            hot[:, near] = one_hot(group_at, cols // GROUP)
        total[...] += lax.dot_general(
            load[...], hot[...], (((1,), (1,)), ((), ())), preferred_element_type=F32
        )

    groups = []
    for j in range(GROUP + 1):
        at = 2 * flat * j
        groups.append(total[at : at + flat, :] + total[at + flat : at + 2 * flat, :])
    groups[0] = groups[0] + pltpu.roll(groups[GROUP], 1, 1)
    spread = spread_matrix(PIECE, True)
    each = PIECE // GROUP
    for t in range(cols // PIECE):
        value = jnp.concatenate([g[:, t * each : (t + 1) * each] for g in groups[:GROUP]], axis=1)
        high, low = split(value * scale)
        force = dot(high, spread) + dot(low, spread)
        for level in range(levels):
            forcing[level, :, t * PIECE : (t + 1) * PIECE] = force[level * rows : (level + 1) * rows]
    values = ((level, work_rows(members, forcing, level)) for level in range(levels))
    put_row_edges(False, rates, count, rows, values, message)
    bit = lax.axis_index("row") & 1
    base = message.shape[0] - keep.shape[0]
    steps = (half // 2).bit_length() - 1

    def of_row(row):
        at = 2 * block_place(True, steps, row)
        return misfits[at : at + 2, :]

    for h in range(half // 4):
        zero, one = of_row(2 * h), of_row(2 * h + 1)
        message[base + 2 * h : base + 2 * h + 2, :], keep[2 * h : 2 * h + 2, :] = join(bit, one, zero)


def finish_kernel(rates, per_level, reach, part, received, keep, *refs):
    levels = reach.shape[0]
    bases, (out, returned, states, buffer, sems) = refs[:levels], refs[levels:]
    half = buffer.shape[0]
    outer_states(False, rates, per_level, half, part, received, states)
    members, _, _, cols = buffer.shape
    chunks = cols // LANES
    copies = []
    for m in range(members):
        for level in range(levels):
            for t in range(chunks):
                near = slice(t * LANES, (t + 1) * LANES)
                at = (2 * level * chunks + t) * members + m
                later = at + chunks * members
                entered = reach[level, 0] * states[at : at + 1, :] + reach[level, 1] * states[later : later + 1, :]
                buffer[m, level, :, near] = bases[level][m, :, near] + entered
        copies.append(pltpu.make_async_copy(buffer.at[m], out.at[m], sems.at[m]))
        copies[-1].start()
    at = 0
    for value in join_columns(1, keep, received, 2 * levels * half):
        returned[:, at : at + LANES] = value
        at += LANES
    for copy in copies:
        copy.wait()


def body(
    control, members, obs_corner, obs_count, offset_y, offset_x, offset_z, innovation, precision
):
    count, levels, rows, cols = control.shape
    n_mem, n_row, n_col = (lax.axis_size(name) for name in ("mem", "row", "col"))
    if n_mem != 2 or n_col != 2 or n_row & (n_row - 1):
        raise ValueError("unsupported mesh")
    grid_rows = rows * n_row
    block = min(256, cols)
    rates_x = filter_rates([cols / 16.0, cols / 64.0])
    rates_y = filter_rates([grid_rows / 2.0, rows / 2.0])
    scale = float(count * n_mem) ** -0.5
    flat = count * rows
    state_rows = levels * 2 * count * cols // LANES
    blocks = cols // block
    last = n_row.bit_length() - 2
    if levels * 2 * (blocks + 1) > HALF or last < 1:
        raise ValueError("unsupported sizes")

    per_level = 2 * (blocks + 1)
    corners = levels * 2 * count

    def tables(forward, *after):
        return call(
            functools.partial(table_kernel, forward, rates_x, rates_y, count, block),
            [((4 * HALF + block + LANES, cols), BF16), ((2, levels, flat, flat), BF16)]
            + [(a.shape, a.dtype) for a in after[1:]],
            after,
            8 * MIB,
            1.0,
        )

    def local(forward, level, *args):
        outs = [((rows, cols), F32), ((TURNED, flat), F32)] if forward else [((count, rows, cols), F32)]
        return call(
            functools.partial(local_kernel, forward, level, block),
            outs,
            args,
            16 * MIB,
            2.5,
            apart=() if forward else (len(args) - 1,),
            scratch=[pltpu.VMEM((flat, cols), F32)] * 2,
        )

    def close(forward, unit, edges, states, received, keep, after, more=()):
        moving = keep.shape[0] * 2 // unit * (unit // 2) * (1 + len(more) // 2)
        turned = TURNED * flat // LANES if forward else 0
        states, message, keep = call(
            functools.partial(
                corner_kernel, forward, rates_y, last, n_row, rows, unit, count, block, len(after)
            ),
            [((state_rows, LANES), F32), ((corners + moving + turned, LANES), F32), ((moving, LANES), F32)],
            (*after, *more, edges, states, received, keep),
            8 * MIB,
            0.4,
            apart=() if forward else range(len(after)),
        )
        received = swap(message, "col", n_col, 0)
        (part,) = call(
            functools.partial(inner_kernel, levels, count, block),
            [((state_rows, LANES), F32)],
            (edges, states, message),
            8 * MIB,
            0.4,
        )
        return part, received, keep

    row_reach = row_reach_of(rates_y, rows, True)
    args = (control, obs_count, obs_corner, offset_y, offset_x, offset_z, innovation, precision)
    moving = n_row * FIELDS
    message, blocks_out = call(
        functools.partial(first_kernel, rates_y),
        [((state_rows + moving, LANES), F32), ((moving, LANES), F32)],
        args,
        OBS * MIB,
        2.0,
        apart=range(len(args)),
        scratch=[pltpu.VMEM(a.shape, a.dtype) for a in args]
        + [pltpu.SemaphoreType.DMA((len(args) + levels - 1,))],
    )
    edges, row_matrix = tables(True, message)
    partial = []
    turned = []

    def beside(step, message):
        now = [row_matrix] if step == 0 else []
        while step and len(partial) < levels and (len(partial) < levels - 1 or step == last):
            one, two = local(True, len(partial), control, members, edges, row_matrix)
            partial.append(one)
            turned.append(two)
            now.append(two)
        return now

    states, received, (send,), keep = scan_rows(
        True, rates_y, rows, n_col * FIELDS, message, (blocks_out,), beside
    )
    last_bit = block_bits(True, last + 1)[last]
    pairs = []
    for m in range(n_mem):
        for r in range(n_row):
            pairs.append((m * n_row + r, (1 - m) * n_row + (r ^ (1 << last_bit))))
    row_other = swap(send, "row", n_row, last_bit)
    mem_keep = swap(keep, "mem", n_mem, 0)
    mem_other = lax.ppermute(send, ("mem", "row"), pairs)
    part, received, keep = close(
        True, n_col * FIELDS, edges, states, received, keep, turned, (row_other, mem_keep, mem_other)
    )
    sources = 4 * moving // FIELDS
    states, table, columns = call(
        functools.partial(collect_kernel, rates_x, per_level, count),
        [((state_rows, LANES), F32), ((4 * moving, LANES), F32), ((flat, LANES), F32)],
        (part, received, keep),
        4 * MIB,
        0.1,
    )
    wide = 2
    group = 8
    unpacked = [
        pltpu.VMEM((GROUP + 5, sources, LANES), F32),
        pltpu.VMEM((2, sources, LANES), jnp.int32),
    ]
    (images,) = call(
        functools.partial(observe_kernel, scale, wide, 2 * group, rates_x),
        [((sources, LANES), F32)],
        (states, columns, members, row_reach, table, *partial),
        16 * MIB,
        2.8,
        scratch=[
            pltpu.VMEM((levels * rows, cols), F32),
            pltpu.VMEM((2 * levels * rows * (GROUP + 1), cols // GROUP), BF16),
            *unpacked,
        ],
    )
    others = swap(images, "mem", n_mem, 0)

    row_reach = row_reach_of(rates_y, rows, False)
    edges, row_matrix = tables(False)
    forcing, message, keep = call(
        functools.partial(force_kernel, scale, wide, group, rates_y),
        [
            ((levels, rows, cols), F32),
            ((state_rows + n_row, LANES), F32),
            ((n_row, LANES), F32),
        ],
        (images, others, table, members),
        24 * MIB,
        4.0,
        scratch=[
            pltpu.VMEM((cols // GROUP, group * wide * LANES), BF16),
            pltpu.VMEM((2 * levels * rows * (GROUP + 1), group * wide * LANES), BF16),
            pltpu.VMEM((2 * levels * rows * (GROUP + 1), cols // GROUP), F32),
            pltpu.VMEM((sources, LANES), F32),
            *unpacked,
        ],
    )
    bases = []
    sent = []

    def back_beside(step, message):
        if step == 0:
            sent.extend(
                call(
                    functools.partial(columns_kernel, block),
                    [((flat, LANES), F32)],
                    (members, forcing, edges, message),
                    16 * MIB,
                    1.0,
                    apart=(3,),
                )
            )
            sent.append(swap(sent[0], "col", n_col, 0))
            return sent[1:]
        now = []
        if step == 1 or step == last:
            for level in range(len(bases), levels if step == last else levels - 1):
                now += local(False, level, control, members, forcing, *sent, edges, row_matrix, message)
        bases.extend(now)
        return now

    states, received, _, keep = scan_rows(False, rates_y, rows, n_col, message, (keep,), back_beside)
    part, received, keep = close(False, n_col, edges, states, received, keep, bases)
    return pl.pallas_call(
        functools.partial(finish_kernel, rates_x, per_level),
        out_shape=[
            jax.ShapeDtypeStruct(control.shape, F32),
            jax.ShapeDtypeStruct(precision.shape, F32),
        ],
        in_specs=[pl.BlockSpec(memory_space=pltpu.VMEM)] * (4 + levels),
        out_specs=[pl.BlockSpec(memory_space=pl.ANY), pl.BlockSpec(memory_space=pltpu.VMEM)],
        scratch_shapes=[
            pltpu.VMEM((state_rows, LANES), F32),
            pltpu.VMEM(control.shape, F32),
            pltpu.SemaphoreType.DMA((count,)),
        ],
        compiler_params=pltpu.CompilerParams(vmem_limit_bytes=8 * MIB),
        cost_estimate=cost(2.0),
    )(row_reach, part, received, keep, *bases)


def solution(mesh):
    spread = P(("mem", "row", "col"), None)
    grid = P("mem", None, "row", "col")
    return jax.shard_map(
        body,
        mesh=mesh,
        in_specs=(grid, grid) + (spread,) * 7,
        out_specs=(grid, spread),
        check_vma=False,
    )
```
